32 devices in a mesh: grp: 2 (over x), feed: 16 (over z, y, core).
Axes of the slice: x: 2, y: 2, z: 4, core: 2. Of those that a mesh axis runs over, the one named last changes fastest.
Arguments:
- samples: bfloat16 [32, 256, 65536], P(('grp', 'feed')), parts along dimension 0, may hold values from -6 to 6
- pfb_taps: float32 [4, 8192], replicated, may hold values from -0.03125 to 0.03125
Outputs:
- visibility: float32 [16384, 4096], P(('grp', 'feed')), parts along dimension 0
The draws below stay inside these ranges and needn't reach their ends.
There are 2 independent parts, one for each index of `grp`. The reference program is written for one: setup_inputs(seed, part) draws one part's arguments, and reference() takes and returns one part's arrays. A program takes and returns all parts, laid end to end along the dimension named above; an argument that names none is the same for every part. Nothing has to cross between parts.
All inputs are finite; a program needn't handle non-finite values.
Results may differ from the reference program's by a relative error of at most 0.004.
Values may be sent and summed in bfloat16 or wider, within the bound.
No kernel may reach another device: no remote copies, remote signals or barrier semaphores. Data moves between devices by JAX's collectives and lax.ppermute only.
A program may use at most 192 MiB of HBM per device.

```python
import math
import jax
import jax.numpy as jnp
from jax import lax

FEEDS = 2048
NFFT = 8192
TAPS = 4
FIRST_CH = 1536
TIME_BLOCKS = 2
FRAMES_DEV = 8
CH_SLAB = 4
NSPEC = 16
FEED_DEV = 256
N_FEED = 16


def block_levels(rng, dims, shards, least, largest):
    def one(dim, blocks):
        steps = jax.random.uniform(jax.random.fold_in(jax.random.fold_in(rng, 6), dim), (blocks,), jnp.float32, least / len(shards), largest / len(shards))
        return jnp.repeat(jnp.exp(steps), dims[dim] // blocks).reshape((-1,) + (1,) * (len(dims) - dim - 1))

    gain = one(*shards[0])
    for cut in shards[1:]:
        gain = gain * one(*cut)
    return gain


def bell_draw(own_key, dims, spread, bound, shards=(), held_as=jnp.bfloat16):
    entries = jax.random.normal(own_key, dims, jnp.float32) * spread
    if len(shards) > 0:
        entries = block_levels(own_key, dims, shards, -0.22, 0.18) * entries
    return jnp.clip(entries, min=-bound, max=bound).astype(held_as)


def setup_inputs(seed: int = 0, part: int = 0) -> dict:
    splits = jax.random.split(jax.random.key(seed), 3)
    own_keys = jax.random.split(jax.random.fold_in(splits[2], part), 3)
    return {
        "samples": bell_draw(own_keys[0], (N_FEED, FEED_DEV, FRAMES_DEV * NFFT), 1.0, 6.0, ((0, 16),)),
        "pfb_taps": bell_draw(splits[1], (TAPS, NFFT), (TAPS * NFFT) ** -0.5, 0.03125, (), jnp.float32),
    }


def dft_matrix(fft_len, first_channel, channel_count):
    sample_ids = jnp.arange(fft_len, dtype=jnp.int32)
    channel_ids = first_channel + jnp.arange(channel_count, dtype=jnp.int32)
    phase = (sample_ids[:, None] * channel_ids[None, :]) % fft_len
    angle = phase.astype(jnp.float32) * (2.0 * math.pi / fft_len)
    return jnp.concatenate([jnp.cos(angle), -jnp.sin(angle)], axis=1)


def reference(samples, pfb_taps):
    blocks = samples.reshape(TIME_BLOCKS, N_FEED // TIME_BLOCKS, FEED_DEV, FRAMES_DEV, NFFT)
    frames = jnp.transpose(blocks, (1, 2, 0, 3, 4)).reshape(FEEDS // FEED_DEV, FEED_DEV, NSPEC, NFFT)
    dft_table = dft_matrix(NFFT, FIRST_CH, CH_SLAB)

    def transform(part_frames):
        padded = jnp.concatenate([jnp.zeros((FEED_DEV, TAPS - 1, NFFT), part_frames.dtype), part_frames], axis=1)
        filtered = jnp.zeros((FEED_DEV, NSPEC, NFFT), jnp.float32)
        for tap_index in range(TAPS):
            filtered = filtered + padded[:, tap_index:tap_index + NSPEC].astype(jnp.float32) * pfb_taps[tap_index]
        spectra = jnp.dot(filtered.reshape(FEED_DEV * NSPEC, NFFT), dft_table, precision=lax.Precision.HIGHEST, preferred_element_type=jnp.float32)
        return spectra.astype(jnp.bfloat16).reshape(FEED_DEV, NSPEC, 2 * CH_SLAB)

    spectra = lax.map(transform, frames).reshape(FEEDS, NSPEC, 2 * CH_SLAB)
    real_all = jnp.moveaxis(spectra[:, :, :CH_SLAB], 2, 0)
    imag_all = jnp.moveaxis(spectra[:, :, CH_SLAB:], 2, 0)

    def correlate(pair):
        real_part, imag_part = pair
        all_feeds = jnp.concatenate([real_part, imag_part], axis=1)
        right_matrix = jnp.concatenate([all_feeds, jnp.concatenate([-imag_part, real_part], axis=1)], axis=0).T
        return jnp.dot(all_feeds, right_matrix, preferred_element_type=jnp.float32) * (1.0 / NSPEC)

    visibility = lax.map(correlate, (real_all, imag_all))
    return visibility.reshape(CH_SLAB * FEEDS, 2 * FEEDS)
```

```python
import functools
import math

import jax
import jax.numpy as jnp
import numpy as np
from jax import lax
from jax.experimental import pallas as pl
from jax.experimental.pallas import tpu as pltpu
from jax.sharding import PartitionSpec as P

FIRST_CH = 1536
TIME_BLOCKS = 2
ROWS_DEV = 512
PIECES = 2


def dft_rows(fft_len, first_channel, channel_count):
    sample_ids = np.arange(fft_len, dtype=np.int64)
    channel_ids = first_channel + np.arange(channel_count, dtype=np.int64)
    phase = channel_ids[:, None] * sample_ids[None, :] % fft_len
    angle = phase.astype(np.float64) * (2.0 * math.pi / fft_len)
    return np.concatenate([np.cos(angle), -np.sin(angle)], axis=0).astype(np.float32)


def spectra_kernel(
    group_span, owners, x_hbm, taps_ref, dft_ref, out_ref, x_buf, table, parts, sems
):
    tap_count, fft_len = taps_ref.shape
    columns = dft_ref.shape[0]
    channels = columns // 2
    frame_count = x_hbm.shape[2] // fft_len
    piece = fft_len // PIECES
    edge = tap_count - 1
    width = tap_count * columns
    later_block = lax.axis_index("feed") >= group_span

    def fetch(index):
        span = pl.ds(index * piece, piece)
        return pltpu.make_async_copy(x_hbm.at[0, :, span], x_buf.at[:, span], sems.at[index])

    for index in range(frame_count * PIECES):
        fetch(index).start()

    step = 1024
    for start in range(0, fft_len, step):
        dft = dft_ref[:, start : start + step]
        scaled = jnp.concatenate(
            [taps_ref[m : m + 1, start : start + step] * dft for m in range(tap_count)], axis=0
        )
        high = scaled.astype(jnp.bfloat16).astype(jnp.float32)
        both = jnp.concatenate([high, scaled - high], axis=0)
        table[start : start + step, :] = both.T.astype(jnp.bfloat16)

    window = [None] * (frame_count + edge)
    for frame in range(frame_count):
        total = None
        for p in range(PIECES):
            fetch(frame * PIECES + p).wait()
            start = frame * fft_len + p * piece
            product = jnp.dot(
                x_buf[:, start : start + piece],
                table[p * piece : (p + 1) * piece, :],
                preferred_element_type=jnp.float32,
            )
            total = product if total is None else total + product
        turned = total.T
        summed = turned[:width] + turned[width:]
        for m in range(tap_count):
            term = summed[m * columns : (m + 1) * columns]
            spot = frame + edge - m
            window[spot] = term if window[spot] is None else window[spot] + term
    for spot in range(frame_count + edge):
        parts[:, spot, :] = window[spot]

    for c in range(channels):
        now = jnp.concatenate([parts[c, :frame_count], parts[channels + c, :frame_count]], axis=0)
        high = now.astype(jnp.bfloat16)
        low = now - high.astype(jnp.float32)
        low = jnp.concatenate([low[:4], low[frame_count : frame_count + 4]], axis=0)
        tail = jnp.concatenate(
            [parts[c, frame_count : frame_count + 4], parts[channels + c, frame_count : frame_count + 4]],
            axis=0,
        )
        sublane = lax.broadcasted_iota(jnp.int32, tail.shape, 0)
        tail = jnp.where(sublane % 4 < edge, tail, 0.0)
        tail_high = tail.astype(jnp.bfloat16).astype(jnp.float32)
        tail_low = tail - tail_high
        extra = jnp.concatenate(
            [jnp.where(later_block, low, tail_high), jnp.where(later_block, 0.0, tail_low)], axis=0
        ).astype(jnp.bfloat16)
        whole = jnp.concatenate([high, extra], axis=0)
        for o in range(owners):
            out_ref[c * owners + o] = whole


def correlate_kernel(scale, owners, got_ref, out_ref, right, left, turned):
    devices, rows, feed_count = got_ref.shape
    group_span = devices // TIME_BLOCKS
    frame_count = rows // 4
    depth = right.shape[0]
    block_rows = out_ref.shape[0]
    total_feeds = right.shape[1]

    @pl.when(pl.program_id(0) == 0)
    def _():
        for g in range(group_span):
            span = slice(g * feed_count, (g + 1) * feed_count)
            first = got_ref[g].astype(jnp.float32)
            second = got_ref[group_span + g].astype(jnp.float32)
            extra = (
                first[2 * frame_count : 3 * frame_count]
                + first[3 * frame_count :]
                + second[2 * frame_count : 3 * frame_count]
            )
            zero = jnp.zeros((frame_count - 4, feed_count), jnp.float32)
            extra = jnp.concatenate([extra[:4], zero, extra[4:8], zero], axis=0)
            fixed = second[: 2 * frame_count] + extra
            right[: 2 * frame_count, span] = got_ref[g, : 2 * frame_count]
            right[2 * frame_count :, span] = fixed.astype(jnp.bfloat16)
        row_start = lax.axis_index("feed") % owners * ROWS_DEV
        mine = right[:, pl.ds(pl.multiple_of(row_start, ROWS_DEV), ROWS_DEV)].astype(jnp.float32)
        halves = [mine[k * frame_count : (k + 1) * frame_count] for k in range(4)]
        swapped = jnp.concatenate([halves[1], -halves[0], halves[3], -halves[2]], axis=0)
        left[...] = mine.T.astype(jnp.bfloat16)
        turned[...] = swapped.T.astype(jnp.bfloat16)

    span = pl.ds(pl.multiple_of(pl.program_id(0) * block_rows, block_rows), block_rows)
    out_ref[:, :total_feeds] = (
        jnp.dot(left[span, :], right[...], preferred_element_type=jnp.float32) * scale
    )
    out_ref[:, total_feeds:] = (
        jnp.dot(turned[span, :], right[...], preferred_element_type=jnp.float32) * scale
    )


def body(samples, pfb_taps):
    feed_count = samples.shape[1]
    tap_count, fft_len = pfb_taps.shape
    frame_count = samples.shape[2] // fft_len
    devices = lax.axis_size("feed")
    group_span = devices // TIME_BLOCKS
    total_feeds = feed_count * group_span
    channels = devices * ROWS_DEV // total_feeds
    owners = total_feeds // ROWS_DEV
    spectra_count = TIME_BLOCKS * frame_count
    columns = 2 * channels
    rows = 4 * frame_count
    dft = jnp.asarray(dft_rows(fft_len, FIRST_CH, channels))
    in_vmem = pl.BlockSpec(memory_space=pltpu.VMEM)
    outgoing = pl.pallas_call(
        functools.partial(spectra_kernel, group_span, owners),
        out_shape=jax.ShapeDtypeStruct((devices, rows, feed_count), jnp.bfloat16),
        in_specs=[pl.BlockSpec(memory_space=pl.ANY), in_vmem, in_vmem],
        out_specs=in_vmem,
        scratch_shapes=[
            pltpu.VMEM((feed_count, samples.shape[2]), jnp.bfloat16),
            pltpu.VMEM((fft_len, 2 * tap_count * columns), jnp.bfloat16),
            pltpu.VMEM((columns, 2 * frame_count, feed_count), jnp.float32),
            pltpu.SemaphoreType.DMA((frame_count * PIECES,)),
        ],
        compiler_params=pltpu.CompilerParams(vmem_limit_bytes=56 * 2**20),
        name="spectra",
    )(samples, pfb_taps, dft)
    gathered = lax.all_to_all(outgoing, "feed", split_axis=0, concat_axis=0, tiled=True)
    block_rows = 64
    return pl.pallas_call(
        functools.partial(correlate_kernel, 1.0 / spectra_count, owners),
        out_shape=jax.ShapeDtypeStruct((ROWS_DEV, 2 * total_feeds), jnp.float32),
        grid=(ROWS_DEV // block_rows,),
        in_specs=[pl.BlockSpec((devices, rows, feed_count), lambda i: (0, 0, 0))],
        out_specs=pl.BlockSpec((block_rows, 2 * total_feeds), lambda i: (i, 0)),
        scratch_shapes=[
            pltpu.VMEM((rows, total_feeds), jnp.bfloat16),
            pltpu.VMEM((ROWS_DEV, rows), jnp.bfloat16),
            pltpu.VMEM((ROWS_DEV, rows), jnp.bfloat16),
        ],
        compiler_params=pltpu.CompilerParams(vmem_limit_bytes=32 * 2**20),
        name="correlate",
    )(gathered)


def solution(mesh):
    placed = (P(("grp", "feed"), None, None), P())
    return jax.shard_map(
        body, mesh=mesh, in_specs=placed, out_specs=P(("grp", "feed"), None), check_vma=False
    )
```

```python
import functools
import math

import jax
import jax.numpy as jnp
import numpy as np
from jax import lax
from jax.experimental import pallas as pl
from jax.experimental.pallas import tpu as pltpu
from jax.sharding import PartitionSpec as P

FIRST_CH = 1536
TIME_BLOCKS = 2
ROWS_DEV = 512
PIECES = 2
TABLE_STEP = 1024
BLOCK_ROWS = 64


def dft_rows(fft_len, first_channel, channel_count):
    sample_ids = np.arange(fft_len, dtype=np.int64)
    channel_ids = first_channel + np.arange(channel_count, dtype=np.int64)
    phase = channel_ids[:, None] * sample_ids[None, :] % fft_len
    angle = phase.astype(np.float64) * (2.0 * math.pi / fft_len)
    return np.concatenate([np.cos(angle), -np.sin(angle)], axis=0).astype(np.float32)


def spectra_kernel(
    group_span, owners, x_hbm, taps_ref, dft_ref, out_ref, x_buf, table, window, parts, sems
):
    tap_count, fft_len = taps_ref.shape
    columns = dft_ref.shape[0]
    channels = columns // 2
    frame_count = x_hbm.shape[2] // fft_len
    piece = fft_len // PIECES
    edge = tap_count - 1
    width = tap_count * columns
    later_block = lax.axis_index("feed") >= group_span

    def fetch(index):
        span = pl.ds(pl.multiple_of(index * piece, piece), piece)
        return pltpu.make_async_copy(x_hbm.at[0, :, span], x_buf.at[:, span], sems.at[index])

    @pl.loop(0, frame_count * PIECES)
    def _(index):
        fetch(index).start()

    window[...] = jnp.zeros_like(window)

    @pl.loop(0, fft_len // TABLE_STEP)
    def _(index):
        span = pl.ds(pl.multiple_of(index * TABLE_STEP, TABLE_STEP), TABLE_STEP)
        dft = dft_ref[:, span]
        scaled = jnp.concatenate([taps_ref[m : m + 1, span] * dft for m in range(tap_count)], axis=0)
        high = scaled.astype(jnp.bfloat16)
        table[:width, span] = high
        table[width:, span] = (scaled - high.astype(jnp.float32)).astype(jnp.bfloat16)

    @pl.loop(0, frame_count)
    def _(frame):
        for p in range(PIECES):
            fetch(frame * PIECES + p).wait()
            start = pl.multiple_of(frame * fft_len + p * piece, piece)
            product = lax.dot_general(
                table[:, p * piece : (p + 1) * piece],
                x_buf[:, pl.ds(start, piece)],
                (((1,), (1,)), ((), ())),
                preferred_element_type=jnp.float32,
            )
            summed = product[:width] + product[width:]
            for m in range(tap_count):
                window[frame + edge - m] += summed[m * columns : (m + 1) * columns]

    for spot in range(frame_count + edge):
        parts[:, spot, :] = window[spot]

    for c in range(channels):
        now = jnp.concatenate([parts[c, :frame_count], parts[channels + c, :frame_count]], axis=0)
        high = now.astype(jnp.bfloat16)
        low = now - high.astype(jnp.float32)
        low = jnp.concatenate([low[:4], low[frame_count : frame_count + 4]], axis=0)
        tail = jnp.concatenate(
            [parts[c, frame_count : frame_count + 4], parts[channels + c, frame_count : frame_count + 4]],
            axis=0,
        )
        sublane = lax.broadcasted_iota(jnp.int32, tail.shape, 0)
        tail = jnp.where(sublane % 4 < edge, tail, 0.0)
        tail_high = tail.astype(jnp.bfloat16).astype(jnp.float32)
        tail_low = tail - tail_high
        extra = jnp.concatenate(
            [jnp.where(later_block, low, tail_high), jnp.where(later_block, 0.0, tail_low)], axis=0
        ).astype(jnp.bfloat16)
        whole = jnp.concatenate([high, extra], axis=0)
        for o in range(owners):
            out_ref[c * owners + o] = whole


def correlate_kernel(scale, owners, got_ref, out_hbm, right, left, out_buf, sems):
    devices, rows, feed_count = got_ref.shape
    group_span = devices // TIME_BLOCKS
    frame_count = rows // 4
    total_feeds = right.shape[1]
    blocks = left.shape[0]
    block_rows = left.shape[1] // 2

    for g in range(group_span):
        span = slice(g * feed_count, (g + 1) * feed_count)
        first = got_ref[g].astype(jnp.float32)
        second = got_ref[group_span + g].astype(jnp.float32)
        extra = (
            first[2 * frame_count : 3 * frame_count]
            + first[3 * frame_count :]
            + second[2 * frame_count : 3 * frame_count]
        )
        zero = jnp.zeros((frame_count - 4, feed_count), jnp.float32)
        extra = jnp.concatenate([extra[:4], zero, extra[4:8], zero], axis=0)
        fixed = second[: 2 * frame_count] + extra
        right[: 2 * frame_count, span] = got_ref[g, : 2 * frame_count]
        right[2 * frame_count :, span] = fixed.astype(jnp.bfloat16)
    row_start = lax.axis_index("feed") % owners * ROWS_DEV
    mine = right[:, pl.ds(pl.multiple_of(row_start, ROWS_DEV), ROWS_DEV)].astype(jnp.float32)
    halves = [mine[k * frame_count : (k + 1) * frame_count] for k in range(4)]
    swapped = jnp.concatenate([halves[1], -halves[0], halves[3], -halves[2]], axis=0)
    left[:, :block_rows, :] = mine.T.astype(jnp.bfloat16).reshape(blocks, block_rows, rows)
    left[:, block_rows:, :] = swapped.T.astype(jnp.bfloat16).reshape(blocks, block_rows, rows)

    def store(block):
        span = pl.ds(pl.multiple_of(block * block_rows, block_rows), block_rows)
        return pltpu.make_async_copy(out_buf.at[span], out_hbm.at[span], sems.at[block])

    @pl.loop(0, blocks)
    def _(block):
        product = jnp.dot(left[block], right[...], preferred_element_type=jnp.float32) * scale
        span = pl.ds(pl.multiple_of(block * block_rows, block_rows), block_rows)
        out_buf[span, :total_feeds] = product[:block_rows]
        out_buf[span, total_feeds:] = product[block_rows:]
        store(block).start()

    @pl.loop(0, blocks)
    def _(block):
        store(block).wait()


def body(samples, pfb_taps):
    feed_count = samples.shape[1]
    tap_count, fft_len = pfb_taps.shape
    frame_count = samples.shape[2] // fft_len
    devices = lax.axis_size("feed")
    group_span = devices // TIME_BLOCKS
    total_feeds = feed_count * group_span
    channels = devices * ROWS_DEV // total_feeds
    owners = total_feeds // ROWS_DEV
    spectra_count = TIME_BLOCKS * frame_count
    columns = 2 * channels
    rows = 4 * frame_count
    dft = jnp.asarray(dft_rows(fft_len, FIRST_CH, channels))
    in_vmem = pl.BlockSpec(memory_space=pltpu.VMEM)
    outgoing = pl.pallas_call(
        functools.partial(spectra_kernel, group_span, owners),
        out_shape=jax.ShapeDtypeStruct((devices, rows, feed_count), jnp.bfloat16),
        in_specs=[pl.BlockSpec(memory_space=pl.ANY), in_vmem, in_vmem],
        out_specs=in_vmem,
        scratch_shapes=[
            pltpu.VMEM((feed_count, samples.shape[2]), jnp.bfloat16),
            pltpu.VMEM((2 * tap_count * columns, fft_len), jnp.bfloat16),
            pltpu.VMEM((frame_count + tap_count - 1, columns, feed_count), jnp.float32),
            pltpu.VMEM((columns, 2 * frame_count, feed_count), jnp.float32),
            pltpu.SemaphoreType.DMA((frame_count * PIECES,)),
        ],
        compiler_params=pltpu.CompilerParams(vmem_limit_bytes=56 * 2**20),
        name="spectra",
    )(samples, pfb_taps, dft)
    gathered = lax.all_to_all(outgoing, "feed", split_axis=0, concat_axis=0, tiled=True)
    blocks = ROWS_DEV // BLOCK_ROWS
    return pl.pallas_call(
        functools.partial(correlate_kernel, 1.0 / spectra_count, owners),
        out_shape=jax.ShapeDtypeStruct((ROWS_DEV, 2 * total_feeds), jnp.float32),
        in_specs=[in_vmem],
        out_specs=pl.BlockSpec(memory_space=pl.ANY),
        scratch_shapes=[
            pltpu.VMEM((rows, total_feeds), jnp.bfloat16),
            pltpu.VMEM((blocks, 2 * BLOCK_ROWS, rows), jnp.bfloat16),
            pltpu.VMEM((ROWS_DEV, 2 * total_feeds), jnp.float32),
            pltpu.SemaphoreType.DMA((blocks,)),
        ],
        compiler_params=pltpu.CompilerParams(vmem_limit_bytes=32 * 2**20),
        name="correlate",
    )(gathered)


def solution(mesh):
    placed = (P(("grp", "feed"), None, None), P())
    return jax.shard_map(
        body, mesh=mesh, in_specs=placed, out_specs=P(("grp", "feed"), None), check_vma=False
    )
```

```python
import functools
import math

import jax
import jax.numpy as jnp
import numpy as np
from jax import lax
from jax.experimental import pallas as pl
from jax.experimental.pallas import tpu as pltpu
from jax.sharding import PartitionSpec as P

FIRST_CH = 1536
TIME_BLOCKS = 2
ROWS_DEV = 512
PIECES = 2
TABLE_STEP = 1024
BLOCK_ROWS = 64


def dft_rows(fft_len, first_channel, channel_count):
    sample_ids = np.arange(fft_len, dtype=np.int64)
    channel_ids = first_channel + np.arange(channel_count, dtype=np.int64)
    phase = channel_ids[:, None] * sample_ids[None, :] % fft_len
    angle = phase.astype(np.float64) * (2.0 * math.pi / fft_len)
    return np.concatenate([np.cos(angle), -np.sin(angle)], axis=0).astype(np.float32)


def spectra_kernel(owners, x_hbm, taps_ref, dft_ref, *rest):
    channels = dft_ref.shape[0] // 2
    outs, (x_buf, table, window, parts, sems) = rest[:channels], rest[channels:]
    tap_count, fft_len = taps_ref.shape
    columns = 2 * channels
    frame_count = x_hbm.shape[2] // fft_len
    piece = fft_len // PIECES
    edge = tap_count - 1
    width = tap_count * columns
    my_plane = lax.axis_index("feed") // owners
    later_block = my_plane >= channels // TIME_BLOCKS

    def fetch(index):
        span = pl.ds(pl.multiple_of(index * piece, piece), piece)
        return pltpu.make_async_copy(x_hbm.at[0, :, span], x_buf.at[:, span], sems.at[index])

    @pl.loop(0, frame_count * PIECES)
    def _(index):
        fetch(index).start()

    window[...] = jnp.zeros_like(window)

    @pl.loop(0, fft_len // TABLE_STEP)
    def _(index):
        span = pl.ds(pl.multiple_of(index * TABLE_STEP, TABLE_STEP), TABLE_STEP)
        dft = dft_ref[:, span]
        scaled = jnp.concatenate([taps_ref[m : m + 1, span] * dft for m in range(tap_count)], axis=0)
        high = scaled.astype(jnp.bfloat16).astype(jnp.float32)
        both = jnp.concatenate([high, scaled - high], axis=0)
        table[span, :] = both.T.astype(jnp.bfloat16)

    @pl.loop(0, frame_count)
    def _(frame):
        total = None
        for p in range(PIECES):
            fetch(frame * PIECES + p).wait()
            start = pl.multiple_of(frame * fft_len + p * piece, piece)
            product = jnp.dot(
                x_buf[:, pl.ds(start, piece)],
                table[p * piece : (p + 1) * piece, :],
                preferred_element_type=jnp.float32,
            )
            total = product if total is None else total + product
        turned = total.T
        summed = turned[:width] + turned[width:]
        for m in range(tap_count):
            window[frame + edge - m] += summed[m * columns : (m + 1) * columns]

    for spot in range(frame_count + edge):
        parts[:, spot, :] = window[spot]

    for k in range(channels):
        c = lax.rem(my_plane + k, channels)
        now = jnp.concatenate([parts[c, :frame_count], parts[channels + c, :frame_count]], axis=0)
        high = now.astype(jnp.bfloat16)
        low = now - high.astype(jnp.float32)
        low = jnp.concatenate([low[:4], low[frame_count : frame_count + 4]], axis=0)
        tail = jnp.concatenate(
            [parts[c, frame_count : frame_count + 4], parts[channels + c, frame_count : frame_count + 4]],
            axis=0,
        )
        sublane = lax.broadcasted_iota(jnp.int32, tail.shape, 0)
        tail = jnp.where(sublane % 4 < edge, tail, 0.0)
        tail_high = tail.astype(jnp.bfloat16).astype(jnp.float32)
        tail_low = tail - tail_high
        extra = jnp.concatenate(
            [jnp.where(later_block, low, tail_high), jnp.where(later_block, 0.0, tail_low)], axis=0
        ).astype(jnp.bfloat16)
        outs[k][...] = jnp.concatenate([high, extra], axis=0)


def join_kernel(owners, *refs):
    channels = len(refs) - 2
    out_ref, slots = refs[channels:]
    rows = slots.shape[1]
    feed_count = slots.shape[2]
    frame_count = rows // 4
    half = channels // TIME_BLOCKS
    my_plane = lax.axis_index("feed") // owners
    for k in range(channels):
        slots[lax.rem(my_plane + channels - k, channels)] = refs[k][...]
    for p in range(half):
        first = slots[p].astype(jnp.float32)
        second = slots[half + p].astype(jnp.float32)
        extra = (
            first[2 * frame_count : 3 * frame_count]
            + first[3 * frame_count :]
            + second[2 * frame_count : 3 * frame_count]
        )
        zero = jnp.zeros((frame_count - 4, feed_count), jnp.float32)
        extra = jnp.concatenate([extra[:4], zero, extra[4:8], zero], axis=0)
        fixed = second[: 2 * frame_count] + extra
        out_ref[p, : 2 * frame_count] = slots[p, : 2 * frame_count]
        out_ref[p, 2 * frame_count :] = fixed.astype(jnp.bfloat16)


def correlate_kernel(scale, owners, *refs):
    got, (out_hbm, slots, right, left, out_buf, sems) = refs[:owners], refs[owners:]
    half, rows, feed_count = got[0].shape
    frame_count = rows // 4
    total_feeds = right.shape[1]
    blocks = left.shape[0]
    block_rows = left.shape[1] // 2
    my_place = lax.axis_index("feed") % owners

    for k in range(owners):
        slots[lax.rem(my_place + owners - k, owners)] = got[k][...]
    for o in range(owners):
        for p in range(half):
            start = (p * owners + o) * feed_count
            right[:, start : start + feed_count] = slots[o, p]
    row_start = my_place * ROWS_DEV
    mine = right[:, pl.ds(pl.multiple_of(row_start, ROWS_DEV), ROWS_DEV)].astype(jnp.float32)
    halves = [mine[k * frame_count : (k + 1) * frame_count] for k in range(4)]
    swapped = jnp.concatenate([halves[1], -halves[0], halves[3], -halves[2]], axis=0)
    left[:, :block_rows, :] = mine.T.astype(jnp.bfloat16).reshape(blocks, block_rows, rows)
    left[:, block_rows:, :] = swapped.T.astype(jnp.bfloat16).reshape(blocks, block_rows, rows)

    def store(block):
        span = pl.ds(pl.multiple_of(block * block_rows, block_rows), block_rows)
        return pltpu.make_async_copy(out_buf.at[span], out_hbm.at[span], sems.at[block])

    @pl.loop(0, blocks)
    def _(block):
        product = jnp.dot(left[block], right[...], preferred_element_type=jnp.float32) * scale
        span = pl.ds(pl.multiple_of(block * block_rows, block_rows), block_rows)
        out_buf[span, :total_feeds] = product[:block_rows]
        out_buf[span, total_feeds:] = product[block_rows:]
        store(block).start()

    @pl.loop(0, blocks)
    def _(block):
        store(block).wait()


def body(samples, pfb_taps):
    feed_count = samples.shape[1]
    tap_count, fft_len = pfb_taps.shape
    frame_count = samples.shape[2] // fft_len
    devices = lax.axis_size("feed")
    total_feeds = feed_count * devices // TIME_BLOCKS
    channels = devices * ROWS_DEV // total_feeds
    owners = total_feeds // ROWS_DEV
    half = channels // TIME_BLOCKS
    spectra_count = TIME_BLOCKS * frame_count
    columns = 2 * channels
    rows = 4 * frame_count
    dft = jnp.asarray(dft_rows(fft_len, FIRST_CH, channels))
    in_vmem = pl.BlockSpec(memory_space=pltpu.VMEM)
    sent = pl.pallas_call(
        functools.partial(spectra_kernel, owners),
        out_shape=[jax.ShapeDtypeStruct((rows, feed_count), jnp.bfloat16)] * channels,
        in_specs=[pl.BlockSpec(memory_space=pl.ANY), in_vmem, in_vmem],
        out_specs=[in_vmem] * channels,
        scratch_shapes=[
            pltpu.VMEM((feed_count, samples.shape[2]), jnp.bfloat16),
            pltpu.VMEM((fft_len, 2 * tap_count * columns), jnp.bfloat16),
            pltpu.VMEM((frame_count + tap_count - 1, columns, feed_count), jnp.float32),
            pltpu.VMEM((columns, 2 * frame_count, feed_count), jnp.float32),
            pltpu.SemaphoreType.DMA((frame_count * PIECES,)),
        ],
        compiler_params=pltpu.CompilerParams(vmem_limit_bytes=56 * 2**20),
        name="spectra",
    )(samples, pfb_taps, dft)

    def to_plane(value, k):
        pairs = [
            (z * owners + q, (z + k) % channels * owners + q)
            for z in range(channels)
            for q in range(owners)
        ]
        return lax.ppermute(value, "feed", pairs)

    def to_place(value, k):
        pairs = [
            (z * owners + q, z * owners + (q + k) % owners)
            for z in range(channels)
            for q in range(owners)
        ]
        return lax.ppermute(value, "feed", pairs)

    arrived = [sent[0]] + [to_plane(sent[k], k) for k in range(1, channels)]
    joined = pl.pallas_call(
        functools.partial(join_kernel, owners),
        out_shape=jax.ShapeDtypeStruct((half, rows, feed_count), jnp.bfloat16),
        in_specs=[in_vmem] * channels,
        out_specs=in_vmem,
        scratch_shapes=[pltpu.VMEM((channels, rows, feed_count), jnp.bfloat16)],
        name="join",
    )(*arrived)
    spread = [joined] + [to_place(joined, k) for k in range(1, owners)]
    blocks = ROWS_DEV // BLOCK_ROWS
    return pl.pallas_call(
        functools.partial(correlate_kernel, 1.0 / spectra_count, owners),
        out_shape=jax.ShapeDtypeStruct((ROWS_DEV, 2 * total_feeds), jnp.float32),
        in_specs=[in_vmem] * owners,
        out_specs=pl.BlockSpec(memory_space=pl.ANY),
        scratch_shapes=[
            pltpu.VMEM((owners, half, rows, feed_count), jnp.bfloat16),
            pltpu.VMEM((rows, total_feeds), jnp.bfloat16),
            pltpu.VMEM((blocks, 2 * BLOCK_ROWS, rows), jnp.bfloat16),
            pltpu.VMEM((ROWS_DEV, 2 * total_feeds), jnp.float32),
            pltpu.SemaphoreType.DMA((blocks,)),
        ],
        compiler_params=pltpu.CompilerParams(vmem_limit_bytes=32 * 2**20),
        name="correlate",
    )(*spread)


def solution(mesh):
    placed = (P(("grp", "feed"), None, None), P())
    return jax.shard_map(
        body, mesh=mesh, in_specs=placed, out_specs=P(("grp", "feed"), None), check_vma=False
    )
```

```python
import functools
import math

import jax
import jax.numpy as jnp
import numpy as np
from jax import lax
from jax.experimental import pallas as pl
from jax.experimental.pallas import tpu as pltpu
from jax.sharding import PartitionSpec as P

FIRST_CH = 1536
TIME_BLOCKS = 2
ROWS_DEV = 512
PIECES = 2
TABLE_STEP = 1024
BLOCK_ROWS = 64


def dft_rows(fft_len, first_channel, channel_count):
    sample_ids = np.arange(fft_len, dtype=np.int64)
    channel_ids = first_channel + np.arange(channel_count, dtype=np.int64)
    phase = channel_ids[:, None] * sample_ids[None, :] % fft_len
    angle = phase.astype(np.float64) * (2.0 * math.pi / fft_len)
    return np.concatenate([np.cos(angle), -np.sin(angle)], axis=0).astype(np.float32)


def spectra_kernel(
    owners, x_hbm, taps_ref, dft_ref, out_ref, x_buf, table, window, parts, sems
):
    channels = dft_ref.shape[0] // 2
    tap_count, fft_len = taps_ref.shape
    columns = 2 * channels
    frame_count = x_hbm.shape[2] // fft_len
    piece = fft_len // PIECES
    edge = tap_count - 1
    width = tap_count * columns
    my_plane = lax.axis_index("feed") // owners
    later_block = my_plane >= channels // TIME_BLOCKS

    def fetch(index):
        span = pl.ds(pl.multiple_of(index * piece, piece), piece)
        return pltpu.make_async_copy(x_hbm.at[0, :, span], x_buf.at[:, span], sems.at[index])

    @pl.loop(0, frame_count * PIECES)
    def _(index):
        fetch(index).start()

    window[...] = jnp.zeros_like(window)

    @pl.loop(0, fft_len // TABLE_STEP)
    def _(index):
        span = pl.ds(pl.multiple_of(index * TABLE_STEP, TABLE_STEP), TABLE_STEP)
        dft = dft_ref[:, span]
        scaled = jnp.concatenate([taps_ref[m : m + 1, span] * dft for m in range(tap_count)], axis=0)
        high = scaled.astype(jnp.bfloat16).astype(jnp.float32)
        both = jnp.concatenate([high, scaled - high], axis=0)
        table[span, :] = both.T.astype(jnp.bfloat16)

    @pl.loop(0, frame_count)
    def _(frame):
        total = None
        for p in range(PIECES):
            fetch(frame * PIECES + p).wait()
        for p in range(PIECES):
            start = pl.multiple_of(frame * fft_len + p * piece, piece)
            product = jnp.dot(
                x_buf[:, pl.ds(start, piece)],
                table[p * piece : (p + 1) * piece, :],
                preferred_element_type=jnp.float32,
            )
            total = product if total is None else total + product
        turned = total.T
        summed = turned[:width] + turned[width:]
        for m in range(tap_count):
            window[frame + edge - m] += summed[m * columns : (m + 1) * columns]

    for spot in range(frame_count + edge):
        parts[:, spot, :] = window[spot]

    for c in range(channels):
        now = jnp.concatenate([parts[c, :frame_count], parts[channels + c, :frame_count]], axis=0)
        high = now.astype(jnp.bfloat16)
        low = now - high.astype(jnp.float32)
        low = jnp.concatenate([low[:4], low[frame_count : frame_count + 4]], axis=0)
        tail = jnp.concatenate(
            [parts[c, frame_count : frame_count + 4], parts[channels + c, frame_count : frame_count + 4]],
            axis=0,
        )
        sublane = lax.broadcasted_iota(jnp.int32, tail.shape, 0)
        tail = jnp.where(sublane % 4 < edge, tail, 0.0)
        tail_high = tail.astype(jnp.bfloat16).astype(jnp.float32)
        tail_low = tail - tail_high
        extra = jnp.concatenate(
            [jnp.where(later_block, low, tail_high), jnp.where(later_block, 0.0, tail_low)], axis=0
        ).astype(jnp.bfloat16)
        out_ref[c] = jnp.concatenate([high, extra], axis=0)


def join_kernel(slots, out_ref):
    channels, rows, feed_count = slots.shape
    frame_count = rows // 4
    half = channels // TIME_BLOCKS
    for p in range(half):
        first = slots[p].astype(jnp.float32)
        second = slots[half + p].astype(jnp.float32)
        extra = (
            first[2 * frame_count : 3 * frame_count]
            + first[3 * frame_count :]
            + second[2 * frame_count : 3 * frame_count]
        )
        zero = jnp.zeros((frame_count - 4, feed_count), jnp.float32)
        extra = jnp.concatenate([extra[:4], zero, extra[4:8], zero], axis=0)
        fixed = second[: 2 * frame_count] + extra
        for o in range(out_ref.shape[0]):
            out_ref[o, p, : 2 * frame_count] = slots[p, : 2 * frame_count]
            out_ref[o, p, 2 * frame_count :] = fixed.astype(jnp.bfloat16)


def correlate_kernel(scale, got, out_hbm, right, left, out_buf, sems):
    owners, half, rows, feed_count = got.shape
    frame_count = rows // 4
    total_feeds = right.shape[1]
    blocks = left.shape[0]
    block_rows = left.shape[1] // 2
    my_place = lax.axis_index("feed") % owners

    for o in range(owners):
        for p in range(half):
            start = (p * owners + o) * feed_count
            right[:, start : start + feed_count] = got[o, p]
    row_start = my_place * ROWS_DEV
    mine = right[:, pl.ds(pl.multiple_of(row_start, ROWS_DEV), ROWS_DEV)].astype(jnp.float32)
    halves = [mine[k * frame_count : (k + 1) * frame_count] for k in range(4)]
    swapped = jnp.concatenate([halves[1], -halves[0], halves[3], -halves[2]], axis=0)
    left[:, :block_rows, :] = mine.T.astype(jnp.bfloat16).reshape(blocks, block_rows, rows)
    left[:, block_rows:, :] = swapped.T.astype(jnp.bfloat16).reshape(blocks, block_rows, rows)

    def store(block):
        span = pl.ds(pl.multiple_of(block * block_rows, block_rows), block_rows)
        return pltpu.make_async_copy(out_buf.at[span], out_hbm.at[span], sems.at[block])

    @pl.loop(0, blocks)
    def _(block):
        product = jnp.dot(left[block], right[...], preferred_element_type=jnp.float32) * scale
        span = pl.ds(pl.multiple_of(block * block_rows, block_rows), block_rows)
        out_buf[span, :total_feeds] = product[:block_rows]
        out_buf[span, total_feeds:] = product[block_rows:]
        store(block).start()

    @pl.loop(0, blocks)
    def _(block):
        store(block).wait()


def body(samples, pfb_taps):
    feed_count = samples.shape[1]
    tap_count, fft_len = pfb_taps.shape
    frame_count = samples.shape[2] // fft_len
    devices = lax.axis_size("feed")
    total_feeds = feed_count * devices // TIME_BLOCKS
    channels = devices * ROWS_DEV // total_feeds
    owners = total_feeds // ROWS_DEV
    half = channels // TIME_BLOCKS
    spectra_count = TIME_BLOCKS * frame_count
    columns = 2 * channels
    rows = 4 * frame_count
    dft = jnp.asarray(dft_rows(fft_len, FIRST_CH, channels))
    in_vmem = pl.BlockSpec(memory_space=pltpu.VMEM)
    sent = pl.pallas_call(
        functools.partial(spectra_kernel, owners),
        out_shape=jax.ShapeDtypeStruct((channels, rows, feed_count), jnp.bfloat16),
        in_specs=[pl.BlockSpec(memory_space=pl.ANY), in_vmem, in_vmem],
        out_specs=in_vmem,
        scratch_shapes=[
            pltpu.VMEM((feed_count, samples.shape[2]), jnp.bfloat16),
            pltpu.VMEM((fft_len, 2 * tap_count * columns), jnp.bfloat16),
            pltpu.VMEM((frame_count + tap_count - 1, columns, feed_count), jnp.float32),
            pltpu.VMEM((columns, 2 * frame_count, feed_count), jnp.float32),
            pltpu.SemaphoreType.DMA((frame_count * PIECES,)),
        ],
        compiler_params=pltpu.CompilerParams(vmem_limit_bytes=56 * 2**20),
        name="spectra",
    )(samples, pfb_taps, dft)

    lines = [[z * owners + q for z in range(channels)] for q in range(owners)]
    planes = [[z * owners + q for q in range(owners)] for z in range(channels)]
    arrived = lax.all_to_all(sent, "feed", 0, 0, axis_index_groups=lines, tiled=True)
    joined = pl.pallas_call(
        join_kernel,
        out_shape=jax.ShapeDtypeStruct((owners, half, rows, feed_count), jnp.bfloat16),
        in_specs=[in_vmem],
        out_specs=in_vmem,
        name="join",
    )(arrived)
    spread = lax.all_to_all(joined, "feed", 0, 0, axis_index_groups=planes, tiled=True)
    blocks = ROWS_DEV // BLOCK_ROWS
    return pl.pallas_call(
        functools.partial(correlate_kernel, 1.0 / spectra_count),
        out_shape=jax.ShapeDtypeStruct((ROWS_DEV, 2 * total_feeds), jnp.float32),
        in_specs=[in_vmem],
        out_specs=pl.BlockSpec(memory_space=pl.ANY),
        scratch_shapes=[
            pltpu.VMEM((rows, total_feeds), jnp.bfloat16),
            pltpu.VMEM((blocks, 2 * BLOCK_ROWS, rows), jnp.bfloat16),
            pltpu.VMEM((ROWS_DEV, 2 * total_feeds), jnp.float32),
            pltpu.SemaphoreType.DMA((blocks,)),
        ],
        compiler_params=pltpu.CompilerParams(vmem_limit_bytes=32 * 2**20),
        name="correlate",
    )(spread)


def solution(mesh):
    placed = (P(("grp", "feed"), None, None), P())
    return jax.shard_map(
        body, mesh=mesh, in_specs=placed, out_specs=P(("grp", "feed"), None), check_vma=False
    )
```

```python
import functools
import math

import jax
import jax.numpy as jnp
import numpy as np
from jax import lax
from jax.experimental import pallas as pl
from jax.experimental.pallas import tpu as pltpu
from jax.sharding import PartitionSpec as P

FIRST_CH = 1536
TIME_BLOCKS = 2
ROWS_DEV = 512
PIECES = 2
AHEAD = 2
TABLE_STEP = 1024
BLOCK_ROWS = 64


def dft_rows(fft_len, first_channel, channel_count):
    sample_ids = np.arange(fft_len, dtype=np.int64)
    channel_ids = first_channel + np.arange(channel_count, dtype=np.int64)
    phase = channel_ids[:, None] * sample_ids[None, :] % fft_len
    angle = phase.astype(np.float64) * (2.0 * math.pi / fft_len)
    return np.concatenate([np.cos(angle), -np.sin(angle)], axis=0).astype(np.float32)


def spectra_kernel(
    owners, x_hbm, taps_ref, dft_ref, out_ref, x_buf, table, raw, window, parts, sems
):
    channels = dft_ref.shape[0] // 2
    tap_count, fft_len = taps_ref.shape
    columns = 2 * channels
    frame_count = x_hbm.shape[2] // fft_len
    piece = fft_len // PIECES
    edge = tap_count - 1
    width = tap_count * columns
    my_plane = lax.axis_index("feed") // owners
    later_block = my_plane >= channels // TIME_BLOCKS

    def fetch(index):
        span = pl.ds(pl.multiple_of(index * piece, piece), piece)
        return pltpu.make_async_copy(x_hbm.at[0, :, span], x_buf.at[:, span], sems.at[index])

    for index in range(AHEAD * PIECES):
        fetch(index).start()

    window[...] = jnp.zeros_like(window)

    @pl.loop(0, fft_len // TABLE_STEP)
    def _(index):
        span = pl.ds(pl.multiple_of(index * TABLE_STEP, TABLE_STEP), TABLE_STEP)
        dft = dft_ref[:, span]
        scaled = jnp.concatenate([taps_ref[m : m + 1, span] * dft for m in range(tap_count)], axis=0)
        high = scaled.astype(jnp.bfloat16).astype(jnp.float32)
        both = jnp.concatenate([high, scaled - high], axis=0)
        table[span, :] = both.T.astype(jnp.bfloat16)

    def fold(frame, total):
        turned = total.T
        summed = turned[:width] + turned[width:]
        for m in range(tap_count):
            window[frame + edge - m] += summed[m * columns : (m + 1) * columns]

    raw[...] = jnp.zeros_like(raw)

    @pl.loop(0, frame_count)
    def _(frame):
        for p in range(PIECES):
            fetch(frame * PIECES + p).wait()

        @pl.when(frame + AHEAD < frame_count)
        def _():
            for p in range(PIECES):
                fetch((frame + AHEAD) * PIECES + p).start()

        fold(jnp.maximum(frame - 1, 0), raw[...])
        total = None
        for p in range(PIECES):
            start = pl.multiple_of(frame * fft_len + p * piece, piece)
            product = jnp.dot(
                x_buf[:, pl.ds(start, piece)],
                table[p * piece : (p + 1) * piece, :],
                preferred_element_type=jnp.float32,
            )
            total = product if total is None else total + product
        raw[...] = total

    fold(frame_count - 1, raw[...])

    for spot in range(frame_count + edge):
        parts[:, spot, :] = window[spot]

    for c in range(channels):
        now = jnp.concatenate([parts[c, :frame_count], parts[channels + c, :frame_count]], axis=0)
        high = now.astype(jnp.bfloat16)
        low = now - high.astype(jnp.float32)
        low = jnp.concatenate([low[:4], low[frame_count : frame_count + 4]], axis=0)
        tail = jnp.concatenate(
            [parts[c, frame_count : frame_count + 4], parts[channels + c, frame_count : frame_count + 4]],
            axis=0,
        )
        sublane = lax.broadcasted_iota(jnp.int32, tail.shape, 0)
        tail = jnp.where(sublane % 4 < edge, tail, 0.0)
        tail_high = tail.astype(jnp.bfloat16).astype(jnp.float32)
        tail_low = tail - tail_high
        extra = jnp.concatenate(
            [jnp.where(later_block, low, tail_high), jnp.where(later_block, 0.0, tail_low)], axis=0
        ).astype(jnp.bfloat16)
        out_ref[c] = jnp.concatenate([high, extra], axis=0)


def correlate_kernel(scale, owners, got_hbm, out_hbm, got, right, left, out_buf, got_sem, sems):
    devices, rows, feed_count = got.shape
    group_span = devices // TIME_BLOCKS
    frame_count = rows // 4
    total_feeds = right.shape[1]
    blocks = left.shape[0]
    block_rows = left.shape[1] // 2
    my_place = lax.axis_index("feed") % owners
    load = pltpu.make_async_copy(got_hbm.at[:, lax.axis_index("feed") // owners], got, got_sem)
    load.start()
    load.wait()

    for g in range(group_span):
        span = slice(g * feed_count, (g + 1) * feed_count)
        first = got[g].astype(jnp.float32)
        second = got[group_span + g].astype(jnp.float32)
        extra = (
            first[2 * frame_count : 3 * frame_count]
            + first[3 * frame_count :]
            + second[2 * frame_count : 3 * frame_count]
        )
        zero = jnp.zeros((frame_count - 4, feed_count), jnp.float32)
        extra = jnp.concatenate([extra[:4], zero, extra[4:8], zero], axis=0)
        fixed = second[: 2 * frame_count] + extra
        right[: 2 * frame_count, span] = got[g, : 2 * frame_count]
        right[2 * frame_count :, span] = fixed.astype(jnp.bfloat16)
    row_start = my_place * ROWS_DEV
    mine = right[:, pl.ds(pl.multiple_of(row_start, ROWS_DEV), ROWS_DEV)].astype(jnp.float32)
    halves = [mine[k * frame_count : (k + 1) * frame_count] for k in range(4)]
    swapped = jnp.concatenate([halves[1], -halves[0], halves[3], -halves[2]], axis=0)
    left[:, :block_rows, :] = mine.T.astype(jnp.bfloat16).reshape(blocks, block_rows, rows)
    left[:, block_rows:, :] = swapped.T.astype(jnp.bfloat16).reshape(blocks, block_rows, rows)

    def store(block):
        span = pl.ds(pl.multiple_of(block * block_rows, block_rows), block_rows)
        return pltpu.make_async_copy(out_buf.at[span], out_hbm.at[span], sems.at[block])

    @pl.loop(0, blocks)
    def _(block):
        product = jnp.dot(left[block], right[...], preferred_element_type=jnp.float32) * scale
        span = pl.ds(pl.multiple_of(block * block_rows, block_rows), block_rows)
        out_buf[span, :total_feeds] = product[:block_rows]
        out_buf[span, total_feeds:] = product[block_rows:]
        store(block).start()

    @pl.loop(0, blocks)
    def _(block):
        store(block).wait()


def body(samples, pfb_taps):
    feed_count = samples.shape[1]
    tap_count, fft_len = pfb_taps.shape
    frame_count = samples.shape[2] // fft_len
    devices = lax.axis_size("feed")
    total_feeds = feed_count * devices // TIME_BLOCKS
    channels = devices * ROWS_DEV // total_feeds
    owners = total_feeds // ROWS_DEV
    half = channels // TIME_BLOCKS
    spectra_count = TIME_BLOCKS * frame_count
    columns = 2 * channels
    rows = 4 * frame_count
    dft = jnp.asarray(dft_rows(fft_len, FIRST_CH, channels))
    in_vmem = pl.BlockSpec(memory_space=pltpu.VMEM)
    sent = pl.pallas_call(
        functools.partial(spectra_kernel, owners),
        out_shape=jax.ShapeDtypeStruct((channels, rows, feed_count), jnp.bfloat16),
        in_specs=[pl.BlockSpec(memory_space=pl.ANY), in_vmem, in_vmem],
        out_specs=in_vmem,
        scratch_shapes=[
            pltpu.VMEM((feed_count, samples.shape[2]), jnp.bfloat16),
            pltpu.VMEM((fft_len, 2 * tap_count * columns), jnp.bfloat16),
            pltpu.VMEM((feed_count, 2 * tap_count * columns), jnp.float32),
            pltpu.VMEM((frame_count + tap_count - 1, columns, feed_count), jnp.float32),
            pltpu.VMEM((columns, 2 * frame_count, feed_count), jnp.float32),
            pltpu.SemaphoreType.DMA((frame_count * PIECES,)),
        ],
        compiler_params=pltpu.CompilerParams(vmem_limit_bytes=56 * 2**20),
        name="spectra",
    )(samples, pfb_taps, dft)

    spread = lax.all_gather(sent, "feed", axis=0, tiled=False)
    blocks = ROWS_DEV // BLOCK_ROWS
    return pl.pallas_call(
        functools.partial(correlate_kernel, 1.0 / spectra_count, owners),
        out_shape=jax.ShapeDtypeStruct((ROWS_DEV, 2 * total_feeds), jnp.float32),
        in_specs=[pl.BlockSpec(memory_space=pl.ANY)],
        out_specs=pl.BlockSpec(memory_space=pl.ANY),
        scratch_shapes=[
            pltpu.VMEM((devices, rows, feed_count), jnp.bfloat16),
            pltpu.VMEM((rows, total_feeds), jnp.bfloat16),
            pltpu.VMEM((blocks, 2 * BLOCK_ROWS, rows), jnp.bfloat16),
            pltpu.VMEM((ROWS_DEV, 2 * total_feeds), jnp.float32),
            pltpu.SemaphoreType.DMA,
            pltpu.SemaphoreType.DMA((blocks,)),
        ],
        compiler_params=pltpu.CompilerParams(vmem_limit_bytes=60 * 2**20),
        name="correlate",
    )(spread)


def solution(mesh):
    placed = (P(("grp", "feed"), None, None), P())
    return jax.shard_map(
        body, mesh=mesh, in_specs=placed, out_specs=P(("grp", "feed"), None), check_vma=False
    )
```

```python
import functools
import math

import jax
import jax.numpy as jnp
import numpy as np
from jax import lax
from jax.experimental import pallas as pl
from jax.experimental.pallas import tpu as pltpu
from jax.sharding import PartitionSpec as P

FIRST_CH = 1536
TIME_BLOCKS = 2
ROWS_DEV = 512
CORES = 2
DEPTH = 1024
BLOCK_ROWS = 64


def dft_rows(fft_len, first_channel, channel_count):
    sample_ids = np.arange(fft_len, dtype=np.int64)
    channel_ids = first_channel + np.arange(channel_count, dtype=np.int64)
    phase = channel_ids[:, None] * sample_ids[None, :] % fft_len
    angle = phase.astype(np.float64) * (2.0 * math.pi / fft_len)
    return np.concatenate([np.cos(angle), -np.sin(angle)], axis=0).astype(np.float32)


def spectra_kernel(
    owners, x_hbm, taps_ref, dft_ref, out_ref, x_buf, table, total, parts, sems
):
    tap_count, fft_len = taps_ref.shape
    columns = dft_ref.shape[0]
    channels = columns // 2
    feed_count = x_hbm.shape[1]
    frame_count = x_hbm.shape[2] // fft_len
    edge = tap_count - 1
    width = tap_count * columns
    later_block = lax.axis_index("feed") >= channels * owners // TIME_BLOCKS

    def fetch(index):
        piece, frame = index // frame_count, lax.rem(index, frame_count)
        source = pl.ds(pl.multiple_of(frame * fft_len + piece * DEPTH, DEPTH), DEPTH)
        rows = pl.ds(pl.multiple_of(frame * feed_count, feed_count), feed_count)
        span = pl.ds(pl.multiple_of(piece * DEPTH, DEPTH), DEPTH)
        return pltpu.make_async_copy(x_hbm.at[0, :, source], x_buf.at[rows, span], sems.at[index])

    @pl.loop(0, frame_count * fft_len // DEPTH)
    def _(index):
        fetch(index).start()

    total[...] = jnp.zeros_like(total)

    @pl.loop(0, fft_len // DEPTH)
    def _(index):
        span = pl.ds(pl.multiple_of(index * DEPTH, DEPTH), DEPTH)
        dft = dft_ref[:, span]
        scaled = jnp.concatenate([taps_ref[m : m + 1, span] * dft for m in range(tap_count)], axis=0)
        high = scaled.astype(jnp.bfloat16).astype(jnp.float32)
        both = jnp.concatenate([high, scaled - high], axis=0)
        table[span, :] = both.T.astype(jnp.bfloat16)

    @pl.loop(0, fft_len // DEPTH)
    def _(piece):
        @pl.loop(0, frame_count)
        def _(frame):
            fetch(piece * frame_count + frame).wait()

        span = pl.ds(pl.multiple_of(piece * DEPTH, DEPTH), DEPTH)
        total[...] += jnp.dot(x_buf[:, span], table[span, :], preferred_element_type=jnp.float32)

    window = [None] * (frame_count + edge)
    for frame in range(frame_count):
        turned = total[frame * feed_count : (frame + 1) * feed_count].T
        summed = turned[:width] + turned[width:]
        for m in range(tap_count):
            term = summed[m * columns : (m + 1) * columns]
            spot = frame + edge - m
            window[spot] = term if window[spot] is None else window[spot] + term
    for spot in range(frame_count + edge):
        parts[:, spot, :] = window[spot]

    copies = out_ref.shape[0] // channels
    for c in range(channels):
        now = jnp.concatenate([parts[c, :frame_count], parts[channels + c, :frame_count]], axis=0)
        high = now.astype(jnp.bfloat16)
        low = now - high.astype(jnp.float32)
        low = jnp.concatenate([low[:4], low[frame_count : frame_count + 4]], axis=0)
        tail = jnp.concatenate(
            [parts[c, frame_count : frame_count + 4], parts[channels + c, frame_count : frame_count + 4]],
            axis=0,
        )
        sublane = lax.broadcasted_iota(jnp.int32, tail.shape, 0)
        tail = jnp.where(sublane % 4 < edge, tail, 0.0)
        tail_high = tail.astype(jnp.bfloat16).astype(jnp.float32)
        tail_low = tail - tail_high
        extra = jnp.concatenate(
            [jnp.where(later_block, low, tail_high), jnp.where(later_block, 0.0, tail_low)], axis=0
        ).astype(jnp.bfloat16)
        whole = jnp.concatenate([high, extra], axis=0)
        for o in range(copies):
            out_ref[c * copies + o] = whole


def correlate_kernel(
    scale, owners, own_ref, other_ref, out_hbm, right, left, out_buf, sems
):
    lines, rows, feed_count = own_ref.shape
    group_span = lines * CORES // TIME_BLOCKS
    frame_count = rows // 4
    total_feeds = right.shape[1]
    blocks = left.shape[0]
    block_rows = left.shape[1] // 2
    my_index = lax.axis_index("feed")
    my_core = my_index % CORES

    def arrived(device):
        mine, core = device // CORES, device % CORES
        return jnp.where(my_core == core, own_ref[mine], other_ref[mine])

    for g in range(group_span):
        span = slice(g * feed_count, (g + 1) * feed_count)
        low, high = arrived(g), arrived(group_span + g)
        first = low.astype(jnp.float32)
        second = high.astype(jnp.float32)
        extra = (
            first[2 * frame_count : 3 * frame_count]
            + first[3 * frame_count :]
            + second[2 * frame_count : 3 * frame_count]
        )
        zero = jnp.zeros((frame_count - 4, feed_count), jnp.float32)
        extra = jnp.concatenate([extra[:4], zero, extra[4:8], zero], axis=0)
        fixed = second[: 2 * frame_count] + extra
        right[: 2 * frame_count, span] = low[: 2 * frame_count]
        right[2 * frame_count :, span] = fixed.astype(jnp.bfloat16)
    row_start = my_index % owners * ROWS_DEV
    mine = right[:, pl.ds(pl.multiple_of(row_start, ROWS_DEV), ROWS_DEV)].astype(jnp.float32)
    halves = [mine[k * frame_count : (k + 1) * frame_count] for k in range(4)]
    swapped = jnp.concatenate([halves[1], -halves[0], halves[3], -halves[2]], axis=0)
    left[:, :block_rows, :] = mine.T.astype(jnp.bfloat16).reshape(blocks, block_rows, rows)
    left[:, block_rows:, :] = swapped.T.astype(jnp.bfloat16).reshape(blocks, block_rows, rows)

    def store(block):
        span = pl.ds(pl.multiple_of(block * block_rows, block_rows), block_rows)
        return pltpu.make_async_copy(out_buf.at[span], out_hbm.at[span], sems.at[block])

    @pl.loop(0, blocks)
    def _(block):
        product = jnp.dot(left[block], right[...], preferred_element_type=jnp.float32) * scale
        span = pl.ds(pl.multiple_of(block * block_rows, block_rows), block_rows)
        out_buf[span, :total_feeds] = product[:block_rows]
        out_buf[span, total_feeds:] = product[block_rows:]
        store(block).start()

    @pl.loop(0, blocks)
    def _(block):
        store(block).wait()


def body(samples, pfb_taps):
    feed_count = samples.shape[1]
    tap_count, fft_len = pfb_taps.shape
    frame_count = samples.shape[2] // fft_len
    devices = lax.axis_size("feed")
    total_feeds = feed_count * devices // TIME_BLOCKS
    channels = devices * ROWS_DEV // total_feeds
    owners = total_feeds // ROWS_DEV
    spectra_count = TIME_BLOCKS * frame_count
    columns = 2 * channels
    rows = 4 * frame_count
    lines = devices // CORES
    dft = jnp.asarray(dft_rows(fft_len, FIRST_CH, channels))
    in_vmem = pl.BlockSpec(memory_space=pltpu.VMEM)
    outgoing = pl.pallas_call(
        functools.partial(spectra_kernel, owners),
        out_shape=jax.ShapeDtypeStruct((lines, rows, feed_count), jnp.bfloat16),
        in_specs=[pl.BlockSpec(memory_space=pl.ANY), in_vmem, in_vmem],
        out_specs=in_vmem,
        scratch_shapes=[
            pltpu.VMEM((frame_count * feed_count, fft_len), jnp.bfloat16),
            pltpu.VMEM((fft_len, 2 * tap_count * columns), jnp.bfloat16),
            pltpu.VMEM((frame_count * feed_count, 2 * tap_count * columns), jnp.float32),
            pltpu.VMEM((columns, 2 * frame_count, feed_count), jnp.float32),
            pltpu.SemaphoreType.DMA((frame_count * fft_len // DEPTH,)),
        ],
        compiler_params=pltpu.CompilerParams(vmem_limit_bytes=56 * 2**20),
        name="spectra",
    )(samples, pfb_taps, dft)
    same_core = [[line * CORES + core for line in range(lines)] for core in range(CORES)]
    own = lax.all_to_all(outgoing, "feed", 0, 0, axis_index_groups=same_core, tiled=True)
    other = lax.ppermute(own, "feed", [(d, d ^ 1) for d in range(devices)])
    blocks = ROWS_DEV // BLOCK_ROWS
    return pl.pallas_call(
        functools.partial(correlate_kernel, 1.0 / spectra_count, owners),
        out_shape=jax.ShapeDtypeStruct((ROWS_DEV, 2 * total_feeds), jnp.float32),
        in_specs=[in_vmem, in_vmem],
        out_specs=pl.BlockSpec(memory_space=pl.ANY),
        scratch_shapes=[
            pltpu.VMEM((rows, total_feeds), jnp.bfloat16),
            pltpu.VMEM((blocks, 2 * BLOCK_ROWS, rows), jnp.bfloat16),
            pltpu.VMEM((ROWS_DEV, 2 * total_feeds), jnp.float32),
            pltpu.SemaphoreType.DMA((blocks,)),
        ],
        compiler_params=pltpu.CompilerParams(vmem_limit_bytes=32 * 2**20),
        name="correlate",
    )(own, other)


def solution(mesh):
    placed = (P(("grp", "feed"), None, None), P())
    return jax.shard_map(
        body, mesh=mesh, in_specs=placed, out_specs=P(("grp", "feed"), None), check_vma=False
    )
```

```python
import functools
import math

import jax
import jax.numpy as jnp
import numpy as np
from jax import lax
from jax.experimental import pallas as pl
from jax.experimental.pallas import tpu as pltpu
from jax.sharding import PartitionSpec as P

FIRST_CH = 1536
TIME_BLOCKS = 2
ROWS_DEV = 512
PIECES = 2
TABLE_STEP = 1024
BLOCK_ROWS = 64


def dft_rows(fft_len, first_channel, channel_count):
    sample_ids = np.arange(fft_len, dtype=np.int64)
    channel_ids = first_channel + np.arange(channel_count, dtype=np.int64)
    phase = channel_ids[:, None] * sample_ids[None, :] % fft_len
    angle = phase.astype(np.float64) * (2.0 * math.pi / fft_len)
    return np.concatenate([np.cos(angle), -np.sin(angle)], axis=0).astype(np.float32)


def spectra_kernel(owners, x_hbm, taps_hbm, dft_hbm, *rest):
    channels = dft_hbm.shape[0] // 2
    outs, (taps_ref, dft_ref, x_buf, table, parts, small_sems, sems) = rest[:channels], rest[channels:]
    tap_count, fft_len = taps_ref.shape
    columns = 2 * channels
    feed_count = x_hbm.shape[1]
    frame_count = x_hbm.shape[2] // fft_len
    piece = fft_len // PIECES
    edge = tap_count - 1
    width = tap_count * columns
    my_plane = lax.axis_index("feed") // owners
    later_block = my_plane >= channels // TIME_BLOCKS

    def fetch(frame):
        source = pl.ds(pl.multiple_of(frame * fft_len, fft_len), fft_len)
        rows = pl.ds(pl.multiple_of(frame * feed_count, feed_count), feed_count)
        return pltpu.make_async_copy(x_hbm.at[0, :, source], x_buf.at[rows], sems.at[frame])

    small = [
        pltpu.make_async_copy(taps_hbm, taps_ref, small_sems.at[0]),
        pltpu.make_async_copy(dft_hbm, dft_ref, small_sems.at[1]),
    ]
    for copy in small:
        copy.start()

    @pl.loop(0, frame_count)
    def _(frame):
        fetch(frame).start()

    for copy in small:
        copy.wait()

    @pl.loop(0, fft_len // TABLE_STEP)
    def _(index):
        span = pl.ds(pl.multiple_of(index * TABLE_STEP, TABLE_STEP), TABLE_STEP)
        dft = dft_ref[:, span]
        scaled = jnp.concatenate([taps_ref[m : m + 1, span] * dft for m in range(tap_count)], axis=0)
        high = scaled.astype(jnp.bfloat16).astype(jnp.float32)
        both = jnp.concatenate([high, scaled - high], axis=0)
        table[span, :] = both.T.astype(jnp.bfloat16)

    window = [None] * (frame_count + edge)

    def fold(first, total):
        for k in range(total.shape[0] // feed_count):
            turned = total[k * feed_count : (k + 1) * feed_count].T
            summed = turned[:width] + turned[width:]
            for m in range(tap_count):
                term = summed[m * columns : (m + 1) * columns]
                spot = first + k + edge - m
                window[spot] = term if window[spot] is None else window[spot] + term

    before = None
    starts = [0, *range(1, frame_count - 1, 2), frame_count - 1, frame_count]
    for first, last in zip(starts[:-1], starts[1:]):
        for frame in range(first, last):
            fetch(frame).wait()
        total = None
        for p in range(PIECES):
            span = slice(p * piece, (p + 1) * piece)
            product = jnp.dot(
                x_buf[first * feed_count : last * feed_count, span],
                table[span, :],
                preferred_element_type=jnp.float32,
            )
            total = product if total is None else total + product
        if before is not None:
            fold(*before)
        before = (first, total)
    fold(*before)

    for spot in range(frame_count + edge):
        parts[:, spot, :] = window[spot]

    for k in range(channels):
        c = lax.bitwise_xor(my_plane, k)
        now = jnp.concatenate([parts[c, :frame_count], parts[channels + c, :frame_count]], axis=0)
        high = now.astype(jnp.bfloat16)
        low = now - high.astype(jnp.float32)
        low = jnp.concatenate([low[:4], low[frame_count : frame_count + 4]], axis=0)
        tail = jnp.concatenate(
            [parts[c, frame_count : frame_count + 4], parts[channels + c, frame_count : frame_count + 4]],
            axis=0,
        )
        sublane = lax.broadcasted_iota(jnp.int32, tail.shape, 0)
        tail = jnp.where(sublane % 4 < edge, tail, 0.0)
        tail_high = tail.astype(jnp.bfloat16).astype(jnp.float32)
        tail_low = tail - tail_high
        extra = jnp.concatenate(
            [jnp.where(later_block, low, tail_high), jnp.where(later_block, 0.0, tail_low)], axis=0
        ).astype(jnp.bfloat16)
        outs[k][...] = jnp.concatenate([high, extra], axis=0)


def join_kernel(owners, *refs):
    channels = len(refs) - 2
    out_ref, slots = refs[channels:]
    rows = slots.shape[1]
    feed_count = slots.shape[2]
    frame_count = rows // 4
    half = channels // TIME_BLOCKS
    my_plane = lax.axis_index("feed") // owners
    for k in range(channels):
        slots[lax.bitwise_xor(my_plane, k)] = refs[k][...]
    for p in range(half):
        first = slots[p].astype(jnp.float32)
        second = slots[half + p].astype(jnp.float32)
        extra = (
            first[2 * frame_count : 3 * frame_count]
            + first[3 * frame_count :]
            + second[2 * frame_count : 3 * frame_count]
        )
        zero = jnp.zeros((frame_count - 4, feed_count), jnp.float32)
        extra = jnp.concatenate([extra[:4], zero, extra[4:8], zero], axis=0)
        fixed = second[: 2 * frame_count] + extra
        out_ref[p, : 2 * frame_count] = slots[p, : 2 * frame_count]
        out_ref[p, 2 * frame_count :] = fixed.astype(jnp.bfloat16)


def correlate_kernel(scale, owners, *refs):
    got, (out_hbm, slots, right, left, out_buf, sems) = refs[:owners], refs[owners:]
    half, rows, feed_count = got[0].shape
    frame_count = rows // 4
    total_feeds = right.shape[1]
    blocks = left.shape[0]
    block_rows = left.shape[1] // 2
    my_place = lax.axis_index("feed") % owners

    for k in range(owners):
        slots[lax.bitwise_xor(my_place, k)] = got[k][...]
    for o in range(owners):
        for p in range(half):
            start = (p * owners + o) * feed_count
            right[:, start : start + feed_count] = slots[o, p]
    row_start = my_place * ROWS_DEV
    mine = right[:, pl.ds(pl.multiple_of(row_start, ROWS_DEV), ROWS_DEV)].astype(jnp.float32)
    halves = [mine[k * frame_count : (k + 1) * frame_count] for k in range(4)]
    swapped = jnp.concatenate([halves[1], -halves[0], halves[3], -halves[2]], axis=0)
    left[:, :block_rows, :] = mine.T.astype(jnp.bfloat16).reshape(blocks, block_rows, rows)
    left[:, block_rows:, :] = swapped.T.astype(jnp.bfloat16).reshape(blocks, block_rows, rows)

    def store(block):
        span = pl.ds(pl.multiple_of(block * block_rows, block_rows), block_rows)
        return pltpu.make_async_copy(out_buf.at[span], out_hbm.at[span], sems.at[block])

    @pl.loop(0, blocks)
    def _(block):
        product = jnp.dot(left[block], right[...], preferred_element_type=jnp.float32) * scale
        span = pl.ds(pl.multiple_of(block * block_rows, block_rows), block_rows)
        out_buf[span, :total_feeds] = product[:block_rows]
        out_buf[span, total_feeds:] = product[block_rows:]
        store(block).start()

    @pl.loop(0, blocks)
    def _(block):
        store(block).wait()


def body(samples, pfb_taps):
    feed_count = samples.shape[1]
    tap_count, fft_len = pfb_taps.shape
    frame_count = samples.shape[2] // fft_len
    devices = lax.axis_size("feed")
    total_feeds = feed_count * devices // TIME_BLOCKS
    channels = devices * ROWS_DEV // total_feeds
    owners = total_feeds // ROWS_DEV
    half = channels // TIME_BLOCKS
    spectra_count = TIME_BLOCKS * frame_count
    columns = 2 * channels
    rows = 4 * frame_count
    dft = jnp.asarray(dft_rows(fft_len, FIRST_CH, channels))
    in_vmem = pl.BlockSpec(memory_space=pltpu.VMEM)
    sent = pl.pallas_call(
        functools.partial(spectra_kernel, owners),
        out_shape=[jax.ShapeDtypeStruct((rows, feed_count), jnp.bfloat16)] * channels,
        in_specs=[pl.BlockSpec(memory_space=pl.ANY)] * 3,
        out_specs=[in_vmem] * channels,
        scratch_shapes=[
            pltpu.VMEM(pfb_taps.shape, jnp.float32),
            pltpu.VMEM(dft.shape, jnp.float32),
            pltpu.VMEM((frame_count * feed_count, fft_len), jnp.bfloat16),
            pltpu.VMEM((fft_len, 2 * tap_count * columns), jnp.bfloat16),
            pltpu.VMEM((columns, 2 * frame_count, feed_count), jnp.float32),
            pltpu.SemaphoreType.DMA((2,)),
            pltpu.SemaphoreType.DMA((frame_count,)),
        ],
        compiler_params=pltpu.CompilerParams(vmem_limit_bytes=55200 * 2**10),
        name="spectra",
    )(samples, pfb_taps, dft)

    def swap(value, bit):
        return lax.ppermute(value, "feed", [(d, d ^ bit) for d in range(devices)])

    held = {k: {0: sent[k]} for k in range(channels)}
    bit = channels // 2
    while bit:
        for k in range(bit, 2 * bit):
            for origin in sorted(held[k]):
                held[k ^ bit][origin ^ bit] = swap(held[k][origin], bit * owners)
        bit //= 2
    arrived = [held[0][k] for k in range(channels)]
    joined = pl.pallas_call(
        functools.partial(join_kernel, owners),
        out_shape=jax.ShapeDtypeStruct((half, rows, feed_count), jnp.bfloat16),
        in_specs=[in_vmem] * channels,
        out_specs=in_vmem,
        scratch_shapes=[pltpu.VMEM((channels, rows, feed_count), jnp.bfloat16)],
        name="join",
    )(*arrived)
    spread = {0: joined}
    bit = owners // 2
    while bit:
        for k in sorted(spread):
            spread[k ^ bit] = swap(spread[k], bit)
        bit //= 2
    blocks = ROWS_DEV // BLOCK_ROWS
    return pl.pallas_call(
        functools.partial(correlate_kernel, 1.0 / spectra_count, owners),
        out_shape=jax.ShapeDtypeStruct((ROWS_DEV, 2 * total_feeds), jnp.float32),
        in_specs=[in_vmem] * owners,
        out_specs=pl.BlockSpec(memory_space=pl.ANY),
        scratch_shapes=[
            pltpu.VMEM((owners, half, rows, feed_count), jnp.bfloat16),
            pltpu.VMEM((rows, total_feeds), jnp.bfloat16),
            pltpu.VMEM((blocks, 2 * BLOCK_ROWS, rows), jnp.bfloat16),
            pltpu.VMEM((ROWS_DEV, 2 * total_feeds), jnp.float32),
            pltpu.SemaphoreType.DMA((blocks,)),
        ],
        compiler_params=pltpu.CompilerParams(vmem_limit_bytes=24 * 2**20),
        name="correlate",
    )(*[spread[k] for k in range(owners)])


def solution(mesh):
    placed = (P(("grp", "feed"), None, None), P())
    return jax.shard_map(
        body, mesh=mesh, in_specs=placed, out_specs=P(("grp", "feed"), None), check_vma=False
    )
```

```python
import functools
import math

import jax
import jax.numpy as jnp
import numpy as np
from jax import lax
from jax.experimental import pallas as pl
from jax.experimental.pallas import tpu as pltpu
from jax.sharding import PartitionSpec as P

FIRST_CH = 1536
TIME_BLOCKS = 2
ROWS_DEV = 512
CORES = 2
GROUP = 8
BLOCK_ROWS = 64


def dft_rows(fft_len, first_channel, channel_count):
    sample_ids = np.arange(fft_len, dtype=np.int64)
    channel_ids = first_channel + np.arange(channel_count, dtype=np.int64)
    phase = channel_ids[:, None] * sample_ids[None, :] % fft_len
    angle = phase.astype(np.float64) * (2.0 * math.pi / fft_len)
    return np.concatenate([np.cos(angle), -np.sin(angle)], axis=0).astype(np.float32)


def pack_kernel(owners, tap_count, product_ref, out_ref, parts):
    groups, frame_count, group_rows, width = product_ref.shape
    width //= 2
    columns = width // tap_count
    channels = columns // 2
    feed_count = groups * group_rows
    edge = tap_count - 1
    later_block = lax.axis_index("feed") >= channels * owners // TIME_BLOCKS

    window = [None] * (frame_count + edge)
    for frame in range(frame_count):
        turned = product_ref[:, frame].reshape(feed_count, 2 * width).T
        summed = turned[:width] + turned[width:]
        for m in range(tap_count):
            term = summed[m * columns : (m + 1) * columns]
            spot = frame + edge - m
            window[spot] = term if window[spot] is None else window[spot] + term
    for spot in range(frame_count + edge):
        parts[:, spot, :] = window[spot]

    copies = out_ref.shape[0] // channels
    for c in range(channels):
        now = jnp.concatenate([parts[c, :frame_count], parts[channels + c, :frame_count]], axis=0)
        high = now.astype(jnp.bfloat16)
        low = now - high.astype(jnp.float32)
        low = jnp.concatenate([low[:4], low[frame_count : frame_count + 4]], axis=0)
        tail = jnp.concatenate(
            [parts[c, frame_count : frame_count + 4], parts[channels + c, frame_count : frame_count + 4]],
            axis=0,
        )
        sublane = lax.broadcasted_iota(jnp.int32, tail.shape, 0)
        tail = jnp.where(sublane % 4 < edge, tail, 0.0)
        tail_high = tail.astype(jnp.bfloat16).astype(jnp.float32)
        tail_low = tail - tail_high
        extra = jnp.concatenate(
            [jnp.where(later_block, low, tail_high), jnp.where(later_block, 0.0, tail_low)], axis=0
        ).astype(jnp.bfloat16)
        whole = jnp.concatenate([high, extra], axis=0)
        for o in range(copies):
            out_ref[c * copies + o] = whole


def correlate_kernel(
    scale, owners, own_ref, other_ref, out_hbm, right, left, out_buf, sems
):
    lines, rows, feed_count = own_ref.shape
    group_span = lines * CORES // TIME_BLOCKS
    frame_count = rows // 4
    total_feeds = right.shape[1]
    blocks = left.shape[0]
    block_rows = left.shape[1] // 2
    my_index = lax.axis_index("feed")
    my_core = my_index % CORES

    def arrived(device):
        mine, core = device // CORES, device % CORES
        return jnp.where(my_core == core, own_ref[mine], other_ref[mine])

    for g in range(group_span):
        span = slice(g * feed_count, (g + 1) * feed_count)
        low, high = arrived(g), arrived(group_span + g)
        first = low.astype(jnp.float32)
        second = high.astype(jnp.float32)
        extra = (
            first[2 * frame_count : 3 * frame_count]
            + first[3 * frame_count :]
            + second[2 * frame_count : 3 * frame_count]
        )
        zero = jnp.zeros((frame_count - 4, feed_count), jnp.float32)
        extra = jnp.concatenate([extra[:4], zero, extra[4:8], zero], axis=0)
        fixed = second[: 2 * frame_count] + extra
        right[: 2 * frame_count, span] = low[: 2 * frame_count]
        right[2 * frame_count :, span] = fixed.astype(jnp.bfloat16)
    row_start = my_index % owners * ROWS_DEV
    mine = right[:, pl.ds(pl.multiple_of(row_start, ROWS_DEV), ROWS_DEV)].astype(jnp.float32)
    halves = [mine[k * frame_count : (k + 1) * frame_count] for k in range(4)]
    swapped = jnp.concatenate([halves[1], -halves[0], halves[3], -halves[2]], axis=0)
    left[:, :block_rows, :] = mine.T.astype(jnp.bfloat16).reshape(blocks, block_rows, rows)
    left[:, block_rows:, :] = swapped.T.astype(jnp.bfloat16).reshape(blocks, block_rows, rows)

    def store(block):
        span = pl.ds(pl.multiple_of(block * block_rows, block_rows), block_rows)
        return pltpu.make_async_copy(out_buf.at[span], out_hbm.at[span], sems.at[block])

    @pl.loop(0, blocks)
    def _(block):
        product = jnp.dot(left[block], right[...], preferred_element_type=jnp.float32) * scale
        span = pl.ds(pl.multiple_of(block * block_rows, block_rows), block_rows)
        out_buf[span, :total_feeds] = product[:block_rows]
        out_buf[span, total_feeds:] = product[block_rows:]
        store(block).start()

    @pl.loop(0, blocks)
    def _(block):
        store(block).wait()


def body(samples, pfb_taps):
    feed_count = samples.shape[1]
    tap_count, fft_len = pfb_taps.shape
    frame_count = samples.shape[2] // fft_len
    devices = lax.axis_size("feed")
    total_feeds = feed_count * devices // TIME_BLOCKS
    channels = devices * ROWS_DEV // total_feeds
    owners = total_feeds // ROWS_DEV
    spectra_count = TIME_BLOCKS * frame_count
    columns = 2 * channels
    rows = 4 * frame_count
    lines = devices // CORES
    dft = jnp.asarray(dft_rows(fft_len, FIRST_CH, channels))
    in_vmem = pl.BlockSpec(memory_space=pltpu.VMEM)
    groups = feed_count // GROUP
    tiled = samples.reshape(groups, GROUP, frame_count, fft_len).transpose(0, 2, 1, 3)
    scaled = (pfb_taps[:, None] * dft).reshape(tap_count * columns, fft_len)
    high = scaled.astype(jnp.bfloat16)
    table = jnp.concatenate([high, (scaled - high.astype(jnp.float32)).astype(jnp.bfloat16)], axis=0)
    product = lax.dot_general(
        tiled.reshape(groups * frame_count * GROUP, fft_len),
        table,
        (((1,), (1,)), ((), ())),
        preferred_element_type=jnp.float32,
    ).reshape(groups, frame_count, GROUP, 2 * tap_count * columns)
    outgoing = pl.pallas_call(
        functools.partial(pack_kernel, owners, tap_count),
        out_shape=jax.ShapeDtypeStruct((lines, rows, feed_count), jnp.bfloat16),
        in_specs=[in_vmem],
        out_specs=in_vmem,
        scratch_shapes=[pltpu.VMEM((columns, 2 * frame_count, feed_count), jnp.float32)],
        compiler_params=pltpu.CompilerParams(vmem_limit_bytes=24 * 2**20),
        name="pack",
    )(product)
    same_core = [[line * CORES + core for line in range(lines)] for core in range(CORES)]
    own = lax.all_to_all(outgoing, "feed", 0, 0, axis_index_groups=same_core, tiled=True)
    other = lax.ppermute(own, "feed", [(d, d ^ 1) for d in range(devices)])
    blocks = ROWS_DEV // BLOCK_ROWS
    return pl.pallas_call(
        functools.partial(correlate_kernel, 1.0 / spectra_count, owners),
        out_shape=jax.ShapeDtypeStruct((ROWS_DEV, 2 * total_feeds), jnp.float32),
        in_specs=[in_vmem, in_vmem],
        out_specs=pl.BlockSpec(memory_space=pl.ANY),
        scratch_shapes=[
            pltpu.VMEM((rows, total_feeds), jnp.bfloat16),
            pltpu.VMEM((blocks, 2 * BLOCK_ROWS, rows), jnp.bfloat16),
            pltpu.VMEM((ROWS_DEV, 2 * total_feeds), jnp.float32),
            pltpu.SemaphoreType.DMA((blocks,)),
        ],
        compiler_params=pltpu.CompilerParams(vmem_limit_bytes=24 * 2**20),
        name="correlate",
    )(own, other)


def solution(mesh):
    placed = (P(("grp", "feed"), None, None), P())
    return jax.shard_map(
        body, mesh=mesh, in_specs=placed, out_specs=P(("grp", "feed"), None), check_vma=False
    )
```

```python
import functools
import math

import jax
import jax.numpy as jnp
import numpy as np
from jax import lax
from jax.experimental import pallas as pl
from jax.experimental.pallas import tpu as pltpu
from jax.sharding import PartitionSpec as P

FIRST_CH = 1536
TIME_BLOCKS = 2
ROWS_DEV = 512
CORES = 2
PIECES = 4
TABLE_STEP = 1024
BLOCK_ROWS = 64


def dft_rows(fft_len, first_channel, channel_count):
    sample_ids = np.arange(fft_len, dtype=np.int64)
    channel_ids = first_channel + np.arange(channel_count, dtype=np.int64)
    phase = channel_ids[:, None] * sample_ids[None, :] % fft_len
    angle = phase.astype(np.float64) * (2.0 * math.pi / fft_len)
    return np.concatenate([np.cos(angle), -np.sin(angle)], axis=0).astype(np.float32)


def spectra_kernel(
    owners, x_hbm, taps_hbm, dft_hbm, out_ref,
    taps_ref, dft_ref, x_buf, table, raw, window, parts, small_sems, sems,
):
    tap_count, fft_len = taps_ref.shape
    columns = dft_ref.shape[0]
    channels = columns // 2
    frame_count = x_hbm.shape[2] // fft_len
    piece = fft_len // PIECES
    edge = tap_count - 1
    width = tap_count * columns
    later_block = lax.axis_index("feed") >= channels * owners // TIME_BLOCKS

    small = [
        pltpu.make_async_copy(taps_hbm, taps_ref, small_sems.at[0]),
        pltpu.make_async_copy(dft_hbm, dft_ref, small_sems.at[1]),
    ]
    for copy in small:
        copy.start()

    def fetch(index):
        span = pl.ds(pl.multiple_of(index * piece, piece), piece)
        return pltpu.make_async_copy(x_hbm.at[0, :, span], x_buf.at[:, span], sems.at[index])

    @pl.loop(0, frame_count * PIECES)
    def _(index):
        fetch(index).start()

    window[...] = jnp.zeros_like(window)
    raw[...] = jnp.zeros_like(raw)
    for copy in small:
        copy.wait()

    @pl.loop(0, fft_len // TABLE_STEP)
    def _(index):
        span = pl.ds(pl.multiple_of(index * TABLE_STEP, TABLE_STEP), TABLE_STEP)
        dft = dft_ref[:, span]
        scaled = jnp.concatenate([taps_ref[m : m + 1, span] * dft for m in range(tap_count)], axis=0)
        high = scaled.astype(jnp.bfloat16).astype(jnp.float32)
        both = jnp.concatenate([high, scaled - high], axis=0)
        table[span, :] = both.T.astype(jnp.bfloat16)

    def fold(frame, total):
        turned = total.T
        summed = turned[:width] + turned[width:]
        for m in range(tap_count):
            window[frame + edge - m] += summed[m * columns : (m + 1) * columns]

    def two_dots(frame, begin, depth):
        total = None
        for offset in (begin, begin + depth):
            start = pl.multiple_of(frame * fft_len + offset, depth)
            product = jnp.dot(
                x_buf[:, pl.ds(start, depth)],
                table[offset : offset + depth, :],
                preferred_element_type=jnp.float32,
            )
            total = product if total is None else total + product
        return total

    @pl.loop(0, frame_count - 1)
    def _(frame):
        for p in range(PIECES):
            fetch(frame * PIECES + p).wait()
        fold(jnp.maximum(frame - 1, 0), raw[...])
        raw[...] = two_dots(frame, 0, fft_len // 2)

    last = frame_count - 1
    total = None
    for p in range(0, PIECES, 2):
        for k in (p, p + 1):
            fetch(last * PIECES + k).wait()
        if p == 0:
            fold(last - 1, raw[...])
        product = two_dots(last, p * piece, piece)
        total = product if total is None else total + product
    fold(last, total)

    for spot in range(frame_count + edge):
        parts[:, spot, :] = window[spot]

    copies = out_ref.shape[0] // channels
    for c in range(channels):
        now = jnp.concatenate([parts[c, :frame_count], parts[channels + c, :frame_count]], axis=0)
        high = now.astype(jnp.bfloat16)
        low = now - high.astype(jnp.float32)
        low = jnp.concatenate([low[:4], low[frame_count : frame_count + 4]], axis=0)
        tail = jnp.concatenate(
            [parts[c, frame_count : frame_count + 4], parts[channels + c, frame_count : frame_count + 4]],
            axis=0,
        )
        sublane = lax.broadcasted_iota(jnp.int32, tail.shape, 0)
        tail = jnp.where(sublane % 4 < edge, tail, 0.0)
        tail_high = tail.astype(jnp.bfloat16).astype(jnp.float32)
        tail_low = tail - tail_high
        extra = jnp.concatenate(
            [jnp.where(later_block, low, tail_high), jnp.where(later_block, 0.0, tail_low)], axis=0
        ).astype(jnp.bfloat16)
        whole = jnp.concatenate([high, extra], axis=0)
        for o in range(copies):
            out_ref[c * copies + o] = whole


def correlate_kernel(
    scale, owners, own_ref, other_ref, out_hbm, right, left, out_buf, sems
):
    lines, rows, feed_count = own_ref.shape
    group_span = lines * CORES // TIME_BLOCKS
    frame_count = rows // 4
    total_feeds = right.shape[1]
    blocks = left.shape[0]
    block_rows = left.shape[1] // 2
    my_index = lax.axis_index("feed")
    my_core = my_index % CORES

    def arrived(device):
        mine, core = device // CORES, device % CORES
        return jnp.where(my_core == core, own_ref[mine], other_ref[mine])

    for g in range(group_span):
        span = slice(g * feed_count, (g + 1) * feed_count)
        low, high = arrived(g), arrived(group_span + g)
        first = low.astype(jnp.float32)
        second = high.astype(jnp.float32)
        extra = (
            first[2 * frame_count : 3 * frame_count]
            + first[3 * frame_count :]
            + second[2 * frame_count : 3 * frame_count]
        )
        zero = jnp.zeros((frame_count - 4, feed_count), jnp.float32)
        extra = jnp.concatenate([extra[:4], zero, extra[4:8], zero], axis=0)
        fixed = second[: 2 * frame_count] + extra
        right[: 2 * frame_count, span] = low[: 2 * frame_count]
        right[2 * frame_count :, span] = fixed.astype(jnp.bfloat16)
    row_start = my_index % owners * ROWS_DEV
    mine = right[:, pl.ds(pl.multiple_of(row_start, ROWS_DEV), ROWS_DEV)].astype(jnp.float32)
    halves = [mine[k * frame_count : (k + 1) * frame_count] for k in range(4)]
    swapped = jnp.concatenate([halves[1], -halves[0], halves[3], -halves[2]], axis=0)
    left[:, :block_rows, :] = mine.T.astype(jnp.bfloat16).reshape(blocks, block_rows, rows)
    left[:, block_rows:, :] = swapped.T.astype(jnp.bfloat16).reshape(blocks, block_rows, rows)

    def store(block):
        span = pl.ds(pl.multiple_of(block * block_rows, block_rows), block_rows)
        return pltpu.make_async_copy(out_buf.at[span], out_hbm.at[span], sems.at[block])

    @pl.loop(0, blocks)
    def _(block):
        product = jnp.dot(left[block], right[...], preferred_element_type=jnp.float32) * scale
        span = pl.ds(pl.multiple_of(block * block_rows, block_rows), block_rows)
        out_buf[span, :total_feeds] = product[:block_rows]
        out_buf[span, total_feeds:] = product[block_rows:]
        store(block).start()

    @pl.loop(0, blocks)
    def _(block):
        store(block).wait()


def body(samples, pfb_taps):
    feed_count = samples.shape[1]
    tap_count, fft_len = pfb_taps.shape
    frame_count = samples.shape[2] // fft_len
    devices = lax.axis_size("feed")
    total_feeds = feed_count * devices // TIME_BLOCKS
    channels = devices * ROWS_DEV // total_feeds
    owners = total_feeds // ROWS_DEV
    spectra_count = TIME_BLOCKS * frame_count
    columns = 2 * channels
    rows = 4 * frame_count
    lines = devices // CORES
    dft = jnp.asarray(dft_rows(fft_len, FIRST_CH, channels))
    in_vmem = pl.BlockSpec(memory_space=pltpu.VMEM)
    outgoing = pl.pallas_call(
        functools.partial(spectra_kernel, owners),
        out_shape=jax.ShapeDtypeStruct((lines, rows, feed_count), jnp.bfloat16),
        in_specs=[pl.BlockSpec(memory_space=pl.ANY)] * 3,
        out_specs=in_vmem,
        scratch_shapes=[
            pltpu.VMEM(pfb_taps.shape, jnp.float32),
            pltpu.VMEM(dft.shape, jnp.float32),
            pltpu.VMEM((feed_count, samples.shape[2]), jnp.bfloat16),
            pltpu.VMEM((fft_len, 2 * tap_count * columns), jnp.bfloat16),
            pltpu.VMEM((feed_count, 2 * tap_count * columns), jnp.float32),
            pltpu.VMEM((frame_count + tap_count - 1, columns, feed_count), jnp.float32),
            pltpu.VMEM((columns, 2 * frame_count, feed_count), jnp.float32),
            pltpu.SemaphoreType.DMA((2,)),
            pltpu.SemaphoreType.DMA((frame_count * PIECES,)),
        ],
        compiler_params=pltpu.CompilerParams(vmem_limit_bytes=56 * 2**20),
        name="spectra",
    )(samples, pfb_taps, dft)
    same_core = [[line * CORES + core for line in range(lines)] for core in range(CORES)]
    own = lax.all_to_all(outgoing, "feed", 0, 0, axis_index_groups=same_core, tiled=True)
    other = lax.ppermute(own, "feed", [(d, d ^ 1) for d in range(devices)])
    blocks = ROWS_DEV // BLOCK_ROWS
    return pl.pallas_call(
        functools.partial(correlate_kernel, 1.0 / spectra_count, owners),
        out_shape=jax.ShapeDtypeStruct((ROWS_DEV, 2 * total_feeds), jnp.float32),
        in_specs=[in_vmem, in_vmem],
        out_specs=pl.BlockSpec(memory_space=pl.ANY),
        scratch_shapes=[
            pltpu.VMEM((rows, total_feeds), jnp.bfloat16),
            pltpu.VMEM((blocks, 2 * BLOCK_ROWS, rows), jnp.bfloat16),
            pltpu.VMEM((ROWS_DEV, 2 * total_feeds), jnp.float32),
            pltpu.SemaphoreType.DMA((blocks,)),
        ],
        compiler_params=pltpu.CompilerParams(vmem_limit_bytes=32 * 2**20),
        name="correlate",
    )(own, other)


def solution(mesh):
    placed = (P(("grp", "feed"), None, None), P())
    return jax.shard_map(
        body, mesh=mesh, in_specs=placed, out_specs=P(("grp", "feed"), None), check_vma=False
    )
```

```python
import functools
import math

import jax
import jax.numpy as jnp
import numpy as np
from jax import lax
from jax.experimental import pallas as pl
from jax.experimental.pallas import tpu as pltpu
from jax.sharding import PartitionSpec as P

FIRST_CH = 1536
TIME_BLOCKS = 2
ROWS_DEV = 512
CORES = 2
GROUP = 8
BLOCKS = 8
PIECES = 4
TABLE_STEP = 1024
BLOCK_ROWS = 64


def dft_rows(fft_len, first_channel, channel_count):
    sample_ids = np.arange(fft_len, dtype=np.int64)
    channel_ids = first_channel + np.arange(channel_count, dtype=np.int64)
    phase = channel_ids[:, None] * sample_ids[None, :] % fft_len
    angle = phase.astype(np.float64) * (2.0 * math.pi / fft_len)
    return np.concatenate([np.cos(angle), -np.sin(angle)], axis=0).astype(np.float32)


def spectra_kernel(
    owners, x_hbm, taps_hbm, dft_hbm, out_ref,
    taps_ref, dft_ref, x_buf, table, products, parts, small_sems, sems,
):
    tap_count, fft_len = taps_ref.shape
    columns = dft_ref.shape[0]
    channels = columns // 2
    groups, frame_count, _, _ = products.shape
    feed_count = groups * GROUP
    steps = min(BLOCKS, groups)
    block_groups = groups // steps
    block_rows = block_groups * frame_count * GROUP
    piece = fft_len // PIECES
    edge = tap_count - 1
    width = tap_count * columns
    later_block = lax.axis_index("feed") >= channels * owners // TIME_BLOCKS

    small = [
        pltpu.make_async_copy(taps_hbm, taps_ref, small_sems.at[0]),
        pltpu.make_async_copy(dft_hbm, dft_ref, small_sems.at[1]),
    ]
    for copy in small:
        copy.start()

    def fetch_rows(block):
        rows = pl.ds(pl.multiple_of(block * block_rows, block_rows), block_rows)
        return pltpu.make_async_copy(x_hbm.at[rows], x_buf.at[rows], sems.at[block])

    def fetch_piece(p):
        rows = pl.ds((steps - 1) * block_rows, block_rows)
        span = pl.ds(p * piece, piece)
        return pltpu.make_async_copy(
            x_hbm.at[rows, span], x_buf.at[rows, span], sems.at[steps - 1 + p]
        )

    @pl.loop(0, steps - 1)
    def _(block):
        fetch_rows(block).start()

    for p in range(PIECES):
        fetch_piece(p).start()
    for copy in small:
        copy.wait()

    @pl.loop(0, fft_len // TABLE_STEP)
    def _(index):
        span = pl.ds(pl.multiple_of(index * TABLE_STEP, TABLE_STEP), TABLE_STEP)
        dft = dft_ref[:, span]
        scaled = jnp.concatenate([taps_ref[m : m + 1, span] * dft for m in range(tap_count)], axis=0)
        high = scaled.astype(jnp.bfloat16).astype(jnp.float32)
        both = jnp.concatenate([high, scaled - high], axis=0)
        table[span, :] = both.T.astype(jnp.bfloat16)

    def two_dots(block, begin, depth):
        rows = pl.ds(pl.multiple_of(block * block_rows, block_rows), block_rows)
        total = None
        for offset in (begin, begin + depth):
            product = jnp.dot(
                x_buf[rows, offset : offset + depth],
                table[offset : offset + depth, :],
                preferred_element_type=jnp.float32,
            )
            total = product if total is None else total + product
        return total.reshape(block_groups, frame_count, GROUP, 2 * width)

    def place(block):
        return pl.ds(block * block_groups, block_groups)

    @pl.loop(0, steps - 1)
    def _(block):
        fetch_rows(block).wait()
        products[place(block)] = two_dots(block, 0, fft_len // 2)

    total = None
    for p in range(0, PIECES, 2):
        for k in (p, p + 1):
            fetch_piece(k).wait()
        product = two_dots(steps - 1, p * piece, piece)
        total = product if total is None else total + product
    products[place(steps - 1)] = total

    window = [None] * (frame_count + edge)
    for frame in range(frame_count):
        turned = products[:, frame].reshape(feed_count, 2 * width).T
        summed = turned[:width] + turned[width:]
        for m in range(tap_count):
            term = summed[m * columns : (m + 1) * columns]
            spot = frame + edge - m
            window[spot] = term if window[spot] is None else window[spot] + term
    for spot in range(frame_count + edge):
        parts[:, spot, :] = window[spot]

    copies = out_ref.shape[0] // channels
    for c in range(channels):
        now = jnp.concatenate([parts[c, :frame_count], parts[channels + c, :frame_count]], axis=0)
        high = now.astype(jnp.bfloat16)
        low = now - high.astype(jnp.float32)
        low = jnp.concatenate([low[:4], low[frame_count : frame_count + 4]], axis=0)
        tail = jnp.concatenate(
            [parts[c, frame_count : frame_count + 4], parts[channels + c, frame_count : frame_count + 4]],
            axis=0,
        )
        sublane = lax.broadcasted_iota(jnp.int32, tail.shape, 0)
        tail = jnp.where(sublane % 4 < edge, tail, 0.0)
        tail_high = tail.astype(jnp.bfloat16).astype(jnp.float32)
        tail_low = tail - tail_high
        extra = jnp.concatenate(
            [jnp.where(later_block, low, tail_high), jnp.where(later_block, 0.0, tail_low)], axis=0
        ).astype(jnp.bfloat16)
        whole = jnp.concatenate([high, extra], axis=0)
        for o in range(copies):
            out_ref[c * copies + o] = whole


def correlate_kernel(
    scale, owners, own_ref, other_ref, out_hbm, right, left, out_buf, sems
):
    lines, rows, feed_count = own_ref.shape
    group_span = lines * CORES // TIME_BLOCKS
    frame_count = rows // 4
    total_feeds = right.shape[1]
    blocks = left.shape[0]
    block_rows = left.shape[1] // 2
    my_index = lax.axis_index("feed")
    my_core = my_index % CORES

    def arrived(device):
        mine, core = device // CORES, device % CORES
        return jnp.where(my_core == core, own_ref[mine], other_ref[mine])

    for g in range(group_span):
        span = slice(g * feed_count, (g + 1) * feed_count)
        low, high = arrived(g), arrived(group_span + g)
        first = low.astype(jnp.float32)
        second = high.astype(jnp.float32)
        extra = (
            first[2 * frame_count : 3 * frame_count]
            + first[3 * frame_count :]
            + second[2 * frame_count : 3 * frame_count]
        )
        zero = jnp.zeros((frame_count - 4, feed_count), jnp.float32)
        extra = jnp.concatenate([extra[:4], zero, extra[4:8], zero], axis=0)
        fixed = second[: 2 * frame_count] + extra
        right[: 2 * frame_count, span] = low[: 2 * frame_count]
        right[2 * frame_count :, span] = fixed.astype(jnp.bfloat16)
    row_start = my_index % owners * ROWS_DEV
    mine = right[:, pl.ds(pl.multiple_of(row_start, ROWS_DEV), ROWS_DEV)].astype(jnp.float32)
    halves = [mine[k * frame_count : (k + 1) * frame_count] for k in range(4)]
    swapped = jnp.concatenate([halves[1], -halves[0], halves[3], -halves[2]], axis=0)
    left[:, :block_rows, :] = mine.T.astype(jnp.bfloat16).reshape(blocks, block_rows, rows)
    left[:, block_rows:, :] = swapped.T.astype(jnp.bfloat16).reshape(blocks, block_rows, rows)

    def store(block):
        span = pl.ds(pl.multiple_of(block * block_rows, block_rows), block_rows)
        return pltpu.make_async_copy(out_buf.at[span], out_hbm.at[span], sems.at[block])

    @pl.loop(0, blocks)
    def _(block):
        product = jnp.dot(left[block], right[...], preferred_element_type=jnp.float32) * scale
        span = pl.ds(pl.multiple_of(block * block_rows, block_rows), block_rows)
        out_buf[span, :total_feeds] = product[:block_rows]
        out_buf[span, total_feeds:] = product[block_rows:]
        store(block).start()

    @pl.loop(0, blocks)
    def _(block):
        store(block).wait()


def body(samples, pfb_taps):
    feed_count = samples.shape[1]
    tap_count, fft_len = pfb_taps.shape
    frame_count = samples.shape[2] // fft_len
    devices = lax.axis_size("feed")
    total_feeds = feed_count * devices // TIME_BLOCKS
    channels = devices * ROWS_DEV // total_feeds
    owners = total_feeds // ROWS_DEV
    spectra_count = TIME_BLOCKS * frame_count
    columns = 2 * channels
    rows = 4 * frame_count
    lines = devices // CORES
    dft = jnp.asarray(dft_rows(fft_len, FIRST_CH, channels))
    in_vmem = pl.BlockSpec(memory_space=pltpu.VMEM)
    groups = feed_count // GROUP
    tiled = samples.reshape(groups, GROUP, frame_count, fft_len).transpose(0, 2, 1, 3)
    tiled = tiled.reshape(groups * frame_count * GROUP, fft_len)
    outgoing = pl.pallas_call(
        functools.partial(spectra_kernel, owners),
        out_shape=jax.ShapeDtypeStruct((lines, rows, feed_count), jnp.bfloat16),
        in_specs=[pl.BlockSpec(memory_space=pl.ANY)] * 3,
        out_specs=in_vmem,
        scratch_shapes=[
            pltpu.VMEM(pfb_taps.shape, jnp.float32),
            pltpu.VMEM(dft.shape, jnp.float32),
            pltpu.VMEM(tiled.shape, jnp.bfloat16),
            pltpu.VMEM((fft_len, 2 * tap_count * columns), jnp.bfloat16),
            pltpu.VMEM((groups, frame_count, GROUP, 2 * tap_count * columns), jnp.float32),
            pltpu.VMEM((columns, 2 * frame_count, feed_count), jnp.float32),
            pltpu.SemaphoreType.DMA((2,)),
            pltpu.SemaphoreType.DMA((BLOCKS - 1 + PIECES,)),
        ],
        compiler_params=pltpu.CompilerParams(vmem_limit_bytes=56 * 2**20),
        name="spectra",
    )(tiled, pfb_taps, dft)
    same_core = [[line * CORES + core for line in range(lines)] for core in range(CORES)]
    own = lax.all_to_all(outgoing, "feed", 0, 0, axis_index_groups=same_core, tiled=True)
    other = lax.ppermute(own, "feed", [(d, d ^ 1) for d in range(devices)])
    blocks = ROWS_DEV // BLOCK_ROWS
    return pl.pallas_call(
        functools.partial(correlate_kernel, 1.0 / spectra_count, owners),
        out_shape=jax.ShapeDtypeStruct((ROWS_DEV, 2 * total_feeds), jnp.float32),
        in_specs=[in_vmem, in_vmem],
        out_specs=pl.BlockSpec(memory_space=pl.ANY),
        scratch_shapes=[
            pltpu.VMEM((rows, total_feeds), jnp.bfloat16),
            pltpu.VMEM((blocks, 2 * BLOCK_ROWS, rows), jnp.bfloat16),
            pltpu.VMEM((ROWS_DEV, 2 * total_feeds), jnp.float32),
            pltpu.SemaphoreType.DMA((blocks,)),
        ],
        compiler_params=pltpu.CompilerParams(vmem_limit_bytes=32 * 2**20),
        name="correlate",
    )(own, other)


def solution(mesh):
    placed = (P(("grp", "feed"), None, None), P())
    return jax.shard_map(
        body, mesh=mesh, in_specs=placed, out_specs=P(("grp", "feed"), None), check_vma=False
    )
```

```python
import functools
import math

import jax
import jax.numpy as jnp
import numpy as np
from jax import lax
from jax.experimental import pallas as pl
from jax.experimental.pallas import tpu as pltpu
from jax.sharding import PartitionSpec as P

FIRST_CH = 1536
TIME_BLOCKS = 2
ROWS_DEV = 512
CORES = 2
PIECES = 4
TABLE_STEP = 1024
BLOCK_ROWS = 64


def dft_rows(fft_len, first_channel, channel_count):
    sample_ids = np.arange(fft_len, dtype=np.int64)
    channel_ids = first_channel + np.arange(channel_count, dtype=np.int64)
    phase = channel_ids[:, None] * sample_ids[None, :] % fft_len
    angle = phase.astype(np.float64) * (2.0 * math.pi / fft_len)
    return np.concatenate([np.cos(angle), -np.sin(angle)], axis=0).astype(np.float32)


def spectra_kernel(
    owners, x_hbm, taps_hbm, dft_hbm, out_ref,
    taps_ref, dft_ref, x_buf, table, raw, window, parts, small_sems, sems,
):
    tap_count, fft_len = taps_ref.shape
    columns = dft_ref.shape[0]
    channels = columns // 2
    frame_count = x_hbm.shape[2] // fft_len
    piece = fft_len // PIECES
    edge = tap_count - 1
    width = tap_count * columns
    later_block = lax.axis_index("feed") >= channels * owners // TIME_BLOCKS

    small = [
        pltpu.make_async_copy(taps_hbm, taps_ref, small_sems.at[0]),
        pltpu.make_async_copy(dft_hbm, dft_ref, small_sems.at[1]),
    ]
    for copy in small:
        copy.start()

    def fetch(index):
        span = pl.ds(pl.multiple_of(index * piece, piece), piece)
        return pltpu.make_async_copy(x_hbm.at[0, :, span], x_buf.at[:, span], sems.at[index])

    @pl.loop(0, frame_count * PIECES)
    def _(index):
        fetch(index).start()

    window[...] = jnp.zeros_like(window)
    raw[...] = jnp.zeros_like(raw)
    for copy in small:
        copy.wait()

    @pl.loop(0, fft_len // TABLE_STEP)
    def _(index):
        span = pl.ds(pl.multiple_of(index * TABLE_STEP, TABLE_STEP), TABLE_STEP)
        dft = dft_ref[:, span]
        scaled = jnp.concatenate([taps_ref[m : m + 1, span] * dft for m in range(tap_count)], axis=0)
        high = scaled.astype(jnp.bfloat16).astype(jnp.float32)
        both = jnp.concatenate([high, scaled - high], axis=0)
        table[span, :] = both.T.astype(jnp.bfloat16)

    def fold(frame, total):
        turned = total.T
        summed = turned[:width] + turned[width:]
        for m in range(tap_count):
            window[frame + edge - m] += summed[m * columns : (m + 1) * columns]

    def dots(frame, begin, depth, count):
        terms = []
        for offset in range(begin, begin + count * depth, depth):
            start = pl.multiple_of(frame * fft_len + offset, depth)
            terms.append(
                jnp.dot(
                    x_buf[:, pl.ds(start, depth)],
                    table[offset : offset + depth, :],
                    preferred_element_type=jnp.float32,
                )
            )
        while len(terms) > 1:
            terms = [one + two for one, two in zip(terms[::2], terms[1::2])]
        return terms[0]

    @pl.loop(0, frame_count - 1)
    def _(frame):
        for p in range(PIECES):
            fetch(frame * PIECES + p).wait()
        fold(jnp.maximum(frame - 1, 0), raw[...])
        raw[...] = dots(frame, 0, fft_len // 4, 4)

    last = frame_count - 1
    total = None
    for p in range(0, PIECES, 2):
        for k in (p, p + 1):
            fetch(last * PIECES + k).wait()
        if p == 0:
            fold(last - 1, raw[...])
        product = dots(last, p * piece, piece, 2)
        total = product if total is None else total + product
    fold(last, total)

    for spot in range(frame_count + edge):
        parts[:, spot, :] = window[spot]

    copies = out_ref.shape[0] // channels
    for c in range(channels):
        now = jnp.concatenate([parts[c, :frame_count], parts[channels + c, :frame_count]], axis=0)
        high = now.astype(jnp.bfloat16)
        low = now - high.astype(jnp.float32)
        low = jnp.concatenate([low[:4], low[frame_count : frame_count + 4]], axis=0)
        tail = jnp.concatenate(
            [parts[c, frame_count : frame_count + 4], parts[channels + c, frame_count : frame_count + 4]],
            axis=0,
        )
        sublane = lax.broadcasted_iota(jnp.int32, tail.shape, 0)
        tail = jnp.where(sublane % 4 < edge, tail, 0.0)
        tail_high = tail.astype(jnp.bfloat16).astype(jnp.float32)
        tail_low = tail - tail_high
        extra = jnp.concatenate(
            [jnp.where(later_block, low, tail_high), jnp.where(later_block, 0.0, tail_low)], axis=0
        ).astype(jnp.bfloat16)
        whole = jnp.concatenate([high, extra], axis=0)
        for o in range(copies):
            out_ref[c * copies + o] = whole


def correlate_kernel(
    scale, owners, own_ref, other_ref, out_hbm, right, left, out_buf, sems
):
    lines, rows, feed_count = own_ref.shape
    group_span = lines * CORES // TIME_BLOCKS
    frame_count = rows // 4
    total_feeds = right.shape[1]
    blocks = left.shape[0]
    block_rows = left.shape[1] // 2
    my_index = lax.axis_index("feed")
    my_core = my_index % CORES

    def arrived(device):
        mine, core = device // CORES, device % CORES
        return jnp.where(my_core == core, own_ref[mine], other_ref[mine])

    for g in range(group_span):
        span = slice(g * feed_count, (g + 1) * feed_count)
        low, high = arrived(g), arrived(group_span + g)
        first = low.astype(jnp.float32)
        second = high.astype(jnp.float32)
        extra = (
            first[2 * frame_count : 3 * frame_count]
            + first[3 * frame_count :]
            + second[2 * frame_count : 3 * frame_count]
        )
        zero = jnp.zeros((frame_count - 4, feed_count), jnp.float32)
        extra = jnp.concatenate([extra[:4], zero, extra[4:8], zero], axis=0)
        fixed = second[: 2 * frame_count] + extra
        right[: 2 * frame_count, span] = low[: 2 * frame_count]
        right[2 * frame_count :, span] = fixed.astype(jnp.bfloat16)
    row_start = my_index % owners * ROWS_DEV
    mine = right[:, pl.ds(pl.multiple_of(row_start, ROWS_DEV), ROWS_DEV)].astype(jnp.float32)
    halves = [mine[k * frame_count : (k + 1) * frame_count] for k in range(4)]
    swapped = jnp.concatenate([halves[1], -halves[0], halves[3], -halves[2]], axis=0)
    left[:, :block_rows, :] = mine.T.astype(jnp.bfloat16).reshape(blocks, block_rows, rows)
    left[:, block_rows:, :] = swapped.T.astype(jnp.bfloat16).reshape(blocks, block_rows, rows)

    def store(block):
        span = pl.ds(pl.multiple_of(block * block_rows, block_rows), block_rows)
        return pltpu.make_async_copy(out_buf.at[span], out_hbm.at[span], sems.at[block])

    @pl.loop(0, blocks)
    def _(block):
        product = jnp.dot(left[block], right[...], preferred_element_type=jnp.float32) * scale
        span = pl.ds(pl.multiple_of(block * block_rows, block_rows), block_rows)
        out_buf[span, :total_feeds] = product[:block_rows]
        out_buf[span, total_feeds:] = product[block_rows:]
        store(block).start()

    @pl.loop(0, blocks)
    def _(block):
        store(block).wait()


def body(samples, pfb_taps):
    feed_count = samples.shape[1]
    tap_count, fft_len = pfb_taps.shape
    frame_count = samples.shape[2] // fft_len
    devices = lax.axis_size("feed")
    total_feeds = feed_count * devices // TIME_BLOCKS
    channels = devices * ROWS_DEV // total_feeds
    owners = total_feeds // ROWS_DEV
    spectra_count = TIME_BLOCKS * frame_count
    columns = 2 * channels
    rows = 4 * frame_count
    lines = devices // CORES
    dft = jnp.asarray(dft_rows(fft_len, FIRST_CH, channels))
    in_vmem = pl.BlockSpec(memory_space=pltpu.VMEM)
    outgoing = pl.pallas_call(
        functools.partial(spectra_kernel, owners),
        out_shape=jax.ShapeDtypeStruct((lines, rows, feed_count), jnp.bfloat16),
        in_specs=[pl.BlockSpec(memory_space=pl.ANY)] * 3,
        out_specs=in_vmem,
        scratch_shapes=[
            pltpu.VMEM(pfb_taps.shape, jnp.float32),
            pltpu.VMEM(dft.shape, jnp.float32),
            pltpu.VMEM((feed_count, samples.shape[2]), jnp.bfloat16),
            pltpu.VMEM((fft_len, 2 * tap_count * columns), jnp.bfloat16),
            pltpu.VMEM((feed_count, 2 * tap_count * columns), jnp.float32),
            pltpu.VMEM((frame_count + tap_count - 1, columns, feed_count), jnp.float32),
            pltpu.VMEM((columns, 2 * frame_count, feed_count), jnp.float32),
            pltpu.SemaphoreType.DMA((2,)),
            pltpu.SemaphoreType.DMA((frame_count * PIECES,)),
        ],
        compiler_params=pltpu.CompilerParams(vmem_limit_bytes=56 * 2**20),
        name="spectra",
    )(samples, pfb_taps, dft)
    same_core = [[line * CORES + core for line in range(lines)] for core in range(CORES)]
    own = lax.all_to_all(outgoing, "feed", 0, 0, axis_index_groups=same_core, tiled=True)
    other = lax.ppermute(own, "feed", [(d, d ^ 1) for d in range(devices)])
    blocks = ROWS_DEV // BLOCK_ROWS
    return pl.pallas_call(
        functools.partial(correlate_kernel, 1.0 / spectra_count, owners),
        out_shape=jax.ShapeDtypeStruct((ROWS_DEV, 2 * total_feeds), jnp.float32),
        in_specs=[in_vmem, in_vmem],
        out_specs=pl.BlockSpec(memory_space=pl.ANY),
        scratch_shapes=[
            pltpu.VMEM((rows, total_feeds), jnp.bfloat16),
            pltpu.VMEM((blocks, 2 * BLOCK_ROWS, rows), jnp.bfloat16),
            pltpu.VMEM((ROWS_DEV, 2 * total_feeds), jnp.float32),
            pltpu.SemaphoreType.DMA((blocks,)),
        ],
        compiler_params=pltpu.CompilerParams(vmem_limit_bytes=32 * 2**20),
        name="correlate",
    )(own, other)


def solution(mesh):
    placed = (P(("grp", "feed"), None, None), P())
    return jax.shard_map(
        body, mesh=mesh, in_specs=placed, out_specs=P(("grp", "feed"), None), check_vma=False
    )
```

```python
import functools
import math

import jax
import jax.numpy as jnp
import numpy as np
from jax import lax
from jax.experimental import pallas as pl
from jax.experimental.pallas import tpu as pltpu
from jax.sharding import PartitionSpec as P

FIRST_CH = 1536
TIME_BLOCKS = 2
ROWS_DEV = 512
CORES = 2
PIECES = 4
TABLE_STEP = 1024
BLOCK_ROWS = 64


def dft_rows(fft_len, first_channel, channel_count):
    sample_ids = np.arange(fft_len, dtype=np.int64)
    channel_ids = first_channel + np.arange(channel_count, dtype=np.int64)
    phase = channel_ids[:, None] * sample_ids[None, :] % fft_len
    angle = phase.astype(np.float64) * (2.0 * math.pi / fft_len)
    return np.concatenate([np.cos(angle), -np.sin(angle)], axis=0).astype(np.float32)


def spectra_kernel(
    owners, x_hbm, taps_hbm, dft_hbm, out_ref,
    taps_ref, dft_ref, x_buf, table, raw, window, parts, small_sems, sems,
):
    tap_count, fft_len = taps_ref.shape
    columns = dft_ref.shape[0]
    channels = columns // 2
    frame_count = x_hbm.shape[2] // fft_len
    piece = fft_len // PIECES
    edge = tap_count - 1
    width = tap_count * columns
    later_block = lax.axis_index("feed") >= channels * owners // TIME_BLOCKS

    small = [
        pltpu.make_async_copy(taps_hbm, taps_ref, small_sems.at[0]),
        pltpu.make_async_copy(dft_hbm, dft_ref, small_sems.at[1]),
    ]
    for copy in small:
        copy.start()

    def fetch(index):
        span = pl.ds(pl.multiple_of(index * piece, piece), piece)
        return pltpu.make_async_copy(x_hbm.at[0, :, span], x_buf.at[:, span], sems.at[index])

    @pl.loop(0, frame_count * PIECES // 2)
    def _(pair):
        fetch(2 * pair).start(priority=0)
        fetch(2 * pair + 1).start(priority=1)

    window[...] = jnp.zeros_like(window)
    raw[...] = jnp.zeros_like(raw)
    for copy in small:
        copy.wait()

    @pl.loop(0, fft_len // TABLE_STEP)
    def _(index):
        span = pl.ds(pl.multiple_of(index * TABLE_STEP, TABLE_STEP), TABLE_STEP)
        dft = dft_ref[:, span]
        scaled = jnp.concatenate([taps_ref[m : m + 1, span] * dft for m in range(tap_count)], axis=0)
        high = scaled.astype(jnp.bfloat16).astype(jnp.float32)
        both = jnp.concatenate([high, scaled - high], axis=0)
        table[span, :] = both.T.astype(jnp.bfloat16)

    def fold(frame, total):
        turned = total.T
        summed = turned[:width] + turned[width:]
        for m in range(tap_count):
            window[frame + edge - m] += summed[m * columns : (m + 1) * columns]

    def two_dots(frame, begin, depth):
        total = None
        for offset in (begin, begin + depth):
            start = pl.multiple_of(frame * fft_len + offset, depth)
            product = jnp.dot(
                x_buf[:, pl.ds(start, depth)],
                table[offset : offset + depth, :],
                preferred_element_type=jnp.float32,
            )
            total = product if total is None else total + product
        return total

    @pl.loop(0, frame_count - 1)
    def _(frame):
        for p in range(PIECES):
            fetch(frame * PIECES + p).wait()
        fold(jnp.maximum(frame - 1, 0), raw[...])
        raw[...] = two_dots(frame, 0, fft_len // 2)

    last = frame_count - 1
    total = None
    for p in range(0, PIECES, 2):
        for k in (p, p + 1):
            fetch(last * PIECES + k).wait()
        if p == 0:
            fold(last - 1, raw[...])
        product = two_dots(last, p * piece, piece)
        total = product if total is None else total + product
    fold(last, total)

    for spot in range(frame_count + edge):
        parts[:, spot, :] = window[spot]

    copies = out_ref.shape[0] // channels
    for c in range(channels):
        now = jnp.concatenate([parts[c, :frame_count], parts[channels + c, :frame_count]], axis=0)
        high = now.astype(jnp.bfloat16)
        low = now - high.astype(jnp.float32)
        low = jnp.concatenate([low[:4], low[frame_count : frame_count + 4]], axis=0)
        tail = jnp.concatenate(
            [parts[c, frame_count : frame_count + 4], parts[channels + c, frame_count : frame_count + 4]],
            axis=0,
        )
        sublane = lax.broadcasted_iota(jnp.int32, tail.shape, 0)
        tail = jnp.where(sublane % 4 < edge, tail, 0.0)
        tail_high = tail.astype(jnp.bfloat16).astype(jnp.float32)
        tail_low = tail - tail_high
        extra = jnp.concatenate(
            [jnp.where(later_block, low, tail_high), jnp.where(later_block, 0.0, tail_low)], axis=0
        ).astype(jnp.bfloat16)
        whole = jnp.concatenate([high, extra], axis=0)
        for o in range(copies):
            out_ref[c * copies + o] = whole


def correlate_kernel(
    scale, owners, own_ref, other_ref, out_hbm, right, left, out_buf, sems
):
    lines, rows, feed_count = own_ref.shape
    group_span = lines * CORES // TIME_BLOCKS
    frame_count = rows // 4
    total_feeds = right.shape[1]
    blocks = left.shape[0]
    block_rows = left.shape[1] // 2
    my_index = lax.axis_index("feed")
    my_core = my_index % CORES

    def arrived(device):
        mine, core = device // CORES, device % CORES
        return jnp.where(my_core == core, own_ref[mine], other_ref[mine])

    for g in range(group_span):
        span = slice(g * feed_count, (g + 1) * feed_count)
        low, high = arrived(g), arrived(group_span + g)
        first = low.astype(jnp.float32)
        second = high.astype(jnp.float32)
        extra = (
            first[2 * frame_count : 3 * frame_count]
            + first[3 * frame_count :]
            + second[2 * frame_count : 3 * frame_count]
        )
        zero = jnp.zeros((frame_count - 4, feed_count), jnp.float32)
        extra = jnp.concatenate([extra[:4], zero, extra[4:8], zero], axis=0)
        fixed = second[: 2 * frame_count] + extra
        right[: 2 * frame_count, span] = low[: 2 * frame_count]
        right[2 * frame_count :, span] = fixed.astype(jnp.bfloat16)
    row_start = my_index % owners * ROWS_DEV
    mine = right[:, pl.ds(pl.multiple_of(row_start, ROWS_DEV), ROWS_DEV)].astype(jnp.float32)
    halves = [mine[k * frame_count : (k + 1) * frame_count] for k in range(4)]
    swapped = jnp.concatenate([halves[1], -halves[0], halves[3], -halves[2]], axis=0)
    left[:, :block_rows, :] = mine.T.astype(jnp.bfloat16).reshape(blocks, block_rows, rows)
    left[:, block_rows:, :] = swapped.T.astype(jnp.bfloat16).reshape(blocks, block_rows, rows)

    def store(block):
        span = pl.ds(pl.multiple_of(block * block_rows, block_rows), block_rows)
        return pltpu.make_async_copy(out_buf.at[span], out_hbm.at[span], sems.at[block])

    @pl.loop(0, blocks // 2)
    def _(pair):
        for turn in range(2):
            block = 2 * pair + turn
            product = jnp.dot(left[block], right[...], preferred_element_type=jnp.float32) * scale
            span = pl.ds(pl.multiple_of(block * block_rows, block_rows), block_rows)
            out_buf[span, :total_feeds] = product[:block_rows]
            out_buf[span, total_feeds:] = product[block_rows:]
            store(block).start(priority=turn)

    @pl.loop(0, blocks)
    def _(block):
        store(block).wait()


def body(samples, pfb_taps):
    feed_count = samples.shape[1]
    tap_count, fft_len = pfb_taps.shape
    frame_count = samples.shape[2] // fft_len
    devices = lax.axis_size("feed")
    total_feeds = feed_count * devices // TIME_BLOCKS
    channels = devices * ROWS_DEV // total_feeds
    owners = total_feeds // ROWS_DEV
    spectra_count = TIME_BLOCKS * frame_count
    columns = 2 * channels
    rows = 4 * frame_count
    lines = devices // CORES
    dft = jnp.asarray(dft_rows(fft_len, FIRST_CH, channels))
    in_vmem = pl.BlockSpec(memory_space=pltpu.VMEM)
    outgoing = pl.pallas_call(
        functools.partial(spectra_kernel, owners),
        out_shape=jax.ShapeDtypeStruct((lines, rows, feed_count), jnp.bfloat16),
        in_specs=[pl.BlockSpec(memory_space=pl.ANY)] * 3,
        out_specs=in_vmem,
        scratch_shapes=[
            pltpu.VMEM(pfb_taps.shape, jnp.float32),
            pltpu.VMEM(dft.shape, jnp.float32),
            pltpu.VMEM((feed_count, samples.shape[2]), jnp.bfloat16),
            pltpu.VMEM((fft_len, 2 * tap_count * columns), jnp.bfloat16),
            pltpu.VMEM((feed_count, 2 * tap_count * columns), jnp.float32),
            pltpu.VMEM((frame_count + tap_count - 1, columns, feed_count), jnp.float32),
            pltpu.VMEM((columns, 2 * frame_count, feed_count), jnp.float32),
            pltpu.SemaphoreType.DMA((2,)),
            pltpu.SemaphoreType.DMA((frame_count * PIECES,)),
        ],
        compiler_params=pltpu.CompilerParams(vmem_limit_bytes=56 * 2**20),
        name="spectra",
    )(samples, pfb_taps, dft)
    same_core = [[line * CORES + core for line in range(lines)] for core in range(CORES)]
    own = lax.all_to_all(outgoing, "feed", 0, 0, axis_index_groups=same_core, tiled=True)
    other = lax.ppermute(own, "feed", [(d, d ^ 1) for d in range(devices)])
    blocks = ROWS_DEV // BLOCK_ROWS
    return pl.pallas_call(
        functools.partial(correlate_kernel, 1.0 / spectra_count, owners),
        out_shape=jax.ShapeDtypeStruct((ROWS_DEV, 2 * total_feeds), jnp.float32),
        in_specs=[in_vmem, in_vmem],
        out_specs=pl.BlockSpec(memory_space=pl.ANY),
        scratch_shapes=[
            pltpu.VMEM((rows, total_feeds), jnp.bfloat16),
            pltpu.VMEM((blocks, 2 * BLOCK_ROWS, rows), jnp.bfloat16),
            pltpu.VMEM((ROWS_DEV, 2 * total_feeds), jnp.float32),
            pltpu.SemaphoreType.DMA((blocks,)),
        ],
        compiler_params=pltpu.CompilerParams(vmem_limit_bytes=32 * 2**20),
        name="correlate",
    )(own, other)


def solution(mesh):
    placed = (P(("grp", "feed"), None, None), P())
    return jax.shard_map(
        body, mesh=mesh, in_specs=placed, out_specs=P(("grp", "feed"), None), check_vma=False
    )
```

```python
import functools
import math

import jax
import jax.numpy as jnp
import numpy as np
from jax import lax
from jax.experimental import pallas as pl
from jax.experimental.pallas import tpu as pltpu
from jax.sharding import PartitionSpec as P

FIRST_CH = 1536
TIME_BLOCKS = 2
ROWS_DEV = 512
CORES = 2
PIECES = 4
TABLE_STEP = 1024
BLOCK_ROWS = 64


def dft_rows(fft_len, first_channel, channel_count):
    sample_ids = np.arange(fft_len, dtype=np.int64)
    channel_ids = first_channel + np.arange(channel_count, dtype=np.int64)
    phase = channel_ids[:, None] * sample_ids[None, :] % fft_len
    angle = phase.astype(np.float64) * (2.0 * math.pi / fft_len)
    return np.concatenate([np.cos(angle), -np.sin(angle)], axis=0).astype(np.float32)


def spectra_kernel(
    owners, x_hbm, taps_hbm, dft_hbm, out_ref,
    taps_ref, dft_ref, x_buf, table, raw, window, parts, small_sems, sems,
):
    tap_count, fft_len = taps_ref.shape
    columns = dft_ref.shape[0]
    channels = columns // 2
    frame_count = x_hbm.shape[2] // fft_len
    piece = fft_len // PIECES
    edge = tap_count - 1
    width = tap_count * columns
    later_block = lax.axis_index("feed") >= channels * owners // TIME_BLOCKS

    small = [
        pltpu.make_async_copy(taps_hbm, taps_ref, small_sems.at[0]),
        pltpu.make_async_copy(dft_hbm, dft_ref, small_sems.at[1]),
    ]
    for copy in small:
        copy.start()

    def fetch(index):
        span = pl.ds(pl.multiple_of(index * piece, piece), piece)
        return pltpu.make_async_copy(x_hbm.at[0, :, span], x_buf.at[:, span], sems.at[index])

    @pl.loop(0, frame_count * PIECES)
    def _(index):
        fetch(index).start()

    window[...] = jnp.zeros_like(window)
    raw[...] = jnp.zeros_like(raw)
    for copy in small:
        copy.wait()

    @pl.loop(0, fft_len // TABLE_STEP)
    def _(index):
        span = pl.ds(pl.multiple_of(index * TABLE_STEP, TABLE_STEP), TABLE_STEP)
        dft = dft_ref[:, span]
        scaled = jnp.concatenate([taps_ref[m : m + 1, span] * dft for m in range(tap_count)], axis=0)
        high = scaled.astype(jnp.bfloat16).astype(jnp.float32)
        both = jnp.concatenate([high, scaled - high], axis=0)
        table[span, :] = both.T.astype(jnp.bfloat16)

    def fold(frame, total):
        turned = total.T
        summed = turned[:width] + turned[width:]
        for m in range(tap_count):
            window[frame + edge - m] += summed[m * columns : (m + 1) * columns]

    def two_dots(frame, begin, depth):
        total = None
        for offset in (begin, begin + depth):
            start = pl.multiple_of(frame * fft_len + offset, depth)
            product = jnp.dot(
                x_buf[:, pl.ds(start, depth)],
                table[offset : offset + depth, :],
                preferred_element_type=jnp.float32,
            )
            total = product if total is None else total + product
        return total

    @pl.loop(0, frame_count - 1)
    def _(frame):
        for p in range(PIECES):
            fetch(frame * PIECES + p).wait()
        fold(jnp.maximum(frame - 1, 0), raw[...])
        raw[...] = two_dots(frame, 0, fft_len // 2)

    last = frame_count - 1
    total = None
    for p in range(0, PIECES, 2):
        for k in (p, p + 1):
            fetch(last * PIECES + k).wait()
        if p == 0:
            fold(last - 1, raw[...])
        product = two_dots(last, p * piece, piece)
        total = product if total is None else total + product
    fold(last, total)

    for spot in range(frame_count + edge):
        parts[:, spot, :] = window[spot]

    copies = out_ref.shape[0] // channels
    for c in range(channels):
        now = jnp.concatenate([parts[c, :frame_count], parts[channels + c, :frame_count]], axis=0)
        high = now.astype(jnp.bfloat16)
        low = now - high.astype(jnp.float32)
        low = jnp.concatenate([low[:4], low[frame_count : frame_count + 4]], axis=0)
        tail = jnp.concatenate(
            [parts[c, frame_count : frame_count + 4], parts[channels + c, frame_count : frame_count + 4]],
            axis=0,
        )
        sublane = lax.broadcasted_iota(jnp.int32, tail.shape, 0)
        tail = jnp.where(sublane % 4 < edge, tail, 0.0)
        extra = jnp.where(later_block, low, tail).astype(jnp.bfloat16)
        whole = jnp.concatenate([high, extra], axis=0)
        for o in range(copies):
            out_ref[c * copies + o] = whole


def correlate_kernel(
    scale, owners, own_ref, other_ref, out_hbm, right, left, out_buf, sems
):
    lines, rows, feed_count = own_ref.shape
    group_span = lines * CORES // TIME_BLOCKS
    frame_count = rows // 3
    total_feeds = right.shape[1]
    blocks = left.shape[0]
    block_rows = left.shape[1] // 2
    my_index = lax.axis_index("feed")
    my_core = my_index % CORES

    def arrived(device):
        mine, core = device // CORES, device % CORES
        return jnp.where(my_core == core, own_ref[mine], other_ref[mine])

    for g in range(group_span):
        span = slice(g * feed_count, (g + 1) * feed_count)
        low, high = arrived(g), arrived(group_span + g)
        first = low.astype(jnp.float32)
        second = high.astype(jnp.float32)
        extra = first[2 * frame_count :] + second[2 * frame_count :]
        zero = jnp.zeros((frame_count - 4, feed_count), jnp.float32)
        extra = jnp.concatenate([extra[:4], zero, extra[4:8], zero], axis=0)
        fixed = second[: 2 * frame_count] + extra
        right[: 2 * frame_count, span] = low[: 2 * frame_count]
        right[2 * frame_count :, span] = fixed.astype(jnp.bfloat16)
    row_start = my_index % owners * ROWS_DEV
    mine = right[:, pl.ds(pl.multiple_of(row_start, ROWS_DEV), ROWS_DEV)].astype(jnp.float32)
    halves = [mine[k * frame_count : (k + 1) * frame_count] for k in range(4)]
    swapped = jnp.concatenate([halves[1], -halves[0], halves[3], -halves[2]], axis=0)
    left[:, :block_rows, :] = mine.T.astype(jnp.bfloat16).reshape(blocks, block_rows, 4 * frame_count)
    left[:, block_rows:, :] = swapped.T.astype(jnp.bfloat16).reshape(blocks, block_rows, 4 * frame_count)

    def store(block):
        span = pl.ds(pl.multiple_of(block * block_rows, block_rows), block_rows)
        return pltpu.make_async_copy(out_buf.at[span], out_hbm.at[span], sems.at[block])

    @pl.loop(0, blocks)
    def _(block):
        product = jnp.dot(left[block], right[...], preferred_element_type=jnp.float32) * scale
        span = pl.ds(pl.multiple_of(block * block_rows, block_rows), block_rows)
        out_buf[span, :total_feeds] = product[:block_rows]
        out_buf[span, total_feeds:] = product[block_rows:]
        store(block).start()

    @pl.loop(0, blocks)
    def _(block):
        store(block).wait()


def body(samples, pfb_taps):
    feed_count = samples.shape[1]
    tap_count, fft_len = pfb_taps.shape
    frame_count = samples.shape[2] // fft_len
    devices = lax.axis_size("feed")
    total_feeds = feed_count * devices // TIME_BLOCKS
    channels = devices * ROWS_DEV // total_feeds
    owners = total_feeds // ROWS_DEV
    spectra_count = TIME_BLOCKS * frame_count
    columns = 2 * channels
    rows = 3 * frame_count
    lines = devices // CORES
    dft = jnp.asarray(dft_rows(fft_len, FIRST_CH, channels))
    in_vmem = pl.BlockSpec(memory_space=pltpu.VMEM)
    outgoing = pl.pallas_call(
        functools.partial(spectra_kernel, owners),
        out_shape=jax.ShapeDtypeStruct((lines, rows, feed_count), jnp.bfloat16),
        in_specs=[pl.BlockSpec(memory_space=pltpu.HBM)] * 3,
        out_specs=in_vmem,
        scratch_shapes=[
            pltpu.VMEM(pfb_taps.shape, jnp.float32),
            pltpu.VMEM(dft.shape, jnp.float32),
            pltpu.VMEM((feed_count, samples.shape[2]), jnp.bfloat16),
            pltpu.VMEM((fft_len, 2 * tap_count * columns), jnp.bfloat16),
            pltpu.VMEM((feed_count, 2 * tap_count * columns), jnp.float32),
            pltpu.VMEM((frame_count + tap_count - 1, columns, feed_count), jnp.float32),
            pltpu.VMEM((columns, 2 * frame_count, feed_count), jnp.float32),
            pltpu.SemaphoreType.DMA((2,)),
            pltpu.SemaphoreType.DMA((frame_count * PIECES,)),
        ],
        compiler_params=pltpu.CompilerParams(vmem_limit_bytes=44 * 2**20),
        name="spectra",
    )(*[pltpu.with_memory_space_constraint(v, pltpu.HBM) for v in (samples, pfb_taps, dft)])
    same_core = [[line * CORES + core for line in range(lines)] for core in range(CORES)]
    own = lax.all_to_all(outgoing, "feed", 0, 0, axis_index_groups=same_core, tiled=True)
    other = lax.ppermute(own, "feed", [(d, d ^ 1) for d in range(devices)])
    blocks = ROWS_DEV // BLOCK_ROWS
    return pl.pallas_call(
        functools.partial(correlate_kernel, 1.0 / spectra_count, owners),
        out_shape=jax.ShapeDtypeStruct((ROWS_DEV, 2 * total_feeds), jnp.float32),
        in_specs=[in_vmem, in_vmem],
        out_specs=pl.BlockSpec(memory_space=pl.ANY),
        scratch_shapes=[
            pltpu.VMEM((2 * spectra_count, total_feeds), jnp.bfloat16),
            pltpu.VMEM((blocks, 2 * BLOCK_ROWS, 2 * spectra_count), jnp.bfloat16),
            pltpu.VMEM((ROWS_DEV, 2 * total_feeds), jnp.float32),
            pltpu.SemaphoreType.DMA((blocks,)),
        ],
        compiler_params=pltpu.CompilerParams(vmem_limit_bytes=32 * 2**20),
        name="correlate",
    )(own, other)


def solution(mesh):
    placed = (P(("grp", "feed"), None, None), P())
    return jax.shard_map(
        body, mesh=mesh, in_specs=placed, out_specs=P(("grp", "feed"), None), check_vma=False
    )
```

```python
import functools
import math

import jax
import jax.numpy as jnp
import numpy as np
from jax import lax
from jax.experimental import pallas as pl
from jax.experimental.pallas import tpu as pltpu
from jax.sharding import PartitionSpec as P

FIRST_CH = 1536
TIME_BLOCKS = 2
ROWS_DEV = 512
CORES = 2
PIECES = 8
TABLE_STEP = 1024
BLOCK_ROWS = 64


def dft_rows(fft_len, first_channel, channel_count):
    sample_ids = np.arange(fft_len, dtype=np.int64)
    channel_ids = first_channel + np.arange(channel_count, dtype=np.int64)
    phase = channel_ids[:, None] * sample_ids[None, :] % fft_len
    angle = phase.astype(np.float64) * (2.0 * math.pi / fft_len)
    return np.concatenate([np.cos(angle), -np.sin(angle)], axis=0).astype(np.float32)


def spectra_kernel(
    owners, x_hbm, taps_hbm, dft_hbm, out_ref,
    taps_ref, dft_ref, x_buf, table, raw, window, parts, small_sems, sems,
):
    tap_count, fft_len = taps_ref.shape
    columns = dft_ref.shape[0]
    channels = columns // 2
    frame_count = x_hbm.shape[2] // fft_len
    piece = fft_len // PIECES
    edge = tap_count - 1
    width = tap_count * columns
    later_block = lax.axis_index("feed") >= channels * owners // TIME_BLOCKS

    small = [
        pltpu.make_async_copy(taps_hbm, taps_ref, small_sems.at[0]),
        pltpu.make_async_copy(dft_hbm, dft_ref, small_sems.at[1]),
    ]
    for copy in small:
        copy.start()

    def fetch(index):
        span = pl.ds(pl.multiple_of(index * piece, piece), piece)
        return pltpu.make_async_copy(x_hbm.at[0, :, span], x_buf.at[:, span], sems.at[index])

    @pl.loop(0, frame_count * PIECES)
    def _(index):
        fetch(index).start()

    window[...] = jnp.zeros_like(window)
    raw[...] = jnp.zeros_like(raw)
    for copy in small:
        copy.wait()

    @pl.loop(0, fft_len // TABLE_STEP)
    def _(index):
        span = pl.ds(pl.multiple_of(index * TABLE_STEP, TABLE_STEP), TABLE_STEP)
        dft = dft_ref[:, span]
        scaled = jnp.concatenate([taps_ref[m : m + 1, span] * dft for m in range(tap_count)], axis=0)
        high = scaled.astype(jnp.bfloat16).astype(jnp.float32)
        both = jnp.concatenate([high, scaled - high], axis=0)
        table[span, :] = both.T.astype(jnp.bfloat16)

    def fold(frame, total):
        turned = total.T
        summed = turned[:width] + turned[width:]
        for m in range(tap_count):
            window[frame + edge - m] += summed[m * columns : (m + 1) * columns]

    def two_dots(frame, begin, depth):
        total = None
        for offset in (begin, begin + depth):
            start = pl.multiple_of(frame * fft_len + offset, depth)
            product = jnp.dot(
                x_buf[:, pl.ds(start, depth)],
                table[offset : offset + depth, :],
                preferred_element_type=jnp.float32,
            )
            total = product if total is None else total + product
        return total

    @pl.loop(0, frame_count - 1)
    def _(frame):
        for p in range(PIECES):
            fetch(frame * PIECES + p).wait()
        fold(jnp.maximum(frame - 1, 0), raw[...])
        raw[...] = two_dots(frame, 0, fft_len // 2)

    last = frame_count - 1
    fold(last - 1, raw[...])
    for spot in range(last):
        parts[:, spot, :] = window[spot]
    total = None
    for begin, end in ((0, PIECES // 2), (PIECES // 2, 3 * PIECES // 4), (3 * PIECES // 4, PIECES)):
        for p in range(begin, end):
            fetch(last * PIECES + p).wait()
        product = two_dots(last, begin * piece, (end - begin) * piece // 2)
        total = product if total is None else total + product
    fold(last, total)
    for spot in range(last, frame_count + edge):
        parts[:, spot, :] = window[spot]

    copies = out_ref.shape[0] // channels
    for c in range(channels):
        now = jnp.concatenate([parts[c, :frame_count], parts[channels + c, :frame_count]], axis=0)
        high = now.astype(jnp.bfloat16)
        low = now - high.astype(jnp.float32)
        low = jnp.concatenate([low[:4], low[frame_count : frame_count + 4]], axis=0)
        tail = jnp.concatenate(
            [parts[c, frame_count : frame_count + 4], parts[channels + c, frame_count : frame_count + 4]],
            axis=0,
        )
        sublane = lax.broadcasted_iota(jnp.int32, tail.shape, 0)
        tail = jnp.where(sublane % 4 < edge, tail, 0.0)
        extra = jnp.where(later_block, low, tail).astype(jnp.bfloat16)
        whole = jnp.concatenate([high, extra], axis=0)
        for o in range(copies):
            out_ref[c * copies + o] = whole


def correlate_kernel(
    scale, owners, own_ref, other_ref, out_hbm, right, left, out_buf, sems
):
    lines, rows, feed_count = own_ref.shape
    frame_count = rows // 3
    total_feeds = right.shape[1]
    blocks = left.shape[0]
    block_rows = left.shape[1] // 2
    my_index = lax.axis_index("feed")
    my_core = my_index % CORES

    def join(group, low, high):
        span = pl.ds(group * feed_count, feed_count)
        if not isinstance(group, int):
            span = pl.ds(pl.multiple_of(group * feed_count, feed_count), feed_count)
        extra = low[2 * frame_count :].astype(jnp.float32) + high[2 * frame_count :].astype(jnp.float32)
        zero = jnp.zeros((frame_count - 4, feed_count), jnp.float32)
        extra = jnp.concatenate([extra[:4], zero, extra[4:8], zero], axis=0)
        fixed = high[: 2 * frame_count].astype(jnp.float32) + extra
        right[: 2 * frame_count, span] = low[: 2 * frame_count]
        right[2 * frame_count :, span] = fixed.astype(jnp.bfloat16)

    later = lines // TIME_BLOCKS
    for line in range(later):
        if feed_count % 128 == 0:
            for ref, core in ((own_ref, my_core), (other_ref, CORES - 1 - my_core)):
                join(line * CORES + core, ref[line], ref[later + line])
        else:
            for core in range(CORES):
                low, high = [
                    jnp.where(my_core == core, own_ref[k], other_ref[k]) for k in (line, later + line)
                ]
                join(line * CORES + core, low, high)
    row_start = my_index % owners * ROWS_DEV
    mine = right[:, pl.ds(pl.multiple_of(row_start, ROWS_DEV), ROWS_DEV)].astype(jnp.float32)
    halves = [mine[k * frame_count : (k + 1) * frame_count] for k in range(4)]
    swapped = jnp.concatenate([halves[1], -halves[0], halves[3], -halves[2]], axis=0)
    left[:, :block_rows, :] = mine.T.astype(jnp.bfloat16).reshape(blocks, block_rows, 4 * frame_count)
    left[:, block_rows:, :] = swapped.T.astype(jnp.bfloat16).reshape(blocks, block_rows, 4 * frame_count)

    def store(block):
        span = pl.ds(pl.multiple_of(block * block_rows, block_rows), block_rows)
        return pltpu.make_async_copy(out_buf.at[span], out_hbm.at[span], sems.at[block])

    @pl.loop(0, blocks)
    def _(block):
        product = jnp.dot(left[block], right[...], preferred_element_type=jnp.float32) * scale
        span = pl.ds(pl.multiple_of(block * block_rows, block_rows), block_rows)
        out_buf[span, :total_feeds] = product[:block_rows]
        out_buf[span, total_feeds:] = product[block_rows:]
        store(block).start()

    @pl.loop(0, blocks)
    def _(block):
        store(block).wait()


def body(samples, pfb_taps):
    feed_count = samples.shape[1]
    tap_count, fft_len = pfb_taps.shape
    frame_count = samples.shape[2] // fft_len
    devices = lax.axis_size("feed")
    total_feeds = feed_count * devices // TIME_BLOCKS
    channels = devices * ROWS_DEV // total_feeds
    owners = total_feeds // ROWS_DEV
    spectra_count = TIME_BLOCKS * frame_count
    columns = 2 * channels
    rows = 3 * frame_count
    lines = devices // CORES
    dft = jnp.asarray(dft_rows(fft_len, FIRST_CH, channels))
    in_vmem = pl.BlockSpec(memory_space=pltpu.VMEM)
    outgoing = pl.pallas_call(
        functools.partial(spectra_kernel, owners),
        out_shape=jax.ShapeDtypeStruct((lines, rows, feed_count), jnp.bfloat16),
        in_specs=[pl.BlockSpec(memory_space=pltpu.HBM)] * 3,
        out_specs=in_vmem,
        scratch_shapes=[
            pltpu.VMEM(pfb_taps.shape, jnp.float32),
            pltpu.VMEM(dft.shape, jnp.float32),
            pltpu.VMEM((feed_count, samples.shape[2]), jnp.bfloat16),
            pltpu.VMEM((fft_len, 2 * tap_count * columns), jnp.bfloat16),
            pltpu.VMEM((feed_count, 2 * tap_count * columns), jnp.float32),
            pltpu.VMEM((frame_count + tap_count - 1, columns, feed_count), jnp.float32),
            pltpu.VMEM((columns, 2 * frame_count, feed_count), jnp.float32),
            pltpu.SemaphoreType.DMA((2,)),
            pltpu.SemaphoreType.DMA((frame_count * PIECES,)),
        ],
        compiler_params=pltpu.CompilerParams(vmem_limit_bytes=44 * 2**20),
        name="spectra",
    )(*[pltpu.with_memory_space_constraint(v, pltpu.HBM) for v in (samples, pfb_taps, dft)])
    same_core = [[line * CORES + core for line in range(lines)] for core in range(CORES)]
    own = lax.all_to_all(outgoing, "feed", 0, 0, axis_index_groups=same_core, tiled=True)
    other = lax.ppermute(own, "feed", [(d, d ^ 1) for d in range(devices)])
    blocks = ROWS_DEV // BLOCK_ROWS
    return pl.pallas_call(
        functools.partial(correlate_kernel, 1.0 / spectra_count, owners),
        out_shape=jax.ShapeDtypeStruct((ROWS_DEV, 2 * total_feeds), jnp.float32),
        in_specs=[in_vmem, in_vmem],
        out_specs=pl.BlockSpec(memory_space=pl.ANY),
        scratch_shapes=[
            pltpu.VMEM((2 * spectra_count, total_feeds), jnp.bfloat16),
            pltpu.VMEM((blocks, 2 * BLOCK_ROWS, 2 * spectra_count), jnp.bfloat16),
            pltpu.VMEM((ROWS_DEV, 2 * total_feeds), jnp.float32),
            pltpu.SemaphoreType.DMA((blocks,)),
        ],
        compiler_params=pltpu.CompilerParams(vmem_limit_bytes=32 * 2**20),
        name="correlate",
    )(own, other)


def solution(mesh):
    placed = (P(("grp", "feed"), None, None), P())
    return jax.shard_map(
        body, mesh=mesh, in_specs=placed, out_specs=P(("grp", "feed"), None), check_vma=False
    )
```

```python
import functools
import math

import jax
import jax.numpy as jnp
import numpy as np
from jax import lax
from jax.experimental import pallas as pl
from jax.experimental.pallas import tpu as pltpu
from jax.sharding import PartitionSpec as P

FIRST_CH = 1536
TIME_BLOCKS = 2
ROWS_DEV = 512
CORES = 2
PIECES = 4
TABLE_STEP = 1024
BLOCK_ROWS = 64


def dft_rows(fft_len, first_channel, channel_count):
    sample_ids = np.arange(fft_len, dtype=np.int64)
    channel_ids = first_channel + np.arange(channel_count, dtype=np.int64)
    phase = channel_ids[:, None] * sample_ids[None, :] % fft_len
    angle = phase.astype(np.float64) * (2.0 * math.pi / fft_len)
    return np.concatenate([np.cos(angle), -np.sin(angle)], axis=0).astype(np.float32)


def spectra_kernel(
    owners, x_hbm, taps_hbm, dft_hbm, out_ref,
    taps_ref, dft_ref, x_buf, table, raw, window, parts, small_sems, sems,
):
    tap_count, fft_len = taps_ref.shape
    columns = dft_ref.shape[0]
    channels = columns // 2
    frame_count = x_hbm.shape[2] // fft_len
    piece = fft_len // PIECES
    edge = tap_count - 1
    width = tap_count * columns
    later_block = lax.axis_index("feed") >= channels * owners // TIME_BLOCKS

    small = [
        pltpu.make_async_copy(taps_hbm, taps_ref, small_sems.at[0]),
        pltpu.make_async_copy(dft_hbm, dft_ref, small_sems.at[1]),
    ]
    for copy in small:
        copy.start()

    def fetch(index):
        span = pl.ds(pl.multiple_of(index * piece, piece), piece)
        return pltpu.make_async_copy(x_hbm.at[0, :, span], x_buf.at[:, span], sems.at[index])

    @pl.loop(0, frame_count * PIECES)
    def _(index):
        fetch(index).start()

    window[...] = jnp.zeros_like(window)
    for copy in small:
        copy.wait()

    def build(start):
        span = slice(start, start + TABLE_STEP)
        dft = dft_ref[:, span]
        scaled = jnp.concatenate([taps_ref[m : m + 1, span] * dft for m in range(tap_count)], axis=0)
        high = scaled.astype(jnp.bfloat16)
        low = (scaled - high.astype(jnp.float32)).astype(jnp.bfloat16)
        table[span, :] = jnp.concatenate([high, low], axis=0).T

    def fold(frame, total):
        turned = total.T
        summed = turned[:width] + turned[width:]
        for m in range(tap_count):
            window[frame + edge - m] += summed[m * columns : (m + 1) * columns]

    def two_dots(frame, begin, depth):
        total = None
        for offset in (begin, begin + depth):
            start = pl.multiple_of(frame * fft_len + offset, depth)
            product = jnp.dot(
                x_buf[:, pl.ds(start, depth)],
                table[offset : offset + depth, :],
                preferred_element_type=jnp.float32,
            )
            total = product if total is None else total + product
        return total

    build(0)
    for p in range(PIECES):
        fetch(p).wait()
    total = None
    for start in range(0, fft_len, TABLE_STEP):
        product = jnp.dot(
            x_buf[:, start : start + TABLE_STEP],
            table[start : start + TABLE_STEP, :],
            preferred_element_type=jnp.float32,
        )
        total = product if total is None else total + product
        if start + TABLE_STEP < fft_len:
            build(start + TABLE_STEP)
    raw[...] = total

    @pl.loop(1, frame_count - 1)
    def _(frame):
        for p in range(PIECES):
            fetch(frame * PIECES + p).wait()
        fold(frame - 1, raw[...])
        raw[...] = two_dots(frame, 0, fft_len // 2)

    last = frame_count - 1
    total = None
    for p in range(0, PIECES, 2):
        for k in (p, p + 1):
            fetch(last * PIECES + k).wait()
        if p == 0:
            fold(last - 1, raw[...])
        product = two_dots(last, p * piece, piece)
        total = product if total is None else total + product
    fold(last, total)

    for spot in range(frame_count + edge):
        parts[:, spot, :] = window[spot]

    copies = out_ref.shape[0] // channels
    for c in range(channels):
        now = jnp.concatenate([parts[c, :frame_count], parts[channels + c, :frame_count]], axis=0)
        high = now.astype(jnp.bfloat16)
        low = now - high.astype(jnp.float32)
        low = jnp.concatenate([low[:4], low[frame_count : frame_count + 4]], axis=0)
        tail = jnp.concatenate(
            [parts[c, frame_count : frame_count + 4], parts[channels + c, frame_count : frame_count + 4]],
            axis=0,
        )
        sublane = lax.broadcasted_iota(jnp.int32, tail.shape, 0)
        tail = jnp.where(sublane % 4 < edge, tail, 0.0)
        extra = jnp.where(later_block, low, tail).astype(jnp.bfloat16)
        whole = jnp.concatenate([high, extra], axis=0)
        for o in range(copies):
            out_ref[c * copies + o] = whole


def correlate_kernel(
    scale, owners, own_ref, other_ref, out_hbm, right, left, out_buf, sems
):
    lines, rows, feed_count = own_ref.shape
    frame_count = rows // 3
    total_feeds = right.shape[1]
    blocks = left.shape[0]
    block_rows = left.shape[1] // 2
    my_index = lax.axis_index("feed")
    my_core = my_index % CORES

    def join(group, low, high):
        span = pl.ds(group * feed_count, feed_count)
        if not isinstance(group, int):
            span = pl.ds(pl.multiple_of(group * feed_count, feed_count), feed_count)
        extra = low[2 * frame_count :].astype(jnp.float32) + high[2 * frame_count :].astype(jnp.float32)
        zero = jnp.zeros((frame_count - 4, feed_count), jnp.float32)
        extra = jnp.concatenate([extra[:4], zero, extra[4:8], zero], axis=0)
        fixed = high[: 2 * frame_count].astype(jnp.float32) + extra
        right[: 2 * frame_count, span] = low[: 2 * frame_count]
        right[2 * frame_count :, span] = fixed.astype(jnp.bfloat16)

    later = lines // TIME_BLOCKS
    for line in range(later):
        if feed_count % 128 == 0:
            for ref, core in ((own_ref, my_core), (other_ref, CORES - 1 - my_core)):
                join(line * CORES + core, ref[line], ref[later + line])
        else:
            for core in range(CORES):
                low, high = [
                    jnp.where(my_core == core, own_ref[k], other_ref[k]) for k in (line, later + line)
                ]
                join(line * CORES + core, low, high)
    row_start = my_index % owners * ROWS_DEV
    mine = right[:, pl.ds(pl.multiple_of(row_start, ROWS_DEV), ROWS_DEV)].astype(jnp.float32)
    halves = [mine[k * frame_count : (k + 1) * frame_count] for k in range(4)]
    swapped = jnp.concatenate([halves[1], -halves[0], halves[3], -halves[2]], axis=0)
    left[:, :block_rows, :] = mine.T.astype(jnp.bfloat16).reshape(blocks, block_rows, 4 * frame_count)
    left[:, block_rows:, :] = swapped.T.astype(jnp.bfloat16).reshape(blocks, block_rows, 4 * frame_count)

    def store(block):
        span = pl.ds(pl.multiple_of(block * block_rows, block_rows), block_rows)
        return pltpu.make_async_copy(out_buf.at[span], out_hbm.at[span], sems.at[block])

    @pl.loop(0, blocks)
    def _(block):
        product = jnp.dot(left[block], right[...], preferred_element_type=jnp.float32) * scale
        span = pl.ds(pl.multiple_of(block * block_rows, block_rows), block_rows)
        out_buf[span, :total_feeds] = product[:block_rows]
        out_buf[span, total_feeds:] = product[block_rows:]
        store(block).start()

    @pl.loop(0, blocks)
    def _(block):
        store(block).wait()


def body(samples, pfb_taps):
    feed_count = samples.shape[1]
    tap_count, fft_len = pfb_taps.shape
    frame_count = samples.shape[2] // fft_len
    devices = lax.axis_size("feed")
    total_feeds = feed_count * devices // TIME_BLOCKS
    channels = devices * ROWS_DEV // total_feeds
    owners = total_feeds // ROWS_DEV
    spectra_count = TIME_BLOCKS * frame_count
    columns = 2 * channels
    rows = 3 * frame_count
    lines = devices // CORES
    dft = jnp.asarray(dft_rows(fft_len, FIRST_CH, channels))
    in_vmem = pl.BlockSpec(memory_space=pltpu.VMEM)
    outgoing = pl.pallas_call(
        functools.partial(spectra_kernel, owners),
        out_shape=jax.ShapeDtypeStruct((lines, rows, feed_count), jnp.bfloat16),
        in_specs=[pl.BlockSpec(memory_space=pltpu.HBM)] * 3,
        out_specs=in_vmem,
        scratch_shapes=[
            pltpu.VMEM(pfb_taps.shape, jnp.float32),
            pltpu.VMEM(dft.shape, jnp.float32),
            pltpu.VMEM((feed_count, samples.shape[2]), jnp.bfloat16),
            pltpu.VMEM((fft_len, 2 * tap_count * columns), jnp.bfloat16),
            pltpu.VMEM((feed_count, 2 * tap_count * columns), jnp.float32),
            pltpu.VMEM((frame_count + tap_count - 1, columns, feed_count), jnp.float32),
            pltpu.VMEM((columns, 2 * frame_count, feed_count), jnp.float32),
            pltpu.SemaphoreType.DMA((2,)),
            pltpu.SemaphoreType.DMA((frame_count * PIECES,)),
        ],
        compiler_params=pltpu.CompilerParams(vmem_limit_bytes=44 * 2**20),
        name="spectra",
    )(*[pltpu.with_memory_space_constraint(v, pltpu.HBM) for v in (samples, pfb_taps, dft)])
    same_core = [[line * CORES + core for line in range(lines)] for core in range(CORES)]
    own = lax.all_to_all(outgoing, "feed", 0, 0, axis_index_groups=same_core, tiled=True)
    other = lax.ppermute(own, "feed", [(d, d ^ 1) for d in range(devices)])
    blocks = ROWS_DEV // BLOCK_ROWS
    return pl.pallas_call(
        functools.partial(correlate_kernel, 1.0 / spectra_count, owners),
        out_shape=jax.ShapeDtypeStruct((ROWS_DEV, 2 * total_feeds), jnp.float32),
        in_specs=[in_vmem, in_vmem],
        out_specs=pl.BlockSpec(memory_space=pl.ANY),
        scratch_shapes=[
            pltpu.VMEM((2 * spectra_count, total_feeds), jnp.bfloat16),
            pltpu.VMEM((blocks, 2 * BLOCK_ROWS, 2 * spectra_count), jnp.bfloat16),
            pltpu.VMEM((ROWS_DEV, 2 * total_feeds), jnp.float32),
            pltpu.SemaphoreType.DMA((blocks,)),
        ],
        compiler_params=pltpu.CompilerParams(vmem_limit_bytes=32 * 2**20),
        name="correlate",
    )(own, other)


def solution(mesh):
    placed = (P(("grp", "feed"), None, None), P())
    return jax.shard_map(
        body, mesh=mesh, in_specs=placed, out_specs=P(("grp", "feed"), None), check_vma=False
    )
```

```python
import functools
import math

import jax
import jax.numpy as jnp
import numpy as np
from jax import lax
from jax.experimental import pallas as pl
from jax.experimental.pallas import tpu as pltpu
from jax.sharding import PartitionSpec as P

FIRST_CH = 1536
TIME_BLOCKS = 2
ROWS_DEV = 512
CORES = 2
PIECES = 4
TABLE_STEP = 1024
COLUMNS = 256


def dft_rows(fft_len, first_channel, channel_count):
    sample_ids = np.arange(fft_len, dtype=np.int64)
    channel_ids = first_channel + np.arange(channel_count, dtype=np.int64)
    phase = channel_ids[:, None] * sample_ids[None, :] % fft_len
    angle = phase.astype(np.float64) * (2.0 * math.pi / fft_len)
    return np.concatenate([np.cos(angle), -np.sin(angle)], axis=0).astype(np.float32)


def spectra_kernel(
    owners, x_hbm, taps_hbm, dft_hbm, out_ref,
    taps_ref, dft_ref, x_buf, table, raw, window, parts, small_sems, sems,
):
    tap_count, fft_len = taps_ref.shape
    columns = dft_ref.shape[0]
    channels = columns // 2
    frame_count = x_hbm.shape[2] // fft_len
    piece = fft_len // PIECES
    edge = tap_count - 1
    width = tap_count * columns
    later_block = lax.axis_index("feed") >= channels * owners // TIME_BLOCKS

    small = [
        pltpu.make_async_copy(taps_hbm, taps_ref, small_sems.at[0]),
        pltpu.make_async_copy(dft_hbm, dft_ref, small_sems.at[1]),
    ]
    for copy in small:
        copy.start()

    def fetch(index):
        span = pl.ds(pl.multiple_of(index * piece, piece), piece)
        return pltpu.make_async_copy(x_hbm.at[0, :, span], x_buf.at[:, span], sems.at[index])

    @pl.loop(0, frame_count * PIECES)
    def _(index):
        fetch(index).start()

    window[...] = jnp.zeros_like(window)
    raw[...] = jnp.zeros_like(raw)
    for copy in small:
        copy.wait()

    @pl.loop(0, fft_len // TABLE_STEP)
    def _(index):
        span = pl.ds(pl.multiple_of(index * TABLE_STEP, TABLE_STEP), TABLE_STEP)
        dft = dft_ref[:, span]
        scaled = jnp.concatenate([taps_ref[m : m + 1, span] * dft for m in range(tap_count)], axis=0)
        high = scaled.astype(jnp.bfloat16).astype(jnp.float32)
        both = jnp.concatenate([high, scaled - high], axis=0)
        table[span, :] = both.T.astype(jnp.bfloat16)

    def fold(frame, total):
        turned = total.T
        summed = turned[:width] + turned[width:]
        for m in range(tap_count):
            window[frame + edge - m] += summed[m * columns : (m + 1) * columns]

    def two_dots(frame, begin, depth):
        total = None
        for offset in (begin, begin + depth):
            start = pl.multiple_of(frame * fft_len + offset, depth)
            product = jnp.dot(
                x_buf[:, pl.ds(start, depth)],
                table[offset : offset + depth, :],
                preferred_element_type=jnp.float32,
            )
            total = product if total is None else total + product
        return total

    @pl.loop(0, frame_count - 1)
    def _(frame):
        for p in range(PIECES):
            fetch(frame * PIECES + p).wait()
        fold(jnp.maximum(frame - 1, 0), raw[...])
        raw[...] = two_dots(frame, 0, fft_len // 2)

    last = frame_count - 1
    total = None
    for p in range(0, PIECES, 2):
        for k in (p, p + 1):
            fetch(last * PIECES + k).wait()
        if p == 0:
            fold(last - 1, raw[...])
        product = two_dots(last, p * piece, piece)
        total = product if total is None else total + product
    fold(last, total)

    for spot in range(frame_count + edge):
        parts[:, spot, :] = window[spot]

    copies = out_ref.shape[0] // channels
    for c in range(channels):
        now = jnp.concatenate([parts[c, :frame_count], parts[channels + c, :frame_count]], axis=0)
        high = now.astype(jnp.bfloat16)
        low = now - high.astype(jnp.float32)
        low = jnp.concatenate([low[:4], low[frame_count : frame_count + 4]], axis=0)
        tail = jnp.concatenate(
            [parts[c, frame_count : frame_count + 4], parts[channels + c, frame_count : frame_count + 4]],
            axis=0,
        )
        sublane = lax.broadcasted_iota(jnp.int32, tail.shape, 0)
        tail = jnp.where(sublane % 4 < edge, tail, 0.0)
        extra = jnp.where(later_block, low, tail).astype(jnp.bfloat16)
        whole = jnp.concatenate([high, extra], axis=0)
        for o in range(copies):
            out_ref[c * copies + o] = whole


def correlate_kernel(
    scale, owners, own_ref, other_ref, out_hbm, right, left, out_buf, sems
):
    lines, rows, feed_count = own_ref.shape
    frame_count = rows // 3
    total_feeds = right.shape[1]
    my_index = lax.axis_index("feed")
    my_core = my_index % CORES

    def join(group, low, high):
        place = pl.ds(group * feed_count, feed_count)
        if not isinstance(group, int):
            place = pl.ds(pl.multiple_of(group * feed_count, feed_count), feed_count)
        extra = low[2 * frame_count :].astype(jnp.float32) + high[2 * frame_count :].astype(jnp.float32)
        zero = jnp.zeros((frame_count - 4, feed_count), jnp.float32)
        extra = jnp.concatenate([extra[:4], zero, extra[4:8], zero], axis=0)
        fixed = high[: 2 * frame_count].astype(jnp.float32) + extra
        right[: 2 * frame_count, place] = low[: 2 * frame_count]
        right[2 * frame_count :, place] = fixed.astype(jnp.bfloat16)

    later = lines // TIME_BLOCKS
    for line in range(later):
        if feed_count % 128 == 0:
            for ref, core in ((own_ref, my_core), (other_ref, CORES - 1 - my_core)):
                join(line * CORES + core, ref[line], ref[later + line])
        else:
            for core in range(CORES):
                low, high = [
                    jnp.where(my_core == core, own_ref[k], other_ref[k]) for k in (line, later + line)
                ]
                join(line * CORES + core, low, high)
    row_start = my_index % owners * ROWS_DEV
    mine = right[:, pl.ds(pl.multiple_of(row_start, ROWS_DEV), ROWS_DEV)].astype(jnp.float32)
    halves = [mine[k * frame_count : (k + 1) * frame_count] for k in range(4)]
    swapped = jnp.concatenate([halves[1], -halves[0], halves[3], -halves[2]], axis=0)
    left[:ROWS_DEV] = mine.T.astype(jnp.bfloat16)
    left[ROWS_DEV:] = swapped.T.astype(jnp.bfloat16)

    def span(block, part):
        start = part * total_feeds + block * COLUMNS
        return pl.ds(pl.multiple_of(start, COLUMNS), COLUMNS)

    def store(block, part):
        cut = span(block, part)
        return pltpu.make_async_copy(out_buf.at[:, cut], out_hbm.at[:, cut], sems.at[block, part])

    @pl.loop(0, total_feeds // COLUMNS)
    def _(block):
        product = jnp.dot(left[...], right[:, span(block, 0)], preferred_element_type=jnp.float32)
        product = product * scale
        for part in range(2):
            out_buf[:, span(block, part)] = product[part * ROWS_DEV : (part + 1) * ROWS_DEV]
            store(block, part).start()

    @pl.loop(0, total_feeds // COLUMNS)
    def _(block):
        for part in range(2):
            store(block, part).wait()


def body(samples, pfb_taps):
    feed_count = samples.shape[1]
    tap_count, fft_len = pfb_taps.shape
    frame_count = samples.shape[2] // fft_len
    devices = lax.axis_size("feed")
    total_feeds = feed_count * devices // TIME_BLOCKS
    channels = devices * ROWS_DEV // total_feeds
    owners = total_feeds // ROWS_DEV
    spectra_count = TIME_BLOCKS * frame_count
    columns = 2 * channels
    rows = 3 * frame_count
    lines = devices // CORES
    dft = jnp.asarray(dft_rows(fft_len, FIRST_CH, channels))
    in_vmem = pl.BlockSpec(memory_space=pltpu.VMEM)
    outgoing = pl.pallas_call(
        functools.partial(spectra_kernel, owners),
        out_shape=jax.ShapeDtypeStruct((lines, rows, feed_count), jnp.bfloat16),
        in_specs=[pl.BlockSpec(memory_space=pltpu.HBM)] * 3,
        out_specs=in_vmem,
        scratch_shapes=[
            pltpu.VMEM(pfb_taps.shape, jnp.float32),
            pltpu.VMEM(dft.shape, jnp.float32),
            pltpu.VMEM((feed_count, samples.shape[2]), jnp.bfloat16),
            pltpu.VMEM((fft_len, 2 * tap_count * columns), jnp.bfloat16),
            pltpu.VMEM((feed_count, 2 * tap_count * columns), jnp.float32),
            pltpu.VMEM((frame_count + tap_count - 1, columns, feed_count), jnp.float32),
            pltpu.VMEM((columns, 2 * frame_count, feed_count), jnp.float32),
            pltpu.SemaphoreType.DMA((2,)),
            pltpu.SemaphoreType.DMA((frame_count * PIECES,)),
        ],
        compiler_params=pltpu.CompilerParams(vmem_limit_bytes=44 * 2**20),
        name="spectra",
    )(*[pltpu.with_memory_space_constraint(v, pltpu.HBM) for v in (samples, pfb_taps, dft)])
    same_core = [[line * CORES + core for line in range(lines)] for core in range(CORES)]
    own = lax.all_to_all(outgoing, "feed", 0, 0, axis_index_groups=same_core, tiled=True)
    other = lax.ppermute(own, "feed", [(d, d ^ 1) for d in range(devices)])
    return pl.pallas_call(
        functools.partial(correlate_kernel, 1.0 / spectra_count, owners),
        out_shape=jax.ShapeDtypeStruct((ROWS_DEV, 2 * total_feeds), jnp.float32),
        in_specs=[in_vmem, in_vmem],
        out_specs=pl.BlockSpec(memory_space=pl.ANY),
        scratch_shapes=[
            pltpu.VMEM((2 * spectra_count, total_feeds), jnp.bfloat16),
            pltpu.VMEM((2 * ROWS_DEV, 2 * spectra_count), jnp.bfloat16),
            pltpu.VMEM((ROWS_DEV, 2 * total_feeds), jnp.float32),
            pltpu.SemaphoreType.DMA((total_feeds // COLUMNS, 2)),
        ],
        compiler_params=pltpu.CompilerParams(vmem_limit_bytes=32 * 2**20),
        name="correlate",
    )(own, other)


def solution(mesh):
    placed = (P(("grp", "feed"), None, None), P())
    return jax.shard_map(
        body, mesh=mesh, in_specs=placed, out_specs=P(("grp", "feed"), None), check_vma=False
    )
```

```python
import functools
import math

import jax
import jax.numpy as jnp
import numpy as np
from jax import lax
from jax.experimental import pallas as pl
from jax.experimental.pallas import tpu as pltpu
from jax.sharding import PartitionSpec as P

FIRST_CH = 1536
TIME_BLOCKS = 2
ROWS_DEV = 512
CORES = 2
PIECES = 4
TABLE_STEP = 1024
COLUMNS = 256


def dft_rows(fft_len, first_channel, channel_count):
    sample_ids = np.arange(fft_len, dtype=np.int64)
    channel_ids = first_channel + np.arange(channel_count, dtype=np.int64)
    phase = channel_ids[:, None] * sample_ids[None, :] % fft_len
    angle = phase.astype(np.float64) * (2.0 * math.pi / fft_len)
    return np.concatenate([np.cos(angle), -np.sin(angle)], axis=0).astype(np.float32)


def spectra_kernel(
    owners, x_hbm, taps_hbm, dft_hbm, out_ref,
    taps_ref, dft_ref, x_buf, table, raw, window, parts, small_sems, sems,
):
    tap_count, fft_len = taps_ref.shape
    columns = dft_ref.shape[0]
    channels = columns // 2
    frame_count = x_hbm.shape[2] // fft_len
    piece = fft_len // PIECES
    edge = tap_count - 1
    width = tap_count * columns
    later_block = lax.axis_index("feed") >= channels * owners // TIME_BLOCKS

    small = [
        pltpu.make_async_copy(taps_hbm, taps_ref, small_sems.at[0]),
        pltpu.make_async_copy(dft_hbm, dft_ref, small_sems.at[1]),
    ]
    for copy in small:
        copy.start()

    def fetch(index):
        span = pl.ds(pl.multiple_of(index * piece, piece), piece)
        return pltpu.make_async_copy(x_hbm.at[0, :, span], x_buf.at[:, span], sems.at[index])

    @pl.loop(0, frame_count * PIECES)
    def _(index):
        fetch(index).start()

    window[...] = jnp.zeros_like(window)
    raw[...] = jnp.zeros_like(raw)
    for copy in small:
        copy.wait()

    @pl.loop(0, fft_len // TABLE_STEP)
    def _(index):
        span = pl.ds(pl.multiple_of(index * TABLE_STEP, TABLE_STEP), TABLE_STEP)
        dft = dft_ref[:, span]
        scaled = jnp.concatenate([taps_ref[m : m + 1, span] * dft for m in range(tap_count)], axis=0)
        high = scaled.astype(jnp.bfloat16).astype(jnp.float32)
        both = jnp.concatenate([high, scaled - high], axis=0)
        table[span, :] = both.T.astype(jnp.bfloat16)

    def fold(frame, total):
        turned = total.T
        summed = turned[:width] + turned[width:]
        for m in range(tap_count):
            window[frame + edge - m] += summed[m * columns : (m + 1) * columns]

    def two_dots(frame, begin, depth):
        total = None
        for offset in (begin, begin + depth):
            start = pl.multiple_of(frame * fft_len + offset, depth)
            product = jnp.dot(
                x_buf[:, pl.ds(start, depth)],
                table[offset : offset + depth, :],
                preferred_element_type=jnp.float32,
            )
            total = product if total is None else total + product
        return total

    @pl.loop(0, frame_count - 1)
    def _(frame):
        for p in range(PIECES):
            fetch(frame * PIECES + p).wait()
        fold(jnp.maximum(frame - 1, 0), raw[...])
        raw[...] = two_dots(frame, 0, fft_len // 2)

    last = frame_count - 1
    total = None
    for p in range(0, PIECES, 2):
        for k in (p, p + 1):
            fetch(last * PIECES + k).wait()
        if p == 0:
            fold(last - 1, raw[...])
        product = two_dots(last, p * piece, piece)
        total = product if total is None else total + product
    fold(last, total)

    for spot in range(frame_count + edge):
        parts[:, spot, :] = window[spot]

    copies = out_ref.shape[0] // channels
    for c in range(channels):
        now = jnp.concatenate([parts[c, :frame_count], parts[channels + c, :frame_count]], axis=0)
        high = now.astype(jnp.bfloat16)
        low = now - high.astype(jnp.float32)
        low = jnp.concatenate([low[:4], low[frame_count : frame_count + 4]], axis=0)
        tail = jnp.concatenate(
            [parts[c, frame_count : frame_count + 4], parts[channels + c, frame_count : frame_count + 4]],
            axis=0,
        )
        sublane = lax.broadcasted_iota(jnp.int32, tail.shape, 0)
        tail = jnp.where(sublane % 4 < edge, tail, 0.0)
        extra = jnp.where(later_block, low, tail).astype(jnp.bfloat16)
        whole = jnp.concatenate([high, extra], axis=0)
        for o in range(copies):
            out_ref[c * copies + o] = whole


def correlate_kernel(
    scale, owners, own_ref, other_ref, out_hbm, right, left, out_buf, sems
):
    lines, rows, feed_count = own_ref.shape
    frame_count = rows // 3
    total_feeds = right.shape[1]
    my_index = lax.axis_index("feed")
    my_core = my_index % CORES

    def join(group, low, high):
        place = pl.ds(group * feed_count, feed_count)
        if not isinstance(group, int):
            place = pl.ds(pl.multiple_of(group * feed_count, feed_count), feed_count)
        extra = low[2 * frame_count :].astype(jnp.float32) + high[2 * frame_count :].astype(jnp.float32)
        zero = jnp.zeros((frame_count - 4, feed_count), jnp.float32)
        extra = jnp.concatenate([extra[:4], zero, extra[4:8], zero], axis=0)
        fixed = high[: 2 * frame_count].astype(jnp.float32) + extra
        right[: 2 * frame_count, place] = low[: 2 * frame_count]
        right[2 * frame_count :, place] = fixed.astype(jnp.bfloat16)

    later = lines // TIME_BLOCKS
    for line in range(later):
        if feed_count % 128 == 0:
            for ref, core in ((own_ref, my_core), (other_ref, CORES - 1 - my_core)):
                join(line * CORES + core, ref[line], ref[later + line])
        else:
            for core in range(CORES):
                low, high = [
                    jnp.where(my_core == core, own_ref[k], other_ref[k]) for k in (line, later + line)
                ]
                join(line * CORES + core, low, high)
    row_start = my_index % owners * ROWS_DEV
    mine = right[:, pl.ds(pl.multiple_of(row_start, ROWS_DEV), ROWS_DEV)].astype(jnp.float32)
    halves = [mine[k * frame_count : (k + 1) * frame_count] for k in range(4)]
    swapped = jnp.concatenate([halves[1], -halves[0], halves[3], -halves[2]], axis=0)
    left[:ROWS_DEV] = mine.T.astype(jnp.bfloat16)
    left[ROWS_DEV:] = swapped.T.astype(jnp.bfloat16)

    def span(block, part):
        start = part * total_feeds + block * COLUMNS
        return pl.ds(pl.multiple_of(start, COLUMNS), COLUMNS)

    def store(block, part):
        cut = span(block, part)
        return pltpu.make_async_copy(out_buf.at[:, cut], out_hbm.at[:, cut], sems.at[block, part])

    @pl.loop(0, total_feeds // COLUMNS)
    def _(block):
        product = jnp.dot(left[...], right[:, span(block, 0)], preferred_element_type=jnp.float32)
        product = product * scale
        for part in range(2):
            out_buf[:, span(block, part)] = product[part * ROWS_DEV : (part + 1) * ROWS_DEV]
            store(block, part).start()

    @pl.loop(0, total_feeds // COLUMNS)
    def _(block):
        for part in range(2):
            store(block, part).wait()


def join_blocks(low, high):
    frame_count = low.shape[0] // 3
    feed_count = low.shape[1]
    extra = low[2 * frame_count :].astype(jnp.float32) + high[2 * frame_count :].astype(jnp.float32)
    zero = jnp.zeros((frame_count - 4, feed_count), jnp.float32)
    extra = jnp.concatenate([extra[:4], zero, extra[4:8], zero], axis=0)
    fixed = high[: 2 * frame_count].astype(jnp.float32) + extra
    return jnp.concatenate([low[: 2 * frame_count], fixed.astype(jnp.bfloat16)], axis=0)


def left_rows(block):
    mine = block.astype(jnp.float32)
    size = mine.shape[0] // 4
    parts = [mine[k * size : (k + 1) * size] for k in range(4)]
    swapped = jnp.concatenate([parts[1], -parts[0], parts[3], -parts[2]], axis=0)
    return jnp.concatenate([mine.T, swapped.T], axis=0).astype(jnp.bfloat16)


def store_block(out_buf, out_hbm, sem, row_group, column_group, part):
    size = out_hbm.shape[0] // CORES
    row = pl.multiple_of(row_group * size, size)
    column = pl.multiple_of(part * (out_hbm.shape[1] // 2) + column_group * size, size)
    place = (pl.ds(row, size), pl.ds(column, size))
    return place, pltpu.make_async_copy(out_buf.at[place], out_hbm.at[place], sem)


def near_kernel(scale, owners, own_ref, out_hbm, right, out_buf, sems):
    lines, _, size = own_ref.shape
    later = lines // TIME_BLOCKS
    my_index = lax.axis_index("feed")
    my_core = my_index % CORES

    for line in range(later):
        right[line] = join_blocks(own_ref[line], own_ref[later + line])
    left = left_rows(right[my_index % owners])
    copies = []
    for line in range(later):
        product = jnp.dot(left, right[line], preferred_element_type=jnp.float32) * scale
        for part in range(2):
            place, copy = store_block(
                out_buf, out_hbm, sems.at[line, part], my_core, line * CORES + my_core, part
            )
            out_buf[place] = product[part * size : (part + 1) * size]
            copy.start()
            copies.append(copy)
    for copy in copies:
        copy.wait()


def far_kernel(scale, owners, own_ref, other_ref, _, out_hbm, near, far, left, out_buf, sems):
    lines, _, size = own_ref.shape
    later = lines // TIME_BLOCKS
    my_index = lax.axis_index("feed")
    my_core = my_index % CORES
    other_core = CORES - 1 - my_core
    place_in_plane = my_index % owners

    for line in range(later):
        near[line] = join_blocks(own_ref[line], own_ref[later + line])
        far[line] = join_blocks(other_ref[line], other_ref[later + line])
    left[0] = left_rows(near[place_in_plane])
    left[1] = left_rows(far[place_in_plane])

    def block(line, turn):
        row_group = my_core if turn == 0 else other_core
        column_group = line * CORES + (my_core if turn == 2 else other_core)
        for part in range(2):
            yield store_block(out_buf, out_hbm, sems.at[line, turn, part], row_group, column_group, part)

    @pl.loop(0, later)
    def _(line):
        for turn in range(3):
            source = near if turn == 2 else far
            product = jnp.dot(left[min(turn, 1)], source[line], preferred_element_type=jnp.float32)
            product = product * scale
            for part, (place, copy) in enumerate(block(line, turn)):
                out_buf[place] = product[part * size : (part + 1) * size]
                copy.start()

    @pl.loop(0, later)
    def _(line):
        for turn in range(3):
            for _, copy in block(line, turn):
                copy.wait()


def correlate_in_two(own, swap, owners, total_feeds, scale):
    lines, rows, size = own.shape
    depth = rows // 3 * 4
    later = lines // TIME_BLOCKS
    in_vmem = pl.BlockSpec(memory_space=pltpu.VMEM)
    anywhere = pl.BlockSpec(memory_space=pl.ANY)
    shape = jax.ShapeDtypeStruct((ROWS_DEV, 2 * total_feeds), jnp.float32)
    other = swap(own)
    started = pl.pallas_call(
        functools.partial(near_kernel, scale, owners),
        out_shape=shape,
        in_specs=[in_vmem],
        out_specs=anywhere,
        scratch_shapes=[
            pltpu.VMEM((later, depth, size), jnp.bfloat16),
            pltpu.VMEM(shape.shape, jnp.float32),
            pltpu.SemaphoreType.DMA((later, 2)),
        ],
        cost_estimate=pl.CostEstimate(
            flops=depth * shape.size // 2, bytes_accessed=shape.size, transcendentals=0
        ),
        compiler_params=pltpu.CompilerParams(vmem_limit_bytes=32 * 2**20),
        name="near",
    )(own)
    return pl.pallas_call(
        functools.partial(far_kernel, scale, owners),
        out_shape=shape,
        in_specs=[in_vmem, in_vmem, anywhere],
        out_specs=anywhere,
        input_output_aliases={2: 0},
        scratch_shapes=[
            pltpu.VMEM((later, depth, size), jnp.bfloat16),
            pltpu.VMEM((later, depth, size), jnp.bfloat16),
            pltpu.VMEM((2, 2 * size, depth), jnp.bfloat16),
            pltpu.VMEM(shape.shape, jnp.float32),
            pltpu.SemaphoreType.DMA((later, 3, 2)),
        ],
        compiler_params=pltpu.CompilerParams(vmem_limit_bytes=32 * 2**20),
        name="far",
    )(own, other, started)


def body(samples, pfb_taps):
    feed_count = samples.shape[1]
    tap_count, fft_len = pfb_taps.shape
    frame_count = samples.shape[2] // fft_len
    devices = lax.axis_size("feed")
    total_feeds = feed_count * devices // TIME_BLOCKS
    channels = devices * ROWS_DEV // total_feeds
    owners = total_feeds // ROWS_DEV
    spectra_count = TIME_BLOCKS * frame_count
    columns = 2 * channels
    rows = 3 * frame_count
    lines = devices // CORES
    dft = jnp.asarray(dft_rows(fft_len, FIRST_CH, channels))
    in_vmem = pl.BlockSpec(memory_space=pltpu.VMEM)
    outgoing = pl.pallas_call(
        functools.partial(spectra_kernel, owners),
        out_shape=jax.ShapeDtypeStruct((lines, rows, feed_count), jnp.bfloat16),
        in_specs=[pl.BlockSpec(memory_space=pltpu.HBM)] * 3,
        out_specs=in_vmem,
        scratch_shapes=[
            pltpu.VMEM(pfb_taps.shape, jnp.float32),
            pltpu.VMEM(dft.shape, jnp.float32),
            pltpu.VMEM((feed_count, samples.shape[2]), jnp.bfloat16),
            pltpu.VMEM((fft_len, 2 * tap_count * columns), jnp.bfloat16),
            pltpu.VMEM((feed_count, 2 * tap_count * columns), jnp.float32),
            pltpu.VMEM((frame_count + tap_count - 1, columns, feed_count), jnp.float32),
            pltpu.VMEM((columns, 2 * frame_count, feed_count), jnp.float32),
            pltpu.SemaphoreType.DMA((2,)),
            pltpu.SemaphoreType.DMA((frame_count * PIECES,)),
        ],
        compiler_params=pltpu.CompilerParams(vmem_limit_bytes=44 * 2**20),
        name="spectra",
    )(*[pltpu.with_memory_space_constraint(v, pltpu.HBM) for v in (samples, pfb_taps, dft)])
    same_core = [[line * CORES + core for line in range(lines)] for core in range(CORES)]
    own = lax.all_to_all(outgoing, "feed", 0, 0, axis_index_groups=same_core, tiled=True)

    def swap(value):
        return lax.ppermute(value, "feed", [(d, d ^ 1) for d in range(devices)])

    if feed_count * CORES == ROWS_DEV and feed_count % 128 == 0:
        return correlate_in_two(own, swap, owners, total_feeds, 1.0 / spectra_count)
    other = swap(own)
    return pl.pallas_call(
        functools.partial(correlate_kernel, 1.0 / spectra_count, owners),
        out_shape=jax.ShapeDtypeStruct((ROWS_DEV, 2 * total_feeds), jnp.float32),
        in_specs=[in_vmem, in_vmem],
        out_specs=pl.BlockSpec(memory_space=pl.ANY),
        scratch_shapes=[
            pltpu.VMEM((2 * spectra_count, total_feeds), jnp.bfloat16),
            pltpu.VMEM((2 * ROWS_DEV, 2 * spectra_count), jnp.bfloat16),
            pltpu.VMEM((ROWS_DEV, 2 * total_feeds), jnp.float32),
            pltpu.SemaphoreType.DMA((total_feeds // COLUMNS, 2)),
        ],
        compiler_params=pltpu.CompilerParams(vmem_limit_bytes=32 * 2**20),
        name="correlate",
    )(own, other)


def solution(mesh):
    placed = (P(("grp", "feed"), None, None), P())
    return jax.shard_map(
        body, mesh=mesh, in_specs=placed, out_specs=P(("grp", "feed"), None), check_vma=False
    )
```

```python
import functools
import math

import jax
import jax.numpy as jnp
import numpy as np
from jax import lax
from jax.experimental import pallas as pl
from jax.experimental.pallas import tpu as pltpu
from jax.sharding import PartitionSpec as P

FIRST_CH = 1536
TIME_BLOCKS = 2
ROWS_DEV = 512
CORES = 2
PIECES = 4
TABLE_STEP = 1024
COLUMNS = 256


def dft_rows(fft_len, first_channel, channel_count):
    sample_ids = np.arange(fft_len, dtype=np.int64)
    channel_ids = first_channel + np.arange(channel_count, dtype=np.int64)
    phase = channel_ids[:, None] * sample_ids[None, :] % fft_len
    angle = phase.astype(np.float64) * (2.0 * math.pi / fft_len)
    return np.concatenate([np.cos(angle), -np.sin(angle)], axis=0).astype(np.float32)


def spectra_kernel(
    owners, x_hbm, taps_hbm, dft_hbm, out_ref,
    taps_ref, dft_ref, x_buf, table, raw, window, parts, small_sems, sems,
):
    tap_count, fft_len = taps_ref.shape
    columns = dft_ref.shape[0]
    channels = columns // 2
    frame_count = x_hbm.shape[2] // fft_len
    piece = fft_len // PIECES
    edge = tap_count - 1
    width = tap_count * columns
    later_block = lax.axis_index("feed") >= channels * owners // TIME_BLOCKS

    small = [
        pltpu.make_async_copy(taps_hbm, taps_ref, small_sems.at[0]),
        pltpu.make_async_copy(dft_hbm, dft_ref, small_sems.at[1]),
    ]
    for copy in small:
        copy.start()

    def fetch(index):
        span = pl.ds(pl.multiple_of(index * piece, piece), piece)
        return pltpu.make_async_copy(x_hbm.at[0, :, span], x_buf.at[:, span], sems.at[index])

    @pl.loop(0, frame_count * PIECES)
    def _(index):
        fetch(index).start()

    window[...] = jnp.zeros_like(window)
    raw[...] = jnp.zeros_like(raw)
    for copy in small:
        copy.wait()

    @pl.loop(0, fft_len // TABLE_STEP)
    def _(index):
        span = pl.ds(pl.multiple_of(index * TABLE_STEP, TABLE_STEP), TABLE_STEP)
        dft = dft_ref[:, span]
        scaled = jnp.concatenate([taps_ref[m : m + 1, span] * dft for m in range(tap_count)], axis=0)
        high = scaled.astype(jnp.bfloat16).astype(jnp.float32)
        both = jnp.concatenate([high, scaled - high], axis=0)
        table[span, :] = both.T.astype(jnp.bfloat16)

    def fold(frame, total):
        turned = total.T
        summed = turned[:width] + turned[width:]
        for m in range(tap_count):
            window[frame + edge - m] += summed[m * columns : (m + 1) * columns]

    def two_dots(frame, begin, depth):
        total = None
        for offset in (begin, begin + depth):
            start = pl.multiple_of(frame * fft_len + offset, depth)
            product = jnp.dot(
                x_buf[:, pl.ds(start, depth)],
                table[offset : offset + depth, :],
                preferred_element_type=jnp.float32,
            )
            total = product if total is None else total + product
        return total

    @pl.loop(0, frame_count - 1)
    def _(frame):
        for p in range(PIECES):
            fetch(frame * PIECES + p).wait()
        fold(jnp.maximum(frame - 1, 0), raw[...])
        raw[...] = two_dots(frame, 0, fft_len // 2)

    last = frame_count - 1
    total = None
    for begin, end in ((0, PIECES // 2), *((p, p + 1) for p in range(PIECES // 2, PIECES))):
        for p in range(begin, end):
            fetch(last * PIECES + p).wait()
        if begin == 0:
            fold(last - 1, raw[...])
        product = two_dots(last, begin * piece, (end - begin) * piece // 2)
        total = product if total is None else total + product
    fold(last, total)

    for spot in range(frame_count + edge):
        parts[:, spot, :] = window[spot]

    copies = out_ref.shape[0] // channels
    for c in range(channels):
        now = jnp.concatenate([parts[c, :frame_count], parts[channels + c, :frame_count]], axis=0)
        high = now.astype(jnp.bfloat16)
        low = now - high.astype(jnp.float32)
        low = jnp.concatenate([low[:4], low[frame_count : frame_count + 4]], axis=0)
        tail = jnp.concatenate(
            [parts[c, frame_count : frame_count + 4], parts[channels + c, frame_count : frame_count + 4]],
            axis=0,
        )
        sublane = lax.broadcasted_iota(jnp.int32, tail.shape, 0)
        tail = jnp.where(sublane % 4 < edge, tail, 0.0)
        extra = jnp.where(later_block, low, tail).astype(jnp.bfloat16)
        whole = jnp.concatenate([high, extra], axis=0)
        for o in range(copies):
            out_ref[c * copies + o] = whole


def correlate_kernel(
    scale, owners, own_ref, other_ref, out_hbm, right, left, out_buf, sems
):
    lines, rows, feed_count = own_ref.shape
    frame_count = rows // 3
    total_feeds = right.shape[1]
    my_index = lax.axis_index("feed")
    my_core = my_index % CORES

    def join(group, low, high):
        place = pl.ds(group * feed_count, feed_count)
        if not isinstance(group, int):
            place = pl.ds(pl.multiple_of(group * feed_count, feed_count), feed_count)
        extra = low[2 * frame_count :].astype(jnp.float32) + high[2 * frame_count :].astype(jnp.float32)
        zero = jnp.zeros((frame_count - 4, feed_count), jnp.float32)
        extra = jnp.concatenate([extra[:4], zero, extra[4:8], zero], axis=0)
        fixed = high[: 2 * frame_count].astype(jnp.float32) + extra
        right[: 2 * frame_count, place] = low[: 2 * frame_count]
        right[2 * frame_count :, place] = fixed.astype(jnp.bfloat16)

    later = lines // TIME_BLOCKS
    for line in range(later):
        if feed_count % 128 == 0:
            for ref, core in ((own_ref, my_core), (other_ref, CORES - 1 - my_core)):
                join(line * CORES + core, ref[line], ref[later + line])
        else:
            for core in range(CORES):
                low, high = [
                    jnp.where(my_core == core, own_ref[k], other_ref[k]) for k in (line, later + line)
                ]
                join(line * CORES + core, low, high)
    row_start = my_index % owners * ROWS_DEV
    mine = right[:, pl.ds(pl.multiple_of(row_start, ROWS_DEV), ROWS_DEV)].astype(jnp.float32)
    halves = [mine[k * frame_count : (k + 1) * frame_count] for k in range(4)]
    swapped = jnp.concatenate([halves[1], -halves[0], halves[3], -halves[2]], axis=0)
    left[:ROWS_DEV] = mine.T.astype(jnp.bfloat16)
    left[ROWS_DEV:] = swapped.T.astype(jnp.bfloat16)

    def span(block, part):
        start = part * total_feeds + block * COLUMNS
        return pl.ds(pl.multiple_of(start, COLUMNS), COLUMNS)

    def store(block, part):
        cut = span(block, part)
        return pltpu.make_async_copy(out_buf.at[:, cut], out_hbm.at[:, cut], sems.at[block, part])

    @pl.loop(0, total_feeds // COLUMNS)
    def _(block):
        product = jnp.dot(left[...], right[:, span(block, 0)], preferred_element_type=jnp.float32)
        product = product * scale
        for part in range(2):
            out_buf[:, span(block, part)] = product[part * ROWS_DEV : (part + 1) * ROWS_DEV]
            store(block, part).start()

    @pl.loop(0, total_feeds // COLUMNS)
    def _(block):
        for part in range(2):
            store(block, part).wait()


def join_blocks(low, high):
    frame_count = low.shape[0] // 3
    feed_count = low.shape[1]
    extra = low[2 * frame_count :].astype(jnp.float32) + high[2 * frame_count :].astype(jnp.float32)
    zero = jnp.zeros((frame_count - 4, feed_count), jnp.float32)
    extra = jnp.concatenate([extra[:4], zero, extra[4:8], zero], axis=0)
    fixed = high[: 2 * frame_count].astype(jnp.float32) + extra
    return jnp.concatenate([low[: 2 * frame_count], fixed.astype(jnp.bfloat16)], axis=0)


def left_rows(block):
    mine = block.astype(jnp.float32)
    size = mine.shape[0] // 4
    parts = [mine[k * size : (k + 1) * size] for k in range(4)]
    swapped = jnp.concatenate([parts[1], -parts[0], parts[3], -parts[2]], axis=0)
    return jnp.concatenate([mine.T, swapped.T], axis=0).astype(jnp.bfloat16)


def store_block(out_buf, out_hbm, sem, row_group, column_group, part):
    size = out_hbm.shape[0] // CORES
    row = pl.multiple_of(row_group * size, size)
    column = pl.multiple_of(part * (out_hbm.shape[1] // 2) + column_group * size, size)
    place = (pl.ds(row, size), pl.ds(column, size))
    return place, pltpu.make_async_copy(out_buf.at[place], out_hbm.at[place], sem)


def near_kernel(scale, owners, own_ref, out_hbm, right, left, out_buf, sems):
    lines, _, size = own_ref.shape
    later = lines // TIME_BLOCKS
    my_index = lax.axis_index("feed")
    my_core = my_index % CORES

    for line in range(later):
        right[line] = join_blocks(own_ref[line], own_ref[later + line])
    left[...] = left_rows(right[my_index % owners])
    copies = []
    for line in range(later):
        product = jnp.dot(left[...], right[line], preferred_element_type=jnp.float32) * scale
        for part in range(2):
            place, copy = store_block(
                out_buf, out_hbm, sems.at[line, part], my_core, line * CORES + my_core, part
            )
            out_buf[place] = product[part * size : (part + 1) * size]
            copy.start()
            copies.append(copy)
    for copy in copies:
        copy.wait()


def far_kernel(
    scale, owners, other_ref, near, near_left, _, out_hbm, far, far_left, out_buf, sems
):
    lines, _, size = other_ref.shape
    later = lines // TIME_BLOCKS
    my_index = lax.axis_index("feed")
    my_core = my_index % CORES
    other_core = CORES - 1 - my_core

    for line in range(later):
        far[line] = join_blocks(other_ref[line], other_ref[later + line])
    far_left[...] = left_rows(far[my_index % owners])

    def block(line, turn):
        row_group = my_core if turn == 0 else other_core
        column_group = line * CORES + (my_core if turn == 2 else other_core)
        for part in range(2):
            yield store_block(out_buf, out_hbm, sems.at[line, turn, part], row_group, column_group, part)

    @pl.loop(0, later)
    def _(line):
        for turn in range(3):
            source = near if turn == 2 else far
            left = near_left if turn == 0 else far_left
            product = jnp.dot(left[...], source[line], preferred_element_type=jnp.float32)
            product = product * scale
            for part, (place, copy) in enumerate(block(line, turn)):
                out_buf[place] = product[part * size : (part + 1) * size]
                copy.start()

    @pl.loop(0, later)
    def _(line):
        for turn in range(3):
            for _, copy in block(line, turn):
                copy.wait()


def correlate_in_two(own, swap, owners, total_feeds, scale):
    lines, rows, size = own.shape
    depth = rows // 3 * 4
    later = lines // TIME_BLOCKS
    in_vmem = pl.BlockSpec(memory_space=pltpu.VMEM)
    anywhere = pl.BlockSpec(memory_space=pl.ANY)
    shape = jax.ShapeDtypeStruct((ROWS_DEV, 2 * total_feeds), jnp.float32)
    other = swap(own)
    joined = jax.ShapeDtypeStruct((later, depth, size), jnp.bfloat16)
    left = jax.ShapeDtypeStruct((2 * size, depth), jnp.bfloat16)
    started, near, near_left = pl.pallas_call(
        functools.partial(near_kernel, scale, owners),
        out_shape=[shape, joined, left],
        in_specs=[in_vmem],
        out_specs=[anywhere, in_vmem, in_vmem],
        scratch_shapes=[
            pltpu.VMEM(shape.shape, jnp.float32),
            pltpu.SemaphoreType.DMA((later, 2)),
        ],
        cost_estimate=pl.CostEstimate(
            flops=depth * shape.size // 2, bytes_accessed=shape.size, transcendentals=0
        ),
        compiler_params=pltpu.CompilerParams(vmem_limit_bytes=32 * 2**20),
        name="near",
    )(own)
    return pl.pallas_call(
        functools.partial(far_kernel, scale, owners),
        out_shape=shape,
        in_specs=[in_vmem, in_vmem, in_vmem, anywhere],
        out_specs=anywhere,
        input_output_aliases={3: 0},
        scratch_shapes=[
            pltpu.VMEM(joined.shape, jnp.bfloat16),
            pltpu.VMEM(left.shape, jnp.bfloat16),
            pltpu.VMEM(shape.shape, jnp.float32),
            pltpu.SemaphoreType.DMA((later, 3, 2)),
        ],
        compiler_params=pltpu.CompilerParams(vmem_limit_bytes=32 * 2**20),
        name="far",
    )(other, near, near_left, started)


def body(samples, pfb_taps):
    feed_count = samples.shape[1]
    tap_count, fft_len = pfb_taps.shape
    frame_count = samples.shape[2] // fft_len
    devices = lax.axis_size("feed")
    total_feeds = feed_count * devices // TIME_BLOCKS
    channels = devices * ROWS_DEV // total_feeds
    owners = total_feeds // ROWS_DEV
    spectra_count = TIME_BLOCKS * frame_count
    columns = 2 * channels
    rows = 3 * frame_count
    lines = devices // CORES
    dft = jnp.asarray(dft_rows(fft_len, FIRST_CH, channels))
    in_vmem = pl.BlockSpec(memory_space=pltpu.VMEM)
    outgoing = pl.pallas_call(
        functools.partial(spectra_kernel, owners),
        out_shape=jax.ShapeDtypeStruct((lines, rows, feed_count), jnp.bfloat16),
        in_specs=[pl.BlockSpec(memory_space=pltpu.HBM)] * 3,
        out_specs=in_vmem,
        scratch_shapes=[
            pltpu.VMEM(pfb_taps.shape, jnp.float32),
            pltpu.VMEM(dft.shape, jnp.float32),
            pltpu.VMEM((feed_count, samples.shape[2]), jnp.bfloat16),
            pltpu.VMEM((fft_len, 2 * tap_count * columns), jnp.bfloat16),
            pltpu.VMEM((feed_count, 2 * tap_count * columns), jnp.float32),
            pltpu.VMEM((frame_count + tap_count - 1, columns, feed_count), jnp.float32),
            pltpu.VMEM((columns, 2 * frame_count, feed_count), jnp.float32),
            pltpu.SemaphoreType.DMA((2,)),
            pltpu.SemaphoreType.DMA((frame_count * PIECES,)),
        ],
        compiler_params=pltpu.CompilerParams(vmem_limit_bytes=44 * 2**20),
        name="spectra",
    )(*[pltpu.with_memory_space_constraint(v, pltpu.HBM) for v in (samples, pfb_taps, dft)])
    same_core = [[line * CORES + core for line in range(lines)] for core in range(CORES)]
    own = lax.all_to_all(outgoing, "feed", 0, 0, axis_index_groups=same_core, tiled=True)

    def swap(value):
        return lax.ppermute(value, "feed", [(d, d ^ 1) for d in range(devices)])

    if feed_count * CORES == ROWS_DEV and feed_count % 128 == 0:
        return correlate_in_two(own, swap, owners, total_feeds, 1.0 / spectra_count)
    other = swap(own)
    return pl.pallas_call(
        functools.partial(correlate_kernel, 1.0 / spectra_count, owners),
        out_shape=jax.ShapeDtypeStruct((ROWS_DEV, 2 * total_feeds), jnp.float32),
        in_specs=[in_vmem, in_vmem],
        out_specs=pl.BlockSpec(memory_space=pl.ANY),
        scratch_shapes=[
            pltpu.VMEM((2 * spectra_count, total_feeds), jnp.bfloat16),
            pltpu.VMEM((2 * ROWS_DEV, 2 * spectra_count), jnp.bfloat16),
            pltpu.VMEM((ROWS_DEV, 2 * total_feeds), jnp.float32),
            pltpu.SemaphoreType.DMA((total_feeds // COLUMNS, 2)),
        ],
        compiler_params=pltpu.CompilerParams(vmem_limit_bytes=32 * 2**20),
        name="correlate",
    )(own, other)


def solution(mesh):
    placed = (P(("grp", "feed"), None, None), P())
    return jax.shard_map(
        body, mesh=mesh, in_specs=placed, out_specs=P(("grp", "feed"), None), check_vma=False
    )
```

```python
import functools
import math

import jax
import jax.numpy as jnp
import numpy as np
from jax import lax
from jax.experimental import pallas as pl
from jax.experimental.pallas import tpu as pltpu
from jax.sharding import PartitionSpec as P

FIRST_CH = 1536
TIME_BLOCKS = 2
ROWS_DEV = 512
CORES = 2
PIECES = 2
TABLE_STEP = 1024
COLUMNS = 256


def dft_rows(fft_len, first_channel, channel_count):
    sample_ids = np.arange(fft_len, dtype=np.int64)
    channel_ids = first_channel + np.arange(channel_count, dtype=np.int64)
    phase = channel_ids[:, None] * sample_ids[None, :] % fft_len
    angle = phase.astype(np.float64) * (2.0 * math.pi / fft_len)
    return np.concatenate([np.cos(angle), -np.sin(angle)], axis=0).astype(np.float32)


def spectra_kernel(
    owners, x_hbm, taps_hbm, dft_hbm, out_ref,
    taps_ref, dft_ref, x_buf, table, raw, window, parts, small_sems, sems,
):
    tap_count, fft_len = taps_ref.shape
    columns = dft_ref.shape[0]
    channels = columns // 2
    frame_count = x_hbm.shape[2] // fft_len
    piece = fft_len // PIECES
    edge = tap_count - 1
    width = tap_count * columns
    later_block = lax.axis_index("feed") >= channels * owners // TIME_BLOCKS

    small = [
        pltpu.make_async_copy(taps_hbm, taps_ref, small_sems.at[0]),
        pltpu.make_async_copy(dft_hbm, dft_ref, small_sems.at[1]),
    ]
    for copy in small:
        copy.start()

    def fetch(index):
        span = pl.ds(pl.multiple_of(index * piece, piece), piece)
        return pltpu.make_async_copy(x_hbm.at[0, :, span], x_buf.at[:, span], sems.at[index])

    @pl.loop(0, frame_count * PIECES)
    def _(index):
        fetch(index).start()

    window[...] = jnp.zeros_like(window)
    raw[...] = jnp.zeros_like(raw)
    for copy in small:
        copy.wait()

    @pl.loop(0, fft_len // TABLE_STEP)
    def _(index):
        span = pl.ds(pl.multiple_of(index * TABLE_STEP, TABLE_STEP), TABLE_STEP)
        dft = dft_ref[:, span]
        scaled = jnp.concatenate([taps_ref[m : m + 1, span] * dft for m in range(tap_count)], axis=0)
        high = scaled.astype(jnp.bfloat16).astype(jnp.float32)
        both = jnp.concatenate([high, scaled - high], axis=0)
        table[span, :] = both.T.astype(jnp.bfloat16)

    def fold(frame, total):
        turned = total.T
        summed = turned[:width] + turned[width:]
        for m in range(tap_count):
            window[frame + edge - m] += summed[m * columns : (m + 1) * columns]

    def two_dots(frame, begin, depth):
        total = None
        for offset in (begin, begin + depth):
            start = pl.multiple_of(frame * fft_len + offset, depth)
            product = jnp.dot(
                x_buf[:, pl.ds(start, depth)],
                table[offset : offset + depth, :],
                preferred_element_type=jnp.float32,
            )
            total = product if total is None else total + product
        return total

    @pl.loop(0, frame_count - 1)
    def _(frame):
        for p in range(PIECES):
            fetch(frame * PIECES + p).wait()
        fold(jnp.maximum(frame - 1, 0), raw[...])
        raw[...] = two_dots(frame, 0, fft_len // 2)

    last = frame_count - 1
    total = None
    for p in range(PIECES):
        fetch(last * PIECES + p).wait()
        if p == 0:
            fold(last - 1, raw[...])
        product = two_dots(last, p * piece, piece // 2)
        total = product if total is None else total + product
    fold(last, total)

    for spot in range(frame_count + edge):
        parts[:, spot, :] = window[spot]

    copies = out_ref.shape[0] // channels
    for c in range(channels):
        now = jnp.concatenate([parts[c, :frame_count], parts[channels + c, :frame_count]], axis=0)
        high = now.astype(jnp.bfloat16)
        low = now - high.astype(jnp.float32)
        low = jnp.concatenate([low[:4], low[frame_count : frame_count + 4]], axis=0)
        tail = jnp.concatenate(
            [parts[c, frame_count : frame_count + 4], parts[channels + c, frame_count : frame_count + 4]],
            axis=0,
        )
        sublane = lax.broadcasted_iota(jnp.int32, tail.shape, 0)
        tail = jnp.where(sublane % 4 < edge, tail, 0.0)
        extra = jnp.where(later_block, low, tail).astype(jnp.bfloat16)
        whole = jnp.concatenate([high, extra], axis=0)
        for o in range(copies):
            out_ref[c * copies + o] = whole


def correlate_kernel(
    scale, owners, own_ref, other_ref, out_hbm, right, left, out_buf, sems
):
    lines, rows, feed_count = own_ref.shape
    frame_count = rows // 3
    total_feeds = right.shape[1]
    my_index = lax.axis_index("feed")
    my_core = my_index % CORES

    def join(group, low, high):
        place = pl.ds(group * feed_count, feed_count)
        if not isinstance(group, int):
            place = pl.ds(pl.multiple_of(group * feed_count, feed_count), feed_count)
        extra = low[2 * frame_count :].astype(jnp.float32) + high[2 * frame_count :].astype(jnp.float32)
        zero = jnp.zeros((frame_count - 4, feed_count), jnp.float32)
        extra = jnp.concatenate([extra[:4], zero, extra[4:8], zero], axis=0)
        fixed = high[: 2 * frame_count].astype(jnp.float32) + extra
        right[: 2 * frame_count, place] = low[: 2 * frame_count]
        right[2 * frame_count :, place] = fixed.astype(jnp.bfloat16)

    later = lines // TIME_BLOCKS
    for line in range(later):
        if feed_count % 128 == 0:
            for ref, core in ((own_ref, my_core), (other_ref, CORES - 1 - my_core)):
                join(line * CORES + core, ref[line], ref[later + line])
        else:
            for core in range(CORES):
                low, high = [
                    jnp.where(my_core == core, own_ref[k], other_ref[k]) for k in (line, later + line)
                ]
                join(line * CORES + core, low, high)
    row_start = my_index % owners * ROWS_DEV
    mine = right[:, pl.ds(pl.multiple_of(row_start, ROWS_DEV), ROWS_DEV)].astype(jnp.float32)
    halves = [mine[k * frame_count : (k + 1) * frame_count] for k in range(4)]
    swapped = jnp.concatenate([halves[1], -halves[0], halves[3], -halves[2]], axis=0)
    left[:ROWS_DEV] = mine.T.astype(jnp.bfloat16)
    left[ROWS_DEV:] = swapped.T.astype(jnp.bfloat16)

    def span(block, part):
        start = part * total_feeds + block * COLUMNS
        return pl.ds(pl.multiple_of(start, COLUMNS), COLUMNS)

    def store(block, part):
        cut = span(block, part)
        return pltpu.make_async_copy(out_buf.at[:, cut], out_hbm.at[:, cut], sems.at[block, part])

    @pl.loop(0, total_feeds // COLUMNS)
    def _(block):
        product = jnp.dot(left[...], right[:, span(block, 0)], preferred_element_type=jnp.float32)
        product = product * scale
        for part in range(2):
            out_buf[:, span(block, part)] = product[part * ROWS_DEV : (part + 1) * ROWS_DEV]
            store(block, part).start()

    @pl.loop(0, total_feeds // COLUMNS)
    def _(block):
        for part in range(2):
            store(block, part).wait()


def join_blocks(low, high):
    frame_count = low.shape[0] // 3
    feed_count = low.shape[1]
    extra = low[2 * frame_count :].astype(jnp.float32) + high[2 * frame_count :].astype(jnp.float32)
    zero = jnp.zeros((frame_count - 4, feed_count), jnp.float32)
    extra = jnp.concatenate([extra[:4], zero, extra[4:8], zero], axis=0)
    fixed = high[: 2 * frame_count].astype(jnp.float32) + extra
    return jnp.concatenate([low[: 2 * frame_count], fixed.astype(jnp.bfloat16)], axis=0)


def left_rows(block):
    mine = block.astype(jnp.float32)
    size = mine.shape[0] // 4
    parts = [mine[k * size : (k + 1) * size] for k in range(4)]
    swapped = jnp.concatenate([parts[1], -parts[0], parts[3], -parts[2]], axis=0)
    return jnp.concatenate([mine.T, swapped.T], axis=0).astype(jnp.bfloat16)


def store_block(out_buf, out_hbm, sem, row_group, column_group, part):
    size = out_hbm.shape[0] // CORES
    row = pl.multiple_of(row_group * size, size)
    column = pl.multiple_of(part * (out_hbm.shape[1] // 2) + column_group * size, size)
    place = (pl.ds(row, size), pl.ds(column, size))
    return place, pltpu.make_async_copy(out_buf.at[place], out_hbm.at[place], sem)


def near_kernel(scale, owners, own_ref, out_hbm, right, out_buf, sems):
    lines, _, size = own_ref.shape
    later = lines // TIME_BLOCKS
    my_index = lax.axis_index("feed")
    my_core = my_index % CORES

    for line in range(later):
        right[line] = join_blocks(own_ref[line], own_ref[later + line])
    left = left_rows(right[my_index % owners])
    copies = []
    for line in range(later):
        product = jnp.dot(left, right[line], preferred_element_type=jnp.float32) * scale
        for part in range(2):
            place, copy = store_block(
                out_buf, out_hbm, sems.at[line, part], my_core, line * CORES + my_core, part
            )
            out_buf[place] = product[part * size : (part + 1) * size]
            copy.start()
            copies.append(copy)
    for copy in copies:
        copy.wait()


def far_kernel(scale, owners, own_ref, other_ref, _, out_hbm, near, far, left, out_buf, sems):
    lines, _, size = own_ref.shape
    later = lines // TIME_BLOCKS
    my_index = lax.axis_index("feed")
    my_core = my_index % CORES
    other_core = CORES - 1 - my_core
    place_in_plane = my_index % owners

    for line in range(later):
        near[line] = join_blocks(own_ref[line], own_ref[later + line])
        far[line] = join_blocks(other_ref[line], other_ref[later + line])
    left[0] = left_rows(near[place_in_plane])
    left[1] = left_rows(far[place_in_plane])

    def block(line, turn):
        row_group = my_core if turn == 0 else other_core
        column_group = line * CORES + (my_core if turn == 2 else other_core)
        for part in range(2):
            yield store_block(out_buf, out_hbm, sems.at[line, turn, part], row_group, column_group, part)

    @pl.loop(0, later)
    def _(line):
        for turn in range(3):
            source = near if turn == 2 else far
            product = jnp.dot(left[min(turn, 1)], source[line], preferred_element_type=jnp.float32)
            product = product * scale
            for part, (place, copy) in enumerate(block(line, turn)):
                out_buf[place] = product[part * size : (part + 1) * size]
                copy.start()

    @pl.loop(0, later)
    def _(line):
        for turn in range(3):
            for _, copy in block(line, turn):
                copy.wait()


def correlate_in_two(own, swap, owners, total_feeds, scale):
    lines, rows, size = own.shape
    depth = rows // 3 * 4
    later = lines // TIME_BLOCKS
    in_vmem = pl.BlockSpec(memory_space=pltpu.VMEM)
    anywhere = pl.BlockSpec(memory_space=pl.ANY)
    shape = jax.ShapeDtypeStruct((ROWS_DEV, 2 * total_feeds), jnp.float32)
    other = swap(own)
    started = pl.pallas_call(
        functools.partial(near_kernel, scale, owners),
        out_shape=shape,
        in_specs=[in_vmem],
        out_specs=anywhere,
        scratch_shapes=[
            pltpu.VMEM((later, depth, size), jnp.bfloat16),
            pltpu.VMEM(shape.shape, jnp.float32),
            pltpu.SemaphoreType.DMA((later, 2)),
        ],
        cost_estimate=pl.CostEstimate(
            flops=depth * shape.size // 2, bytes_accessed=shape.size, transcendentals=0
        ),
        compiler_params=pltpu.CompilerParams(vmem_limit_bytes=32 * 2**20),
        name="near",
    )(own)
    return pl.pallas_call(
        functools.partial(far_kernel, scale, owners),
        out_shape=shape,
        in_specs=[in_vmem, in_vmem, anywhere],
        out_specs=anywhere,
        input_output_aliases={2: 0},
        scratch_shapes=[
            pltpu.VMEM((later, depth, size), jnp.bfloat16),
            pltpu.VMEM((later, depth, size), jnp.bfloat16),
            pltpu.VMEM((2, 2 * size, depth), jnp.bfloat16),
            pltpu.VMEM(shape.shape, jnp.float32),
            pltpu.SemaphoreType.DMA((later, 3, 2)),
        ],
        compiler_params=pltpu.CompilerParams(vmem_limit_bytes=32 * 2**20),
        name="far",
    )(own, other, started)


def body(samples, pfb_taps):
    feed_count = samples.shape[1]
    tap_count, fft_len = pfb_taps.shape
    frame_count = samples.shape[2] // fft_len
    devices = lax.axis_size("feed")
    total_feeds = feed_count * devices // TIME_BLOCKS
    channels = devices * ROWS_DEV // total_feeds
    owners = total_feeds // ROWS_DEV
    spectra_count = TIME_BLOCKS * frame_count
    columns = 2 * channels
    rows = 3 * frame_count
    lines = devices // CORES
    dft = jnp.asarray(dft_rows(fft_len, FIRST_CH, channels))
    in_vmem = pl.BlockSpec(memory_space=pltpu.VMEM)
    outgoing = pl.pallas_call(
        functools.partial(spectra_kernel, owners),
        out_shape=jax.ShapeDtypeStruct((lines, rows, feed_count), jnp.bfloat16),
        in_specs=[pl.BlockSpec(memory_space=pltpu.HBM)] * 3,
        out_specs=in_vmem,
        scratch_shapes=[
            pltpu.VMEM(pfb_taps.shape, jnp.float32),
            pltpu.VMEM(dft.shape, jnp.float32),
            pltpu.VMEM((feed_count, samples.shape[2]), jnp.bfloat16),
            pltpu.VMEM((fft_len, 2 * tap_count * columns), jnp.bfloat16),
            pltpu.VMEM((feed_count, 2 * tap_count * columns), jnp.float32),
            pltpu.VMEM((frame_count + tap_count - 1, columns, feed_count), jnp.float32),
            pltpu.VMEM((columns, 2 * frame_count, feed_count), jnp.float32),
            pltpu.SemaphoreType.DMA((2,)),
            pltpu.SemaphoreType.DMA((frame_count * PIECES,)),
        ],
        compiler_params=pltpu.CompilerParams(vmem_limit_bytes=44 * 2**20),
        name="spectra",
    )(*[pltpu.with_memory_space_constraint(v, pltpu.HBM) for v in (samples, pfb_taps, dft)])
    same_core = [[line * CORES + core for line in range(lines)] for core in range(CORES)]
    own = lax.all_to_all(outgoing, "feed", 0, 0, axis_index_groups=same_core, tiled=True)

    def swap(value):
        return lax.ppermute(value, "feed", [(d, d ^ 1) for d in range(devices)])

    if feed_count * CORES == ROWS_DEV and feed_count % 128 == 0:
        return correlate_in_two(own, swap, owners, total_feeds, 1.0 / spectra_count)
    other = swap(own)
    return pl.pallas_call(
        functools.partial(correlate_kernel, 1.0 / spectra_count, owners),
        out_shape=jax.ShapeDtypeStruct((ROWS_DEV, 2 * total_feeds), jnp.float32),
        in_specs=[in_vmem, in_vmem],
        out_specs=pl.BlockSpec(memory_space=pl.ANY),
        scratch_shapes=[
            pltpu.VMEM((2 * spectra_count, total_feeds), jnp.bfloat16),
            pltpu.VMEM((2 * ROWS_DEV, 2 * spectra_count), jnp.bfloat16),
            pltpu.VMEM((ROWS_DEV, 2 * total_feeds), jnp.float32),
            pltpu.SemaphoreType.DMA((total_feeds // COLUMNS, 2)),
        ],
        compiler_params=pltpu.CompilerParams(vmem_limit_bytes=32 * 2**20),
        name="correlate",
    )(own, other)


def solution(mesh):
    placed = (P(("grp", "feed"), None, None), P())
    return jax.shard_map(
        body, mesh=mesh, in_specs=placed, out_specs=P(("grp", "feed"), None), check_vma=False
    )
```

```python
import functools
import math

import jax
import jax.numpy as jnp
import numpy as np
from jax import lax
from jax.experimental import pallas as pl
from jax.experimental.pallas import tpu as pltpu
from jax.sharding import PartitionSpec as P

FIRST_CH = 1536
TIME_BLOCKS = 2
ROWS_DEV = 512
CORES = 2
PIECES = 2
TABLE_STEP = 1024
COLUMNS = 256


def dft_rows(fft_len, first_channel, channel_count):
    sample_ids = np.arange(fft_len, dtype=np.int64)
    channel_ids = first_channel + np.arange(channel_count, dtype=np.int64)
    phase = channel_ids[:, None] * sample_ids[None, :] % fft_len
    angle = phase.astype(np.float64) * (2.0 * math.pi / fft_len)
    return np.concatenate([np.cos(angle), -np.sin(angle)], axis=0).astype(np.float32)


def spectra_kernel(
    owners, x_hbm, taps_hbm, dft_hbm, out_ref,
    taps_ref, dft_ref, x_buf, table, raw, window, parts, small_sems, sems,
):
    tap_count, fft_len = taps_ref.shape
    columns = dft_ref.shape[0]
    channels = columns // 2
    frame_count = x_hbm.shape[2] // fft_len
    piece = fft_len // PIECES
    edge = tap_count - 1
    width = tap_count * columns
    later_block = lax.axis_index("feed") >= channels * owners // TIME_BLOCKS

    small = [
        pltpu.make_async_copy(taps_hbm, taps_ref, small_sems.at[0]),
        pltpu.make_async_copy(dft_hbm, dft_ref, small_sems.at[1]),
    ]
    for copy in small:
        copy.start()

    def fetch(index):
        span = pl.ds(pl.multiple_of(index * piece, piece), piece)
        return pltpu.make_async_copy(x_hbm.at[0, :, span], x_buf.at[:, span], sems.at[index])

    @pl.loop(0, frame_count * PIECES)
    def _(index):
        fetch(index).start()

    window[...] = jnp.zeros_like(window)
    raw[...] = jnp.zeros_like(raw)
    for copy in small:
        copy.wait()

    @pl.loop(0, fft_len // TABLE_STEP)
    def _(index):
        span = pl.ds(pl.multiple_of(index * TABLE_STEP, TABLE_STEP), TABLE_STEP)
        dft = dft_ref[:, span]
        scaled = jnp.concatenate([taps_ref[m : m + 1, span] * dft for m in range(tap_count)], axis=0)
        high = scaled.astype(jnp.bfloat16).astype(jnp.float32)
        both = jnp.concatenate([high, scaled - high], axis=0)
        table[span, :] = both.T.astype(jnp.bfloat16)

    def fold(frame, total):
        turned = total.T
        summed = turned[:width] + turned[width:]
        for m in range(tap_count):
            window[frame + edge - m] += summed[m * columns : (m + 1) * columns]

    def two_dots(frame, begin, depth):
        total = None
        for offset in (begin, begin + depth):
            start = pl.multiple_of(frame * fft_len + offset, depth)
            product = jnp.dot(
                x_buf[:, pl.ds(start, depth)],
                table[offset : offset + depth, :],
                preferred_element_type=jnp.float32,
            )
            total = product if total is None else total + product
        return total

    @pl.loop(0, frame_count - 1)
    def _(frame):
        for p in range(PIECES):
            fetch(frame * PIECES + p).wait()
        fold(jnp.maximum(frame - 1, 0), raw[...])
        raw[...] = two_dots(frame, 0, fft_len // 2)

    last = frame_count - 1
    total = None
    for p in range(PIECES):
        fetch(last * PIECES + p).wait()
        if p == 0:
            fold(last - 1, raw[...])
        product = two_dots(last, p * piece, piece // 2)
        total = product if total is None else total + product
    fold(last, total)

    for spot in range(frame_count + edge):
        parts[:, spot, :] = window[spot]

    copies = out_ref.shape[0] // channels
    for c in range(channels):
        now = jnp.concatenate([parts[c, :frame_count], parts[channels + c, :frame_count]], axis=0)
        high = now.astype(jnp.bfloat16)
        low = now - high.astype(jnp.float32)
        low = jnp.concatenate([low[:4], low[frame_count : frame_count + 4]], axis=0)
        tail = jnp.concatenate(
            [parts[c, frame_count : frame_count + 4], parts[channels + c, frame_count : frame_count + 4]],
            axis=0,
        )
        sublane = lax.broadcasted_iota(jnp.int32, tail.shape, 0)
        tail = jnp.where(sublane % 4 < edge, tail, 0.0)
        extra = jnp.where(later_block, low, tail).astype(jnp.bfloat16)
        whole = jnp.concatenate([high, extra], axis=0)
        for o in range(copies):
            out_ref[c * copies + o] = whole


def correlate_kernel(
    scale, owners, own_ref, other_ref, out_hbm, right, left, out_buf, sems
):
    lines, rows, feed_count = own_ref.shape
    frame_count = rows // 3
    total_feeds = right.shape[1]
    my_index = lax.axis_index("feed")
    my_core = my_index % CORES

    def join(group, low, high):
        place = pl.ds(group * feed_count, feed_count)
        if not isinstance(group, int):
            place = pl.ds(pl.multiple_of(group * feed_count, feed_count), feed_count)
        extra = low[2 * frame_count :].astype(jnp.float32) + high[2 * frame_count :].astype(jnp.float32)
        zero = jnp.zeros((frame_count - 4, feed_count), jnp.float32)
        extra = jnp.concatenate([extra[:4], zero, extra[4:8], zero], axis=0)
        fixed = high[: 2 * frame_count].astype(jnp.float32) + extra
        right[: 2 * frame_count, place] = low[: 2 * frame_count]
        right[2 * frame_count :, place] = fixed.astype(jnp.bfloat16)

    later = lines // TIME_BLOCKS
    for line in range(later):
        if feed_count % 128 == 0:
            for ref, core in ((own_ref, my_core), (other_ref, CORES - 1 - my_core)):
                join(line * CORES + core, ref[line], ref[later + line])
        else:
            for core in range(CORES):
                low, high = [
                    jnp.where(my_core == core, own_ref[k], other_ref[k]) for k in (line, later + line)
                ]
                join(line * CORES + core, low, high)
    row_start = my_index % owners * ROWS_DEV
    mine = right[:, pl.ds(pl.multiple_of(row_start, ROWS_DEV), ROWS_DEV)].astype(jnp.float32)
    halves = [mine[k * frame_count : (k + 1) * frame_count] for k in range(4)]
    swapped = jnp.concatenate([halves[1], -halves[0], halves[3], -halves[2]], axis=0)
    left[:ROWS_DEV] = mine.T.astype(jnp.bfloat16)
    left[ROWS_DEV:] = swapped.T.astype(jnp.bfloat16)

    def span(block, part):
        start = part * total_feeds + block * COLUMNS
        return pl.ds(pl.multiple_of(start, COLUMNS), COLUMNS)

    def store(block, part):
        cut = span(block, part)
        return pltpu.make_async_copy(out_buf.at[:, cut], out_hbm.at[:, cut], sems.at[block, part])

    @pl.loop(0, total_feeds // COLUMNS)
    def _(block):
        product = jnp.dot(left[...], right[:, span(block, 0)], preferred_element_type=jnp.float32)
        product = product * scale
        for part in range(2):
            out_buf[:, span(block, part)] = product[part * ROWS_DEV : (part + 1) * ROWS_DEV]
            store(block, part).start()

    @pl.loop(0, total_feeds // COLUMNS)
    def _(block):
        for part in range(2):
            store(block, part).wait()


def join_blocks(low, high):
    frame_count = low.shape[0] // 3
    feed_count = low.shape[1]
    extra = low[2 * frame_count :].astype(jnp.float32) + high[2 * frame_count :].astype(jnp.float32)
    zero = jnp.zeros((frame_count - 4, feed_count), jnp.float32)
    extra = jnp.concatenate([extra[:4], zero, extra[4:8], zero], axis=0)
    fixed = high[: 2 * frame_count].astype(jnp.float32) + extra
    return jnp.concatenate([low[: 2 * frame_count], fixed.astype(jnp.bfloat16)], axis=0)


def left_rows(block):
    mine = block.astype(jnp.float32)
    size = mine.shape[0] // 4
    parts = [mine[k * size : (k + 1) * size] for k in range(4)]
    swapped = jnp.concatenate([parts[1], -parts[0], parts[3], -parts[2]], axis=0)
    return jnp.concatenate([mine.T, swapped.T], axis=0).astype(jnp.bfloat16)


def store_block(out_buf, out_hbm, sem, row_group, column_group, part):
    size = out_hbm.shape[0] // CORES
    row = pl.multiple_of(row_group * size, size)
    column = pl.multiple_of(part * (out_hbm.shape[1] // 2) + column_group * size, size)
    place = (pl.ds(row, size), pl.ds(column, size))
    return place, pltpu.make_async_copy(out_buf.at[place], out_hbm.at[place], sem)


def near_kernel(scale, owners, own_ref, out_hbm, out_buf, sems):
    lines, _, size = own_ref.shape
    later = lines // TIME_BLOCKS
    my_index = lax.axis_index("feed")
    my_core = my_index % CORES

    my_line = my_index % owners
    left = left_rows(join_blocks(own_ref[my_line], own_ref[later + my_line]))
    copies = []
    for line in range(later):
        right = join_blocks(own_ref[line], own_ref[later + line])
        product = jnp.dot(left, right, preferred_element_type=jnp.float32) * scale
        for part in range(2):
            place, copy = store_block(
                out_buf, out_hbm, sems.at[line, part], my_core, line * CORES + my_core, part
            )
            out_buf[place] = product[part * size : (part + 1) * size]
            copy.start()
            copies.append(copy)
    for copy in copies:
        copy.wait()


def far_kernel(scale, owners, own_ref, other_ref, _, out_hbm, left, out_buf, sems):
    lines, _, size = own_ref.shape
    later = lines // TIME_BLOCKS
    my_index = lax.axis_index("feed")
    my_core = my_index % CORES
    other_core = CORES - 1 - my_core
    place_in_plane = my_index % owners

    for k, ref in enumerate((own_ref, other_ref)):
        left[k] = left_rows(join_blocks(ref[place_in_plane], ref[later + place_in_plane]))

    def block(line, turn):
        row_group = my_core if turn == 0 else other_core
        column_group = line * CORES + (my_core if turn == 2 else other_core)
        for part in range(2):
            yield store_block(out_buf, out_hbm, sems.at[line, turn, part], row_group, column_group, part)

    @pl.loop(0, later)
    def _(line):
        far = join_blocks(other_ref[line], other_ref[later + line])
        near = join_blocks(own_ref[line], own_ref[later + line])
        for turn in range(3):
            source = near if turn == 2 else far
            product = jnp.dot(left[min(turn, 1)], source, preferred_element_type=jnp.float32)
            product = product * scale
            for part, (place, copy) in enumerate(block(line, turn)):
                out_buf[place] = product[part * size : (part + 1) * size]
                copy.start()

    @pl.loop(0, later)
    def _(line):
        for turn in range(3):
            for _, copy in block(line, turn):
                copy.wait()


def correlate_in_two(own, swap, owners, total_feeds, scale):
    lines, rows, size = own.shape
    depth = rows // 3 * 4
    later = lines // TIME_BLOCKS
    in_vmem = pl.BlockSpec(memory_space=pltpu.VMEM)
    anywhere = pl.BlockSpec(memory_space=pl.ANY)
    shape = jax.ShapeDtypeStruct((ROWS_DEV, 2 * total_feeds), jnp.float32)
    other = swap(own)
    started = pl.pallas_call(
        functools.partial(near_kernel, scale, owners),
        out_shape=shape,
        in_specs=[in_vmem],
        out_specs=anywhere,
        scratch_shapes=[
            pltpu.VMEM(shape.shape, jnp.float32),
            pltpu.SemaphoreType.DMA((later, 2)),
        ],
        cost_estimate=pl.CostEstimate(
            flops=depth * shape.size // 2, bytes_accessed=shape.size, transcendentals=0
        ),
        compiler_params=pltpu.CompilerParams(vmem_limit_bytes=32 * 2**20),
        name="near",
    )(own)
    return pl.pallas_call(
        functools.partial(far_kernel, scale, owners),
        out_shape=shape,
        in_specs=[in_vmem, in_vmem, anywhere],
        out_specs=anywhere,
        input_output_aliases={2: 0},
        scratch_shapes=[
            pltpu.VMEM((2, 2 * size, depth), jnp.bfloat16),
            pltpu.VMEM(shape.shape, jnp.float32),
            pltpu.SemaphoreType.DMA((later, 3, 2)),
        ],
        compiler_params=pltpu.CompilerParams(vmem_limit_bytes=32 * 2**20),
        name="far",
    )(own, other, started)


def body(samples, pfb_taps):
    feed_count = samples.shape[1]
    tap_count, fft_len = pfb_taps.shape
    frame_count = samples.shape[2] // fft_len
    devices = lax.axis_size("feed")
    total_feeds = feed_count * devices // TIME_BLOCKS
    channels = devices * ROWS_DEV // total_feeds
    owners = total_feeds // ROWS_DEV
    spectra_count = TIME_BLOCKS * frame_count
    columns = 2 * channels
    rows = 3 * frame_count
    lines = devices // CORES
    dft = jnp.asarray(dft_rows(fft_len, FIRST_CH, channels))
    in_vmem = pl.BlockSpec(memory_space=pltpu.VMEM)
    outgoing = pl.pallas_call(
        functools.partial(spectra_kernel, owners),
        out_shape=jax.ShapeDtypeStruct((lines, rows, feed_count), jnp.bfloat16),
        in_specs=[pl.BlockSpec(memory_space=pltpu.HBM)] * 3,
        out_specs=in_vmem,
        scratch_shapes=[
            pltpu.VMEM(pfb_taps.shape, jnp.float32),
            pltpu.VMEM(dft.shape, jnp.float32),
            pltpu.VMEM((feed_count, samples.shape[2]), jnp.bfloat16),
            pltpu.VMEM((fft_len, 2 * tap_count * columns), jnp.bfloat16),
            pltpu.VMEM((feed_count, 2 * tap_count * columns), jnp.float32),
            pltpu.VMEM((frame_count + tap_count - 1, columns, feed_count), jnp.float32),
            pltpu.VMEM((columns, 2 * frame_count, feed_count), jnp.float32),
            pltpu.SemaphoreType.DMA((2,)),
            pltpu.SemaphoreType.DMA((frame_count * PIECES,)),
        ],
        compiler_params=pltpu.CompilerParams(vmem_limit_bytes=44 * 2**20),
        name="spectra",
    )(*[pltpu.with_memory_space_constraint(v, pltpu.HBM) for v in (samples, pfb_taps, dft)])
    same_core = [[line * CORES + core for line in range(lines)] for core in range(CORES)]
    own = lax.all_to_all(outgoing, "feed", 0, 0, axis_index_groups=same_core, tiled=True)

    def swap(value):
        return lax.ppermute(value, "feed", [(d, d ^ 1) for d in range(devices)])

    if feed_count * CORES == ROWS_DEV and feed_count % 128 == 0:
        return correlate_in_two(own, swap, owners, total_feeds, 1.0 / spectra_count)
    other = swap(own)
    return pl.pallas_call(
        functools.partial(correlate_kernel, 1.0 / spectra_count, owners),
        out_shape=jax.ShapeDtypeStruct((ROWS_DEV, 2 * total_feeds), jnp.float32),
        in_specs=[in_vmem, in_vmem],
        out_specs=pl.BlockSpec(memory_space=pl.ANY),
        scratch_shapes=[
            pltpu.VMEM((2 * spectra_count, total_feeds), jnp.bfloat16),
            pltpu.VMEM((2 * ROWS_DEV, 2 * spectra_count), jnp.bfloat16),
            pltpu.VMEM((ROWS_DEV, 2 * total_feeds), jnp.float32),
            pltpu.SemaphoreType.DMA((total_feeds // COLUMNS, 2)),
        ],
        compiler_params=pltpu.CompilerParams(vmem_limit_bytes=32 * 2**20),
        name="correlate",
    )(own, other)


def solution(mesh):
    placed = (P(("grp", "feed"), None, None), P())
    return jax.shard_map(
        body, mesh=mesh, in_specs=placed, out_specs=P(("grp", "feed"), None), check_vma=False
    )
```
